32 devices in a mesh: lat: 4 (over y, x), lon: 8 (over z, core).
Axes of the slice: x: 2, y: 2, z: 4, core: 2. Of those that a mesh axis runs over, the one named last changes fastest.
Arguments:
- state_field: bfloat16 [8, 720, 512], P('lat', 'lon'), may hold values from -32 to 32
- cotangent: bfloat16 [8, 720, 512], P('lat', 'lon'), may hold values from -6 to 6
- key_bias: bfloat16 [8, 720, 16], P('lat', 'lon'), may hold values from -3 to 250
- input_gain: float32 [512], replicated, may hold values from 0.1 to 1.9
- expand_weight: bfloat16 [512, 2048], replicated, may hold values from -0.25 to 0.25
- depth_weight: bfloat16 [3, 3, 2048], replicated, may hold values from -2 to 2
- shrink_weight: bfloat16 [2048, 512], replicated, may hold values from -0.125 to 0.125
- attention_gain: float32 [512], replicated, may hold values from 0.1 to 1.9
- attention_in: bfloat16 [512, 1536], replicated, may hold values from -0.25 to 0.25
- attention_out: bfloat16 [512, 512], replicated, may hold values from -0.25 to 0.25
Outputs:
- output_field: bfloat16 [8, 720, 512], P('lat', 'lon')
- input_grad: bfloat16 [8, 720, 512], P('lat', 'lon')
- expand_grad: float32 [512, 2048], P('lat', 'lon')
- shrink_grad: float32 [2048, 512], P('lat', 'lon')
- attention_in_grad: float32 [512, 1536], P('lat', 'lon')
- attention_out_grad: float32 [512, 512], P('lat', 'lon')
- depth_grad: float32 [3, 3, 2048], replicated
- input_gain_grad: float32 [512], replicated
- attention_gain_grad: float32 [512], replicated
The draws below stay inside these ranges and needn't reach their ends.
All inputs are finite; a program needn't handle non-finite values.
Results may differ from the reference program's by a relative error of at most 0.035.
Values may be sent and summed in bfloat16 or wider, within the bound.
No kernel may reach another device: no remote copies, remote signals or barrier semaphores. Data moves between devices by JAX's collectives and lax.ppermute only.
A program may use at most 128 MiB of HBM per device.

```python
import math
import jax
import jax.numpy as jnp
from jax import lax

ROWS_DEV = 2
C = 512
HEADS = 16
HEAD_DIM = 32
WIDE = 2048
LAT = 8
LON = 720


def draw_state_field(key, part):
    base_key, channel_key, cell_key = jax.random.split(key, 3)
    grid_shape = (LAT, LON, C)
    base_values = jnp.clip(jax.random.normal(base_key, grid_shape, jnp.float32), -3.5, 3.5)
    lower_log = math.log(0.3)
    upper_log = math.log(3.0)
    channel_scale = jnp.exp(jax.random.uniform(channel_key, (1, 1, C), jnp.float32, lower_log, upper_log))
    cell_scale = jnp.exp(jax.random.uniform(cell_key, (LAT, LON, 1), jnp.float32, lower_log, upper_log))
    return (base_values * channel_scale * cell_scale).astype(jnp.bfloat16)


def draw_key_bias(key, part):
    base_key = jax.random.fold_in(key, 0)
    base_values = jax.random.uniform(base_key, (LAT, LON, HEADS), jnp.float32, -3.0, 3.0)
    return base_values.astype(jnp.bfloat16)


def shard_levels(rng, shape, cuts, low, high):
    loudness = 1.0
    for dim, blocks in cuts:
        steps = jax.random.uniform(jax.random.fold_in(jax.random.fold_in(rng, 6), dim), (blocks,), jnp.float32, low / len(cuts), high / len(cuts))
        loudness = loudness * jnp.repeat(jnp.exp(steps), shape[dim] // blocks).reshape((-1,) + (1,) * (len(shape) - 1 - dim))
    return loudness


def normal_values(stream_key, shape, scale, limit, shards=(), kind=jnp.bfloat16):
    values = scale * jax.random.normal(stream_key, shape, jnp.float32)
    if shards:
        values = values * shard_levels(stream_key, shape, shards, -0.22, 0.18)
    return jnp.clip(values, -limit, limit).astype(kind)


def setup_inputs(seed: int = 0) -> dict:
    streams_of = jax.random.split(jax.random.key(seed), 11)
    return {
        "state_field": draw_state_field(jax.random.fold_in(streams_of[10], 71), 0),
        "cotangent": normal_values(streams_of[1], (LAT, LON, C), 1.0, 6.0, ((0, 4), (1, 8))),
        "key_bias": draw_key_bias(jax.random.fold_in(streams_of[10], 71), 0),
        "input_gain": jnp.clip(1.0 + 0.18 * jax.random.normal(streams_of[3], (C,), jnp.float32), 0.1, 1.9),
        "expand_weight": normal_values(streams_of[4], (C, WIDE), C ** -0.5, 0.25),
        "depth_weight": normal_values(streams_of[5], (3, 3, WIDE), 9 ** -0.5, 2.0),
        "shrink_weight": normal_values(streams_of[6], (WIDE, C), WIDE ** -0.5, 0.125),
        "attention_gain": jnp.clip(1.0 + 0.18 * jax.random.normal(streams_of[7], (C,), jnp.float32), 0.1, 1.9),
        "attention_in": normal_values(streams_of[8], (C, 3 * C), C ** -0.5, 0.25),
        "attention_out": normal_values(streams_of[9], (C, C), C ** -0.5, 0.25),
    }


EPSILON = 1e-06

def inverse_rms(values):
    return lax.rsqrt(lax.optimization_barrier(jnp.mean(values * values, axis=-1, keepdims=True)) + EPSILON)

def silu_slope(values):
    sigmoid = jax.nn.sigmoid(values)
    return sigmoid * (1.0 + values * (1.0 - sigmoid))

def rounded(values):
    return lax.optimization_barrier(values.astype(jnp.bfloat16)).astype(jnp.float32)

def wrap_longitude(values):
    return jnp.concatenate([values[:, -1:], values, values[:, :1]], axis=1)

def depthwise_sum(padded, weights, row_count, lon_count):
    total = jnp.zeros((row_count, lon_count, padded.shape[2]), jnp.float32)
    for lat_step in range(3):
        for lon_step in range(3):
            total = total + weights[lat_step, lon_step].astype(jnp.float32) * padded[lat_step:lat_step + row_count, lon_step:lon_step + lon_count].astype(jnp.float32)
    return total

def transposed_sum(padded, weights, row_count, lon_count):
    total = jnp.zeros((row_count, lon_count, padded.shape[2]), jnp.float32)
    for lat_step in range(3):
        for lon_step in range(3):
            total = total + weights[lat_step, lon_step].astype(jnp.float32) * padded[2 - lat_step:2 - lat_step + row_count, 2 - lon_step:2 - lon_step + lon_count].astype(jnp.float32)
    return total

def norm_back(back_normed, state, inverse, gain):
    scaled = back_normed * gain
    return inverse * scaled - inverse * inverse * inverse * state * lax.optimization_barrier(jnp.mean(scaled * state, axis=-1, keepdims=True))

def reference(state_field, cotangent, key_bias, input_gain, expand_weight, depth_weight, shrink_weight, attention_gain, attention_in, attention_out):
    norm_factor = 1.0 / math.sqrt(LAT * LON)
    score_scale = 1.0 / math.sqrt(HEAD_DIM)
    band_count = LAT // ROWS_DEV
    state_float = state_field.astype(jnp.float32)
    inverse_first = inverse_rms(state_float)
    normed = (state_float * inverse_first * input_gain).astype(jnp.bfloat16)
    normed_pad = jnp.pad(normed, ((2, 2), (0, 0), (0, 0)))
    band_ids = jnp.arange(band_count, dtype=jnp.int32)

    def band_forward(band):
        start_row = band * ROWS_DEV
        block_rows = lax.dynamic_slice_in_dim(normed_pad, start_row + 1, ROWS_DEV + 2, 0)
        activated = jax.nn.silu(jnp.dot(block_rows, expand_weight, preferred_element_type=jnp.float32)).astype(jnp.bfloat16)
        convolved = depthwise_sum(wrap_longitude(activated), depth_weight, ROWS_DEV, LON)
        mixed = jax.nn.silu(convolved).astype(jnp.bfloat16)
        own_rows = lax.dynamic_slice_in_dim(state_float, start_row, ROWS_DEV, 0)
        return (own_rows + jnp.dot(mixed, shrink_weight, preferred_element_type=jnp.float32)).astype(jnp.bfloat16)
    inner_state = lax.map(band_forward, band_ids).reshape(LAT, LON, C)

    def row_step(carry, operands):
        in_total, out_total, gain_total = carry
        inner_row, back_row, bias_row = operands
        inner_float = inner_row.astype(jnp.float32)
        inverse_second = inverse_rms(inner_float)
        normed_second = (inner_float * inverse_second * attention_gain).astype(jnp.bfloat16)
        projected = rounded(jnp.dot(normed_second, attention_in, preferred_element_type=jnp.float32))
        queries = projected[:, :C].reshape(LON, HEADS, HEAD_DIM)
        keys_all = projected[:, C:2 * C].reshape(LON, HEADS, HEAD_DIM)
        values_all = projected[:, 2 * C:].reshape(LON, HEADS, HEAD_DIM)
        bias_float = bias_row.astype(jnp.float32).T[:, None, :]
        scores = jnp.einsum('qhd,khd->hqk', queries, keys_all) * score_scale + bias_float
        highest = lax.optimization_barrier(jnp.max(scores, axis=-1, keepdims=True))
        exponent = jnp.exp(scores - highest)
        probs_float = exponent / lax.optimization_barrier(jnp.sum(exponent, axis=-1, keepdims=True))
        probs_low = rounded(probs_float)
        heads_field = jnp.einsum('hqk,khd->qhd', probs_low, values_all).reshape(LON, C).astype(jnp.bfloat16)
        output_row = (inner_float + jnp.dot(heads_field, attention_out, preferred_element_type=jnp.float32)).astype(jnp.bfloat16)
        out_total = out_total + jnp.dot(heads_field.T, back_row, preferred_element_type=jnp.float32) * norm_factor
        back_heads = rounded(jnp.dot(back_row, attention_out.T, preferred_element_type=jnp.float32)).reshape(LON, HEADS, HEAD_DIM)
        back_probs = jnp.einsum('qhd,khd->hqk', back_heads, values_all)
        centred = lax.optimization_barrier(jnp.sum(probs_float * back_probs, axis=-1, keepdims=True))
        back_scores = rounded(probs_float * (back_probs - centred))
        back_queries = (jnp.einsum('hqk,khd->qhd', back_scores, keys_all) * score_scale).astype(jnp.bfloat16)
        back_keys = (jnp.einsum('hqk,qhd->khd', back_scores, queries) * score_scale).astype(jnp.bfloat16)
        back_values = jnp.einsum('hqk,qhd->khd', probs_low, back_heads).astype(jnp.bfloat16)
        back_projected = jnp.concatenate([back_queries.reshape(LON, C), back_keys.reshape(LON, C), back_values.reshape(LON, C)], axis=-1)
        in_total = in_total + jnp.dot(normed_second.T, back_projected, preferred_element_type=jnp.float32) * norm_factor
        back_second = jnp.dot(back_projected, attention_in.T, preferred_element_type=jnp.float32)
        gain_total = gain_total + lax.optimization_barrier(jnp.sum(back_second * inner_float * inverse_second, axis=0)) * norm_factor
        back_inner = (back_row.astype(jnp.float32) + norm_back(back_second, inner_float, inverse_second, attention_gain)).astype(jnp.bfloat16)
        return ((in_total, out_total, gain_total), (output_row, back_inner))
    row_start = (jnp.zeros((C, 3 * C), jnp.float32), jnp.zeros((C, C), jnp.float32), jnp.zeros((C,), jnp.float32))
    row_final, row_outputs = lax.scan(row_step, row_start, (inner_state, cotangent, key_bias))
    in_grad, out_grad, gain_two = row_final
    output_field, back_inner = row_outputs
    back_inner_pad = jnp.pad(back_inner, ((1, 1), (0, 0), (0, 0)))

    def band_back(carry, band):
        expand_total, shrink_total, depth_total, gain_total = carry
        start_row = band * ROWS_DEV
        block_rows = lax.dynamic_slice_in_dim(normed_pad, start_row, ROWS_DEV + 4, 0)
        expanded = jnp.dot(block_rows, expand_weight, preferred_element_type=jnp.float32)
        activated = wrap_longitude(jax.nn.silu(expanded).astype(jnp.bfloat16))
        convolved = depthwise_sum(activated, depth_weight, ROWS_DEV + 2, LON)
        mixed = jax.nn.silu(convolved[1:-1]).astype(jnp.bfloat16)
        back_rows = lax.dynamic_slice_in_dim(back_inner_pad, start_row, ROWS_DEV + 2, 0)
        back_convolved = (jnp.dot(back_rows, shrink_weight.T, preferred_element_type=jnp.float32) * silu_slope(convolved)).astype(jnp.bfloat16)
        back_activated = transposed_sum(wrap_longitude(back_convolved), depth_weight, ROWS_DEV, LON)
        centre = back_convolved[1:-1].astype(jnp.float32)
        depth_terms = jnp.stack([jnp.stack([lax.optimization_barrier(jnp.sum(activated[lat_step + 1:lat_step + 1 + ROWS_DEV, lon_step:lon_step + LON].astype(jnp.float32) * centre, axis=(0, 1))) for lon_step in range(3)]) for lat_step in range(3)])
        depth_total = depth_total + depth_terms * norm_factor
        own_back = back_rows[1:-1]
        shrink_total = shrink_total + jnp.dot(mixed.reshape(-1, WIDE).T, own_back.reshape(-1, C), preferred_element_type=jnp.float32) * norm_factor
        back_expanded = (back_activated * silu_slope(expanded[2:-2])).astype(jnp.bfloat16)
        expand_total = expand_total + jnp.dot(block_rows[2:-2].reshape(-1, C).T, back_expanded.reshape(-1, WIDE), preferred_element_type=jnp.float32) * norm_factor
        back_normed = jnp.dot(back_expanded, expand_weight.T, preferred_element_type=jnp.float32)
        own_rows = lax.dynamic_slice_in_dim(state_float, start_row, ROWS_DEV, 0)
        inverse_own = inverse_rms(own_rows)
        gain_total = gain_total + lax.optimization_barrier(jnp.sum(back_normed * own_rows * inverse_own, axis=(0, 1))) * norm_factor
        band_grad = (own_back.astype(jnp.float32) + norm_back(back_normed, own_rows, inverse_own, input_gain)).astype(jnp.bfloat16)
        return ((expand_total, shrink_total, depth_total, gain_total), band_grad)
    band_start = (jnp.zeros((C, WIDE), jnp.float32), jnp.zeros((WIDE, C), jnp.float32), jnp.zeros((3, 3, WIDE), jnp.float32), jnp.zeros((C,), jnp.float32))
    band_final, grad_bands = lax.scan(band_back, band_start, band_ids)
    expand_grad, shrink_grad, depth_grad, gain_one = band_final
    input_grad = grad_bands.reshape(LAT, LON, C)
    return (output_field, input_grad, expand_grad, shrink_grad, in_grad, out_grad, depth_grad, gain_one, gain_two)
```

```python
import functools
import math

import jax
import jax.numpy as jnp
from jax import lax
from jax.experimental import pallas as pl
from jax.experimental.pallas import tpu as pltpu
from jax.sharding import Mesh
from jax.sharding import PartitionSpec as P

EPSILON = 1e-06
LON = ("z", "core")
BF16 = jnp.bfloat16
F32 = jnp.float32
MASKED = -1e30
SIDE = 3
LOG2E = math.log2(math.e)


def inverse_rms(values):
    return lax.rsqrt(jnp.mean(values * values, axis=-1, keepdims=True) + EPSILON)


def silu_slope(values):
    sigmoid = jax.nn.sigmoid(values)
    return sigmoid * (1.0 + values * (1.0 - sigmoid))


def norm_back(back_normed, state, inverse, gain):
    scaled = back_normed * gain
    return inverse * scaled - inverse * inverse * inverse * state * jnp.mean(
        scaled * state, axis=-1, keepdims=True
    )


def shifts(count, step, periodic):
    return [(i, (i + step) % count) for i in range(count) if periodic or 0 <= i + step < count]


def from_sides(block, width, dim, axis, periodic):
    count = lax.axis_size(axis)
    size = block.shape[dim]
    low = lax.ppermute(
        lax.slice_in_dim(block, size - width, size, axis=dim), axis, shifts(count, 1, periodic)
    )
    high = lax.ppermute(
        lax.slice_in_dim(block, 0, width, axis=dim), axis, shifts(count, -1, periodic)
    )
    return low, high


def core_swap(values):
    return lax.ppermute(values, "core", [(0, 1), (1, 0)])


def exchange(values, axis):
    return lax.all_to_all(values, axis, 0, 0, tiled=True)


def own_columns(values, blocks):
    cells = values.shape[0]
    view = values.reshape(cells, blocks, 2, -1)
    first = view[:, :, 0].reshape(cells, -1)
    second = view[:, :, 1].reshape(cells, -1)
    is_first = lax.axis_index("core") == 0
    return jnp.where(is_first, first, second), jnp.where(is_first, second, first)


def both_cores_columns(values, blocks):
    mine, other = own_columns(values, blocks)
    return jnp.concatenate([mine, core_swap(other)], axis=0)


def both_cores(values):
    return jnp.concatenate([values, core_swap(values)], axis=0)


def matmul(left, right):
    return jnp.dot(left, right, preferred_element_type=F32)


def cross_cells(left, right):
    return lax.dot_general(left, right, (((0,), (0,)), ((), ())), preferred_element_type=F32)


def times_transpose(values, weights):
    return lax.dot_general(
        values, weights, (((values.ndim - 1,), (1,)), ((), ())), preferred_element_type=F32
    )


def attention_kernel(
    head_width, query_block, qkv_ref, back_ref, bias_ref, out_ref, heads_t, query_grad_t, key_t,
    value_t, key_grad, value_grad,
):
    head = pl.program_id(0)
    cells, width = back_ref.shape
    scale = 1.0 / math.sqrt(head_width)
    keys = qkv_ref[:, width : 2 * width]
    values = qkv_ref[:, 2 * width : 3 * width]

    @pl.when(head == 0)
    def _():
        key_t[...] = keys.T
        value_t[...] = values.T
        key_grad[...] = jnp.zeros_like(key_grad)
        value_grad[...] = jnp.zeros_like(value_grad)

    lanes = lax.broadcasted_iota(jnp.int32, (1, width), 1) // head_width == head
    zero = jnp.zeros((), BF16)
    head_keys = jnp.where(lanes, keys, zero)
    head_values = jnp.where(lanes, values, zero)
    heads = lax.broadcasted_iota(jnp.int32, bias_ref.shape, 1)
    bias = LOG2E * jnp.sum(
        jnp.where(heads == head, bias_ref[...].astype(F32), 0.0), axis=1, keepdims=True
    )
    rows = pl.ds(pl.multiple_of(head * head_width, head_width), head_width)
    head_key_t = key_t[rows, :]
    head_value_t = value_t[rows, :]
    last_dims = (((1,), (1,)), ((), ()))

    def block(start):
        cols = pl.ds(start, query_block)
        queries = qkv_ref[cols, 0:width]
        backs = back_ref[cols, :]
        scores = lax.dot_general(head_keys, queries, last_dims, preferred_element_type=F32)
        scores = scores * (scale * LOG2E) + bias
        exponent = jnp.exp2(scores - jnp.max(scores, axis=0, keepdims=True))
        probs = exponent * (1.0 / jnp.sum(exponent, axis=0, keepdims=True))
        probs_low = probs.astype(BF16)
        heads_t[rows, cols] = matmul(head_value_t, probs_low)
        back_probs = lax.dot_general(head_values, backs, last_dims, preferred_element_type=F32)
        centred = jnp.sum(probs * back_probs, axis=0, keepdims=True)
        back_scores = (probs * (back_probs - centred)).astype(BF16)
        query_grad_t[rows, cols] = matmul(head_key_t, back_scores)
        value_grad[...] += matmul(probs_low, jnp.where(lanes, backs, zero))
        key_grad[...] += matmul(back_scores, jnp.where(lanes, queries, zero))

    block_count = cells // query_block
    if block_count <= 4:
        for index in range(block_count):
            block(index * query_block)
    else:

        def step(index, carry):
            block(pl.multiple_of(index * query_block, query_block))
            return carry

        lax.fori_loop(0, block_count, step, 0)

    @pl.when(head == pl.num_programs(0) - 1)
    def _():
        out_ref[:, 0:width] = heads_t[...].T.astype(BF16)
        out_ref[:, width : 2 * width] = (query_grad_t[...] * scale).T.astype(BF16)
        out_ref[:, 2 * width : 3 * width] = (key_grad[...] * scale).astype(BF16)
        out_ref[:, 3 * width : 4 * width] = value_grad[...].astype(BF16)


def attention(qkv, backs, bias, head_width):
    cells, width = backs.shape
    items = bias.shape[1]
    query_block = 256 if cells % 256 == 0 else 128
    whole = lambda shape: pl.BlockSpec(shape, lambda head: (0, 0))
    return pl.pallas_call(
        functools.partial(attention_kernel, head_width, query_block),
        grid=(items,),
        out_shape=jax.ShapeDtypeStruct((cells, 4 * width), BF16),
        in_specs=[whole(qkv.shape), whole(backs.shape), whole(bias.shape)],
        out_specs=whole((cells, 4 * width)),
        scratch_shapes=[
            pltpu.VMEM((width, cells), F32),
            pltpu.VMEM((width, cells), F32),
            pltpu.VMEM((width, cells), BF16),
            pltpu.VMEM((width, cells), BF16),
            pltpu.VMEM((cells, width), F32),
            pltpu.VMEM((cells, width), F32),
        ],
        compiler_params=pltpu.CompilerParams(
            vmem_limit_bytes=48 * 1024 * 1024, dimension_semantics=("arbitrary",)
        ),
        cost_estimate=pl.CostEstimate(
            flops=items * cells * cells * 32 * 14,
            bytes_accessed=cells * width * 16,
            transcendentals=items * cells * cells,
        ),
        name="attention",
    )(qkv, backs, bias)


def per_device(
    state_field,
    cotangent,
    key_bias,
    input_gain,
    expand_weight,
    depth_weight,
    shrink_weight,
    attention_gain,
    attention_in,
    attention_out,
):
    row_count, lon_count, channels = state_field.shape
    head_count = key_bias.shape[2]
    head_width = channels // head_count
    wide = expand_weight.shape[1]
    lat_size, z_size = lax.axis_size("lat"), lax.axis_size("z")
    lon_size = 2 * z_size
    norm_factor = 1.0 / math.sqrt(row_count * lon_count * lat_size * lon_size)
    items = row_count * head_count // lon_size
    groups = head_count // items
    width = items * head_width
    frame = lon_count + 2 * SIDE
    own = row_count * frame
    frame_pad = ((0, 0), (SIDE, SIDE), (0, 0))

    cot = jnp.pad(cotangent, frame_pad)
    back_heads = times_transpose(cot, attention_out).astype(BF16)
    bias = jnp.pad(key_bias, frame_pad, constant_values=MASKED)
    early = jnp.concatenate(
        [
            back_heads.reshape(row_count, frame, groups, width),
            bias.reshape(row_count, frame, groups, items),
        ],
        axis=-1,
    ).transpose(0, 2, 1, 3)
    early = exchange(early.reshape(lon_size, frame, width + items), LON)
    early = early.reshape(lon_size * frame, width + items)
    back_rows, bias_rows = early[:, :width], early[:, width:]

    low, high = from_sides(state_field, SIDE, 1, LON, True)
    state = jnp.concatenate([low, state_field, high], axis=1)
    below, above = from_sides(state, 2, 0, "lat", False)
    state = jnp.concatenate([below, state, above], axis=0).astype(F32)
    columns = lax.broadcasted_iota(jnp.int32, (1, frame, 1), 1)
    inside = (columns >= SIDE) & (columns < SIDE + lon_count)

    inverse_first = inverse_rms(state)
    normed = (state * inverse_first * input_gain).astype(BF16)
    expanded = matmul(normed, expand_weight)
    activated = jax.nn.silu(expanded).astype(BF16)
    kernel = depth_weight.astype(F32)

    def shifted(values, step):
        return jnp.roll(values, step, axis=1)

    around = [shifted(activated, 1), activated, shifted(activated, -1)]

    def convolve(first, count):
        total = jnp.zeros((count, frame, wide), F32)
        for a in range(3):
            for b in range(3):
                total = total + kernel[a, b] * around[b][first + a : first + a + count].astype(F32)
        return total

    convolved = convolve(0, row_count + 2)
    own_convolved = convolved[1 : 1 + row_count]
    mixed = jax.nn.silu(own_convolved).astype(BF16)
    own_state = state[2 : 2 + row_count]
    inner_state = (own_state + matmul(mixed, shrink_weight)).astype(BF16)
    inner = inner_state.astype(F32)
    inverse_second = inverse_rms(inner)
    normed_second = (inner * inverse_second * attention_gain).astype(BF16)
    grouped_in = (
        attention_in.reshape(channels, 3, groups, width)
        .transpose(0, 2, 1, 3)
        .reshape(channels, 3 * channels)
    )
    projected = matmul(normed_second, grouped_in).astype(BF16)
    qkv = (
        projected.reshape(row_count, frame, groups, 3 * width)
        .transpose(0, 2, 1, 3)
        .reshape(lon_size, frame, 3 * width)
    )
    qkv = exchange(qkv, LON).reshape(lon_size * frame, 3 * width)

    attended = attention(qkv, back_rows, bias_rows, head_width)
    attended = exchange(attended.reshape(lon_size, frame, 4 * width), LON)
    attended = (
        attended.reshape(row_count, groups, frame, 4, width)
        .transpose(3, 0, 2, 1, 4)
        .reshape(4, row_count, frame, channels)
    )
    heads_field = attended[0]
    back_projected = jnp.concatenate([attended[1], attended[2], attended[3]], axis=-1)
    output_field = (inner + matmul(heads_field, attention_out)).astype(BF16)
    output_field = output_field[:, SIDE : SIDE + lon_count]

    back_second = times_transpose(back_projected, attention_in)
    gain_two = jnp.sum(back_second * inner * inverse_second, axis=(0, 1)) * norm_factor
    back_inner = (
        cot.astype(F32) + norm_back(back_second, inner, inverse_second, attention_gain)
    ).astype(BF16)

    def cells(values):
        return values.reshape(own, values.shape[-1])

    def by_lat(left, right):
        return lax.dot_general(
            left,
            right.reshape(right.shape[0], lat_size, -1),
            (((0,), (0,)), ((), ())),
            preferred_element_type=F32,
        ).transpose(1, 0, 2)

    def scatter(parts):
        parts = jnp.sum(exchange(parts.astype(BF16), "lat").reshape(parts.shape).astype(F32), axis=0)
        parts = parts.reshape((z_size, -1) + parts.shape[1:])
        return jnp.sum(exchange(parts.astype(BF16), "z").astype(F32), axis=0)

    in_part = by_lat(
        both_cores_columns(cells(back_projected), z_size), both_cores(cells(normed_second))
    )
    out_part = by_lat(both_cores_columns(cells(cot), z_size), both_cores(cells(heads_field)))
    block = channels // lat_size
    part = jnp.concatenate(
        [
            in_part.reshape(lat_size, z_size, -1, block),
            out_part.reshape(lat_size, z_size, -1, block),
        ],
        axis=2,
    ).reshape(lat_size, -1, block)
    attention_grads = scatter(part * norm_factor)
    split = 3 * channels // lon_size
    attention_in_grad = attention_grads[:split].T
    attention_out_grad = attention_grads[split:].T

    shrink_part = by_lat(both_cores_columns(cells(back_inner), z_size), both_cores(cells(mixed)))
    shrink_grad = scatter(shrink_part * norm_factor).T

    low, high = from_sides(back_inner[:, SIDE : SIDE + lon_count], 1, 1, LON, True)
    back_sides = jnp.concatenate(
        [
            jnp.zeros((row_count, SIDE - 1, channels), BF16),
            low,
            back_inner[:, SIDE : SIDE + lon_count],
            high,
            jnp.zeros((row_count, SIDE - 1, channels), BF16),
        ],
        axis=1,
    )
    below, above = from_sides(back_sides, 1, 0, "lat", False)
    back_all = jnp.concatenate([below, back_sides, above], axis=0)
    back_convolved = (times_transpose(back_all, shrink_weight) * silu_slope(convolved)).astype(BF16)
    back_around = [shifted(back_convolved, -1), back_convolved, shifted(back_convolved, 1)]
    back_activated = jnp.zeros((row_count, frame, wide), F32)
    for a in range(3):
        for b in range(3):
            back_activated = back_activated + kernel[a, b] * back_around[b][
                2 - a : 2 - a + row_count
            ].astype(F32)
    own_back = jnp.where(inside, back_convolved[1 : 1 + row_count].astype(F32), 0.0)
    depth_part = jnp.stack(
        [
            jnp.sum(around[b][1 + a : 1 + a + row_count].astype(F32) * own_back, axis=(0, 1))
            for a in range(3)
            for b in range(3)
        ]
    )
    own_expanded = expanded[2 : 2 + row_count]
    back_expanded = jnp.where(inside, back_activated * silu_slope(own_expanded), 0.0).astype(BF16)
    own_normed = normed[2 : 2 + row_count]
    back_normed = times_transpose(back_expanded, expand_weight)
    own_inverse = inverse_first[2 : 2 + row_count]
    gain_one = jnp.sum(back_normed * own_state * own_inverse, axis=(0, 1)) * norm_factor
    input_grad = (
        back_inner.astype(F32) + norm_back(back_normed, own_state, own_inverse, input_gain)
    ).astype(BF16)

    expand_part = (
        cross_cells(
            both_cores(cells(own_normed)), both_cores_columns(cells(back_expanded), z_size)
        )
        * norm_factor
    )
    half = wide // 2
    expand_part = expand_part.reshape(lat_size, block, half)
    small = jnp.concatenate([(depth_part * norm_factor).reshape(-1), gain_one, gain_two])
    small = (small + core_swap(small)).reshape(-1, half)
    both = jnp.concatenate(
        [expand_part, jnp.broadcast_to(small, (lat_size,) + small.shape)], axis=1
    ).astype(BF16)
    both = jnp.sum(exchange(both, "lat").astype(F32), axis=0)
    expand_part = both[:block].reshape(block, z_size, -1).transpose(1, 0, 2)
    small = both[block:].reshape(-1, half // z_size)
    both = jnp.concatenate(
        [expand_part, jnp.broadcast_to(small, (z_size,) + small.shape)], axis=1
    ).astype(BF16)
    both = jnp.sum(exchange(both, "z").astype(F32), axis=0)
    expand_grad = both[:block]
    small = both[block:].reshape(-1)
    depth_grad = small[: 9 * wide].reshape(3, 3, wide)
    input_gain_grad = small[9 * wide : 9 * wide + channels]
    attention_gain_grad = small[9 * wide + channels :]
    return (
        output_field,
        input_grad[:, SIDE : SIDE + lon_count],
        expand_grad,
        shrink_grad,
        attention_in_grad,
        attention_out_grad,
        depth_grad,
        input_gain_grad,
        attention_gain_grad,
    )


def solution(mesh):
    lat_size, lon_size = mesh.devices.shape
    split = Mesh(mesh.devices.reshape(lat_size, lon_size // 2, 2), ("lat", "z", "core"))
    grid = P("lat", LON, None)
    weight = P("lat", LON)

    def step(*arrays):
        outputs = jax.shard_map(
            per_device,
            mesh=split,
            in_specs=(grid, grid, grid) + (P(),) * 7,
            out_specs=(grid, grid, weight, weight, weight, weight, P(), P(), P()),
            check_vma=False,
        )(*arrays)
        return outputs

    return step
```

```python
import functools
import math

import jax
import jax.numpy as jnp
from jax import lax
from jax.experimental import pallas as pl
from jax.experimental.pallas import tpu as pltpu
from jax.sharding import Mesh
from jax.sharding import PartitionSpec as P

EPSILON = 1e-06
LON = ("z", "core")
BF16 = jnp.bfloat16
F32 = jnp.float32
MASKED = -1e30
SIDE = 3
LOG2E = math.log2(math.e)


def inverse_rms(values):
    return lax.rsqrt(jnp.mean(values * values, axis=-1, keepdims=True) + EPSILON)


def norm_back(back_normed, state, inverse, gain):
    scaled = back_normed * gain
    return inverse * scaled - inverse * inverse * inverse * state * jnp.mean(
        scaled * state, axis=-1, keepdims=True
    )


def shifts(count, step, periodic):
    return [(i, (i + step) % count) for i in range(count) if periodic or 0 <= i + step < count]


def from_sides(block, width, dim, axis, periodic):
    count = lax.axis_size(axis)
    size = block.shape[dim]
    low = lax.ppermute(
        lax.slice_in_dim(block, size - width, size, axis=dim), axis, shifts(count, 1, periodic)
    )
    high = lax.ppermute(
        lax.slice_in_dim(block, 0, width, axis=dim), axis, shifts(count, -1, periodic)
    )
    return low, high


def core_swap(values):
    return lax.ppermute(values, "core", [(0, 1), (1, 0)])


def exchange(values, axis):
    return lax.all_to_all(values, axis, 0, 0, tiled=True)


def matmul(left, right):
    return jnp.dot(left, right, preferred_element_type=F32)


def cross_cells(left, right):
    return lax.dot_general(left, right, (((0,), (0,)), ((), ())), preferred_element_type=F32)


def times_transpose(values, weights):
    return lax.dot_general(
        values, weights, (((values.ndim - 1,), (1,)), ((), ())), preferred_element_type=F32
    )


def sigmoid(values):
    return 0.5 + 0.5 * jnp.tanh(0.5 * values)


def silu(values):
    return values * sigmoid(values)


def silu_slope(values):
    gate = sigmoid(values)
    return gate * (1.0 + values * (1.0 - gate))


def call(kernel, name, out_shape, *operands, scratch=(), megabytes=24, flops=0):
    return pl.pallas_call(
        kernel,
        out_shape=out_shape,
        scratch_shapes=scratch,
        compiler_params=pltpu.CompilerParams(vmem_limit_bytes=megabytes * 1024 * 1024),
        cost_estimate=pl.CostEstimate(
            flops=flops,
            bytes_accessed=sum(x.size * x.dtype.itemsize for x in operands),
            transcendentals=0,
        ),
        name=name,
    )(*operands)


def early_kernel(groups, cot_ref, bias_ref, out_weight_ref, early_ref, framed_ref, bias_frame):
    row_count, lon_count, channels = cot_ref.shape
    frame = early_ref.shape[1]
    width = channels // groups
    items = bias_ref.shape[2] // groups
    framed_ref[...] = jnp.zeros_like(framed_ref)
    bias_frame[...] = jnp.full_like(bias_frame, MASKED)
    for row in range(row_count):
        framed_ref[row, SIDE : SIDE + lon_count, :] = cot_ref[row]
        bias_frame[row, SIDE : SIDE + lon_count, :] = bias_ref[row].astype(F32)
    for row in range(row_count):
        back_heads = times_transpose(framed_ref[row], out_weight_ref[...]).astype(BF16)
        for group in range(groups):
            target = row * groups + group
            early_ref[target, :, 0:width] = back_heads[:, group * width : (group + 1) * width]
            early_ref[target, :, width : width + items] = bias_frame[
                row, :, group * items : (group + 1) * items
            ].astype(BF16)


def early_parts(cotangent, key_bias, attention_out, groups):
    row_count, lon_count, channels = cotangent.shape
    frame = lon_count + 2 * SIDE
    head_count = key_bias.shape[2]
    return call(
        functools.partial(early_kernel, groups),
        "back_heads",
        (
            jax.ShapeDtypeStruct(
                (row_count * groups, frame, (channels + head_count) // groups), BF16
            ),
            jax.ShapeDtypeStruct((row_count, frame, channels), BF16),
        ),
        cotangent,
        key_bias,
        attention_out,
        scratch=[pltpu.VMEM((row_count, frame, head_count), F32)],
        flops=2 * row_count * frame * channels * channels,
    )


def normalise(values, gain):
    return (values * inverse_rms(values) * gain).astype(BF16)


def convolve(values, kernel, rows, frame):
    size = rows * frame
    total = None
    for b in range(3):
        part = kernel[b : b + 1] * values[0:size]
        for a in range(1, 3):
            part = part + kernel[3 * a + b : 3 * a + b + 1] * values[a * frame : a * frame + size]
        if b != 1:
            part = pltpu.roll(part, 1 if b == 0 else size - 1, 0)
        total = part if total is None else total + part
    return total


def forward_kernel(
    frame, groups, state_ref, gain_ref, expand_ref, kernel_ref, shrink_ref, second_gain_ref, in_ref,
    qkv_ref, inner_ref, normed, total,
):
    step = pl.program_id(0)
    cells, channels = inner_ref.shape
    rows = cells // frame
    width = channels // groups

    @pl.when(step == 0)
    def _():
        normed[...] = normalise(state_ref[...].astype(F32), gain_ref[...])
        total[...] = jnp.zeros_like(total)

    activated = silu(matmul(normed[...], expand_ref[...])).astype(BF16).astype(F32)
    mixed = silu(convolve(activated, kernel_ref[...], rows, frame)).astype(BF16)
    total[...] += matmul(mixed, shrink_ref[...])

    @pl.when(step == pl.num_programs(0) - 1)
    def _():
        inner = (state_ref[frame : frame + cells, :].astype(F32) + total[...]).astype(BF16)
        inner_ref[...] = inner
        normed_second = normalise(inner.astype(F32), second_gain_ref[...])
        projected = matmul(normed_second, in_ref[...]).astype(BF16)
        for row in range(rows):
            for group in range(groups):
                for kind in range(3):
                    start = kind * channels + group * width
                    qkv_ref[row * groups + group, :, kind * width : (kind + 1) * width] = projected[
                        row * frame : (row + 1) * frame, start : start + width
                    ]


def step_width(wide):
    return 256 if wide % 256 == 0 else wide


def forward(state, input_gain, expand_weight, kernel, shrink_weight, gain, attention_in, groups):
    all_rows, frame, channels = state.shape
    rows = all_rows - 2
    cells = rows * frame
    wide = expand_weight.shape[1]
    part = step_width(wide)
    fixed = lambda shape: pl.BlockSpec(shape, lambda step: (0,) * len(shape))
    return pl.pallas_call(
        functools.partial(forward_kernel, frame, groups),
        grid=(wide // part,),
        out_shape=(
            jax.ShapeDtypeStruct((rows * groups, frame, 3 * channels // groups), BF16),
            jax.ShapeDtypeStruct((cells, channels), BF16),
        ),
        in_specs=[
            fixed((all_rows * frame, channels)),
            fixed((1, channels)),
            pl.BlockSpec((channels, part), lambda step: (0, step)),
            pl.BlockSpec((9, part), lambda step: (0, step)),
            pl.BlockSpec((part, channels), lambda step: (step, 0)),
            fixed((1, channels)),
            fixed(attention_in.shape),
        ],
        out_specs=(
            fixed((rows * groups, frame, 3 * channels // groups)),
            fixed((cells, channels)),
        ),
        scratch_shapes=[
            pltpu.VMEM((all_rows * frame, channels), BF16),
            pltpu.VMEM((cells, channels), F32),
        ],
        compiler_params=pltpu.CompilerParams(
            vmem_limit_bytes=24 * 1024 * 1024, dimension_semantics=("arbitrary",)
        ),
        cost_estimate=pl.CostEstimate(
            flops=2 * cells * channels * (3 * wide + 3 * channels),
            bytes_accessed=4 * channels * wide + 6 * channels * channels,
            transcendentals=3 * cells * wide,
        ),
        name="forward",
    )(
        state.reshape(all_rows * frame, channels),
        input_gain,
        expand_weight,
        kernel,
        shrink_weight,
        gain,
        attention_in,
    )


def around_kernel(
    frame, state_ref, gain_ref, expand_ref, kernel_ref, activated_ref, slope_ref, mixed_ref,
    expand_slope_ref, normed,
):
    size = activated_ref.shape[0]
    cells = mixed_ref.shape[0]

    @pl.when(pl.program_id(0) == 0)
    def _():
        normed[...] = normalise(state_ref[...].astype(F32), gain_ref[...])

    expanded = matmul(normed[...], expand_ref[...])
    gate = sigmoid(expanded)
    activated = (expanded * gate).astype(BF16)
    activated_ref[...] = activated[frame : frame + size]
    own_gate, own = gate[2 * frame : 2 * frame + cells], expanded[2 * frame : 2 * frame + cells]
    expand_slope_ref[...] = own_gate * (1.0 + own * (1.0 - own_gate))
    convolved = convolve(activated.astype(F32), kernel_ref[...], size // frame, frame)
    gate = sigmoid(convolved)
    slope_ref[...] = gate * (1.0 + convolved * (1.0 - gate))
    mixed_ref[...] = (
        convolved[frame : frame + cells] * gate[frame : frame + cells]
    ).astype(BF16)


def around(state, input_gain, expand_weight, kernel):
    all_rows, frame, channels = state.shape
    size, cells = (all_rows - 2) * frame, (all_rows - 4) * frame
    wide = expand_weight.shape[1]
    part = step_width(wide)
    fixed = lambda shape: pl.BlockSpec(shape, lambda step: (0,) * len(shape))
    moving = lambda rows: pl.BlockSpec((rows, part), lambda step: (0, step))
    return pl.pallas_call(
        functools.partial(around_kernel, frame),
        grid=(wide // part,),
        out_shape=(
            jax.ShapeDtypeStruct((size, wide), BF16),
            jax.ShapeDtypeStruct((size, wide), F32),
            jax.ShapeDtypeStruct((cells, wide), BF16),
            jax.ShapeDtypeStruct((cells, wide), F32),
        ),
        in_specs=[
            fixed((all_rows * frame, channels)),
            fixed((1, channels)),
            moving(channels),
            moving(9),
        ],
        out_specs=(moving(size), moving(size), moving(cells), moving(cells)),
        scratch_shapes=[pltpu.VMEM((all_rows * frame, channels), BF16)],
        compiler_params=pltpu.CompilerParams(
            vmem_limit_bytes=24 * 1024 * 1024, dimension_semantics=("arbitrary",)
        ),
        cost_estimate=pl.CostEstimate(
            flops=2 * all_rows * frame * channels * wide,
            bytes_accessed=2 * channels * wide + 14 * size * wide,
            transcendentals=2 * size * wide,
        ),
        name="forward_around",
    )(state.reshape(all_rows * frame, channels), input_gain, expand_weight, kernel)


def inner_kernel(
    groups, norm_factor, attended_ref, inner_ref, cot_ref, out_weight_ref, in_weight_ref, gain_ref,
    output_ref, back_inner_ref, unpacked_ref, gain_grad_ref,
):
    targets, frame, width = attended_ref.shape
    width = width // 4
    row_count, lon_count, channels = output_ref.shape
    for target in range(targets):
        row, group = divmod(target, groups)
        for kind in range(4):
            start = kind * channels + group * width
            unpacked_ref[row * frame : (row + 1) * frame, start : start + width] = attended_ref[
                target, :, kind * width : (kind + 1) * width
            ]
    inner = inner_ref[...].astype(F32)
    output = (inner + matmul(unpacked_ref[:, :channels], out_weight_ref[...])).astype(BF16)
    for row in range(row_count):
        start = row * frame + SIDE
        output_ref[row] = output[start : start + lon_count]
    back_second = times_transpose(unpacked_ref[:, channels:], in_weight_ref[...])
    inverse = inverse_rms(inner)
    gain_grad_ref[...] = norm_factor * jnp.sum(back_second * inner * inverse, axis=0, keepdims=True)
    back_inner_ref[...] = (
        cot_ref[...].astype(F32) + norm_back(back_second, inner, inverse, gain_ref[...])
    ).astype(BF16)


def attention_grads_kernel(
    norm_factor, unpacked_ref, inner_ref, gain_ref, cot_ref, part_ref, in_t, out_t
):
    lat_size, lon_size, split, block = part_ref.shape
    channels = inner_ref.shape[1]
    in_split = 3 * channels // lon_size
    out_split = channels // lon_size
    normed_second = normalise(inner_ref[...].astype(F32), gain_ref[...])
    in_t[...] = unpacked_ref[:, channels:].T
    out_t[...] = cot_ref[...].T
    for lat in range(lat_size):
        cols = slice(lat * block, (lat + 1) * block)
        in_grad = (matmul(in_t[...], normed_second[:, cols]) * norm_factor).astype(BF16)
        out_grad = (matmul(out_t[...], unpacked_ref[:, cols]) * norm_factor).astype(BF16)
        for lon in range(lon_size):
            part_ref[lat, lon, 0:in_split, :] = in_grad[lon * in_split : (lon + 1) * in_split]
            part_ref[lat, lon, in_split:, :] = out_grad[lon * out_split : (lon + 1) * out_split]


def shrink_grads_kernel(norm_factor, back_inner_ref, mixed_ref, part_ref, back_t):
    lat_size, _, block = part_ref.shape
    back_t[...] = back_inner_ref[...].T
    for lat in range(lat_size):
        part_ref[lat] = (
            matmul(back_t[...], mixed_ref[:, lat * block : (lat + 1) * block]) * norm_factor
        ).astype(BF16)


def backward_kernel(
    frame, norm_factor, back_ref, state_ref, gain_ref, inside_ref, shrink_ref, slope_ref,
    activated_ref, expand_ref, expand_slope_ref, kernel_ref, part_ref, depth_ref, input_ref,
    gain_grad_ref, normed, back_normed,
):
    step = pl.program_id(0)
    cells, channels = state_ref.shape
    row_count, lon_count, _ = input_ref.shape
    lat_size, _, block, _ = part_ref.shape
    inside = inside_ref[...]

    @pl.when(step == 0)
    def _():
        normed[...] = normalise(state_ref[...].astype(F32), gain_ref[...]).T
        back_normed[...] = jnp.zeros_like(back_normed)

    kernel = kernel_ref[...]
    back_convolved = (
        (times_transpose(back_ref[...], shrink_ref[...]) * slope_ref[...]).astype(BF16).astype(F32)
    )
    flipped = jnp.concatenate([kernel[8 - i : 9 - i] for i in range(9)], axis=0)
    back_activated = convolve(back_convolved, flipped, row_count, frame)
    back_expanded = jnp.where(inside > 0, back_activated * expand_slope_ref[...], 0.0).astype(BF16)
    part_ref[...] = (
        (matmul(normed[...], back_expanded) * norm_factor)
        .astype(BF16)
        .reshape(lat_size, 1, block, back_expanded.shape[1])
    )
    back_normed[...] += times_transpose(back_expanded, expand_ref[...])
    own_back = jnp.where(inside > 0, back_convolved[frame : frame + cells], 0.0)
    activated = activated_ref[...].astype(F32)
    for b in range(3):
        moved = own_back
        if b != 1:
            moved = pltpu.roll(own_back, cells - 1 if b == 0 else 1, 0)
        for a in range(3):
            depth_ref[3 * a + b : 3 * a + b + 1, :] = norm_factor * jnp.sum(
                activated[a * frame : a * frame + cells] * moved, axis=0, keepdims=True
            )

    @pl.when(step == pl.num_programs(0) - 1)
    def _():
        state = state_ref[...].astype(F32)
        inverse = inverse_rms(state)
        grads = back_normed[...]
        gain_grad_ref[...] = norm_factor * jnp.sum(grads * state * inverse, axis=0, keepdims=True)
        result = (
            back_ref[frame : frame + cells, :].astype(F32)
            + norm_back(grads, state, inverse, gain_ref[...])
        ).astype(BF16)
        for row in range(row_count):
            start = row * frame + SIDE
            input_ref[row] = result[start : start + lon_count]


def backward(
    back, state, gain, inside, shrink_weight, slope, activated, expand_weight, expand_slope, kernel,
    norm_factor, lat_size, row_count, lon_count,
):
    cells, channels = state.shape
    frame = cells // row_count
    size = activated.shape[0]
    wide = expand_weight.shape[1]
    part = step_width(wide)
    fixed = lambda shape: pl.BlockSpec(shape, lambda step: (0,) * len(shape))
    moving = lambda rows: pl.BlockSpec((rows, part), lambda step: (0, step))
    block = channels // lat_size
    return pl.pallas_call(
        functools.partial(backward_kernel, frame, norm_factor),
        grid=(wide // part,),
        out_shape=(
            jax.ShapeDtypeStruct((lat_size, wide // part, block, part), BF16),
            jax.ShapeDtypeStruct((9, wide), F32),
            jax.ShapeDtypeStruct((row_count, lon_count, channels), BF16),
            jax.ShapeDtypeStruct((1, channels), F32),
        ),
        in_specs=[
            fixed((size, channels)),
            fixed((cells, channels)),
            fixed((1, channels)),
            fixed((cells, 1)),
            pl.BlockSpec((part, channels), lambda step: (step, 0)),
            moving(size),
            moving(size),
            moving(channels),
            moving(cells),
            moving(9),
        ],
        out_specs=(
            pl.BlockSpec((lat_size, 1, block, part), lambda step: (0, step, 0, 0)),
            moving(9),
            fixed((row_count, lon_count, channels)),
            fixed((1, channels)),
        ),
        scratch_shapes=[
            pltpu.VMEM((channels, cells), BF16),
            pltpu.VMEM((cells, channels), F32),
        ],
        compiler_params=pltpu.CompilerParams(
            vmem_limit_bytes=24 * 1024 * 1024, dimension_semantics=("arbitrary",)
        ),
        cost_estimate=pl.CostEstimate(
            flops=8 * cells * channels * wide,
            bytes_accessed=6 * channels * wide + 12 * size * wide,
            transcendentals=0,
        ),
        name="backward",
    )(
        back, state, gain, inside, shrink_weight, slope, activated, expand_weight, expand_slope,
        kernel,
    )


def attention_kernel(
    head_width, query_block, qkv_ref, early_ref, out_ref, heads_t, query_grad_t, key_t,
    value_t, key_grad, value_grad,
):
    head = pl.program_id(0)
    cells = qkv_ref.shape[0]
    width = qkv_ref.shape[1] // 3
    items = early_ref.shape[1] - width
    scale = 1.0 / math.sqrt(head_width)
    keys = qkv_ref[:, width : 2 * width]
    values = qkv_ref[:, 2 * width : 3 * width]

    @pl.when(head == 0)
    def _():
        key_t[...] = keys.T
        value_t[...] = values.T
        key_grad[...] = jnp.zeros_like(key_grad)
        value_grad[...] = jnp.zeros_like(value_grad)

    lanes = lax.broadcasted_iota(jnp.int32, (1, width), 1) // head_width == head
    zero = jnp.zeros((), BF16)
    head_keys = jnp.where(lanes, keys, zero)
    head_values = jnp.where(lanes, values, zero)
    heads = lax.broadcasted_iota(jnp.int32, (cells, items), 1)
    bias = LOG2E * jnp.sum(
        jnp.where(heads == head, early_ref[:, width:].astype(F32), 0.0), axis=1, keepdims=True
    )
    rows = pl.ds(pl.multiple_of(head * head_width, head_width), head_width)
    head_key_t = key_t[rows, :]
    head_value_t = value_t[rows, :]
    last_dims = (((1,), (1,)), ((), ()))

    def block(start):
        cols = pl.ds(start, query_block)
        queries = qkv_ref[cols, 0:width]
        backs = early_ref[cols, 0:width]
        scores = lax.dot_general(head_keys, queries, last_dims, preferred_element_type=F32)
        scores = scores * (scale * LOG2E) + bias
        exponent = jnp.exp2(scores - jnp.max(scores, axis=0, keepdims=True))
        probs = exponent * (1.0 / jnp.sum(exponent, axis=0, keepdims=True))
        probs_low = probs.astype(BF16)
        heads_t[rows, cols] = matmul(head_value_t, probs_low)
        back_probs = lax.dot_general(head_values, backs, last_dims, preferred_element_type=F32)
        centred = jnp.sum(probs * back_probs, axis=0, keepdims=True)
        back_scores = (probs * (back_probs - centred)).astype(BF16)
        query_grad_t[rows, cols] = matmul(head_key_t, back_scores)
        value_grad[...] += matmul(probs_low, jnp.where(lanes, backs, zero))
        key_grad[...] += matmul(back_scores, jnp.where(lanes, queries, zero))

    block_count = cells // query_block
    if block_count <= 4:
        for index in range(block_count):
            block(index * query_block)
    else:

        def step(index, carry):
            block(pl.multiple_of(index * query_block, query_block))
            return carry

        lax.fori_loop(0, block_count, step, 0)

    @pl.when(head == pl.num_programs(0) - 1)
    def _():
        out_ref[:, 0:width] = heads_t[...].T.astype(BF16)
        out_ref[:, width : 2 * width] = (query_grad_t[...] * scale).T.astype(BF16)
        out_ref[:, 2 * width : 3 * width] = (key_grad[...] * scale).astype(BF16)
        out_ref[:, 3 * width : 4 * width] = value_grad[...].astype(BF16)


def attention(qkv, early, head_width):
    cells = qkv.shape[0]
    width = qkv.shape[1] // 3
    items = early.shape[1] - width
    query_block = 256 if cells % 256 == 0 else 128
    whole = lambda shape: pl.BlockSpec(shape, lambda head: (0, 0))
    return pl.pallas_call(
        functools.partial(attention_kernel, head_width, query_block),
        grid=(items,),
        out_shape=jax.ShapeDtypeStruct((cells, 4 * width), BF16),
        in_specs=[whole(qkv.shape), whole(early.shape)],
        out_specs=whole((cells, 4 * width)),
        scratch_shapes=[
            pltpu.VMEM((width, cells), F32),
            pltpu.VMEM((width, cells), F32),
            pltpu.VMEM((width, cells), BF16),
            pltpu.VMEM((width, cells), BF16),
            pltpu.VMEM((cells, width), F32),
            pltpu.VMEM((cells, width), F32),
        ],
        compiler_params=pltpu.CompilerParams(
            vmem_limit_bytes=48 * 1024 * 1024, dimension_semantics=("arbitrary",)
        ),
        cost_estimate=pl.CostEstimate(
            flops=items * cells * cells * 32 * 14,
            bytes_accessed=cells * width * 16,
            transcendentals=items * cells * cells,
        ),
        name="attention",
    )(qkv, early)


def per_device(
    state_field,
    cotangent,
    key_bias,
    input_gain,
    expand_weight,
    depth_weight,
    shrink_weight,
    attention_gain,
    attention_in,
    attention_out,
):
    row_count, lon_count, channels = state_field.shape
    head_count = key_bias.shape[2]
    head_width = channels // head_count
    wide = expand_weight.shape[1]
    lat_size, z_size = lax.axis_size("lat"), lax.axis_size("z")
    lon_size = 2 * z_size
    core = lax.axis_index("core")
    norm_factor = 1.0 / math.sqrt(row_count * lon_count * lat_size * lon_size)
    items = row_count * head_count // lon_size
    groups = head_count // items
    width = items * head_width
    frame = lon_count + 2 * SIDE
    own = row_count * frame
    kernel = depth_weight.astype(F32).reshape(9, wide)
    input_gain = input_gain.reshape(1, channels)
    attention_gain = attention_gain.reshape(1, channels)

    low, high = from_sides(state_field, SIDE, 1, LON, True)
    state = jnp.concatenate([low, state_field, high], axis=1)
    below, above = from_sides(state, 1, 0, "lat", False)

    early, cot = early_parts(cotangent, key_bias, attention_out, groups)
    early = exchange(early, LON).reshape(lon_size * frame, width + items)

    near = jnp.concatenate([below, state, above], axis=0)
    qkv, inner = forward(
        near, input_gain, expand_weight, kernel, shrink_weight, attention_gain, attention_in, groups
    )
    qkv = exchange(qkv, LON).reshape(lon_size * frame, 3 * width)

    second = (below, above) if row_count == 1 else (state[-2:-1], state[1:2])
    far_below = lax.ppermute(second[0], "lat", shifts(lat_size, 1, False))
    far_above = lax.ppermute(second[1], "lat", shifts(lat_size, -1, False))
    activated, slope, mixed, expand_slope = around(
        jnp.concatenate([far_below, near, far_above], axis=0), input_gain, expand_weight, kernel
    )

    attended = attention(qkv, early, head_width)
    attended = exchange(attended.reshape(lon_size, frame, 4 * width), LON)
    cot = cot.reshape(own, channels)
    output_field, back_inner, unpacked, gain_two = call(
        functools.partial(inner_kernel, groups, norm_factor),
        "back_inner",
        (
            jax.ShapeDtypeStruct((row_count, lon_count, channels), BF16),
            jax.ShapeDtypeStruct((own, channels), BF16),
            jax.ShapeDtypeStruct((own, 4 * channels), BF16),
            jax.ShapeDtypeStruct((1, channels), F32),
        ),
        attended,
        inner,
        cot,
        attention_out,
        attention_in,
        attention_gain,
        flops=8 * own * channels * channels,
    )

    back = back_inner.reshape(row_count, frame, channels)
    centre = back[:, SIDE : SIDE + lon_count]
    low, high = from_sides(centre, 1, 1, LON, True)
    edge = jnp.zeros((row_count, SIDE - 1, channels), BF16)
    back = jnp.concatenate([edge, low, centre, high, edge], axis=1)
    below, above = from_sides(back, 1, 0, "lat", False)
    back = jnp.concatenate([below, back, above], axis=0).reshape(-1, channels)

    def both_cores(parts):
        parts = parts.reshape((lat_size, z_size, 2) + parts.shape[2:])
        mine = lax.dynamic_index_in_dim(parts, core, 2, False)
        theirs = lax.dynamic_index_in_dim(parts, 1 - core, 2, False)
        return (mine.astype(F32) + core_swap(theirs).astype(F32)).astype(BF16)

    def over_lat(parts):
        parts = parts.reshape((lat_size, -1) + parts.shape[3:])
        return jnp.sum(exchange(parts, "lat").astype(F32), axis=0)

    def over_z(parts):
        parts = parts.reshape((z_size, -1) + parts.shape[1:]).astype(BF16)
        return jnp.sum(exchange(parts, "z").astype(F32), axis=0)

    block = channels // lat_size
    in_split, out_split = 3 * channels // lon_size, channels // lon_size
    attention_part = call(
        functools.partial(attention_grads_kernel, norm_factor),
        "attention_grads",
        jax.ShapeDtypeStruct((lat_size, lon_size, in_split + out_split, block), BF16),
        unpacked,
        inner,
        attention_gain,
        cot,
        scratch=[pltpu.VMEM((3 * channels, own), BF16), pltpu.VMEM((channels, own), BF16)],
        flops=8 * own * channels * channels,
    )
    attention_part = over_z(over_lat(both_cores(attention_part)))
    shrink_part = call(
        functools.partial(shrink_grads_kernel, norm_factor),
        "shrink_grads",
        jax.ShapeDtypeStruct((lat_size, channels, wide // lat_size), BF16),
        back_inner,
        mixed,
        scratch=[pltpu.VMEM((channels, own), BF16)],
        flops=2 * own * channels * wide,
    )
    shrink_part = over_z(
        over_lat(both_cores(shrink_part.reshape(lat_size, lon_size, out_split, wide // lat_size)))
    )

    columns = lax.broadcasted_iota(jnp.int32, (row_count, frame, 1), 1).reshape(own, 1)
    inside = ((columns >= SIDE) & (columns < SIDE + lon_count)).astype(F32)
    expand_part, depth_part, input_grad, gain_one = backward(
        back,
        state.reshape(own, channels),
        input_gain,
        inside,
        shrink_weight,
        slope,
        activated,
        expand_weight,
        expand_slope,
        kernel,
        norm_factor,
        lat_size,
        row_count,
        lon_count,
    )

    split = wide // lon_size
    if expand_part.shape[1] != lon_size:
        expand_part = (
            expand_part.reshape(lat_size, expand_part.shape[1], block, -1, split)
            .transpose(0, 1, 3, 2, 4)
            .reshape(lat_size, lon_size, block, split)
        )
    expand_part = both_cores(expand_part).reshape(lat_size, z_size * block, split)
    small = jnp.concatenate([depth_part.reshape(-1), gain_one.reshape(-1), gain_two.reshape(-1)])
    small = (small + core_swap(small)).astype(BF16).reshape(-1, split)
    expand_part = jnp.concatenate(
        [expand_part, jnp.broadcast_to(small, (lat_size,) + small.shape)], axis=1
    )
    expand_part = jnp.sum(exchange(expand_part, "lat").astype(F32), axis=0).astype(BF16)
    small = expand_part[z_size * block :]
    expand_part = jnp.concatenate(
        [
            expand_part[: z_size * block].reshape(z_size, block, split),
            jnp.broadcast_to(small, (z_size,) + small.shape),
        ],
        axis=1,
    )
    expand_part = jnp.sum(exchange(expand_part, "z").astype(F32), axis=0)
    small = expand_part[block:].reshape(-1)
    return (
        output_field,
        input_grad,
        expand_part[:block],
        shrink_part.T,
        attention_part[:in_split].T,
        attention_part[in_split:].T,
        small[: 9 * wide].reshape(3, 3, wide),
        small[9 * wide : 9 * wide + channels],
        small[9 * wide + channels : 9 * wide + 2 * channels],
    )


def solution(mesh):
    lat_size, lon_size = mesh.devices.shape
    split = Mesh(mesh.devices.reshape(lat_size, lon_size // 2, 2), ("lat", "z", "core"))
    grid = P("lat", LON, None)
    weight = P("lat", LON)

    def step(*arrays):
        outputs = jax.shard_map(
            per_device,
            mesh=split,
            in_specs=(grid, grid, grid) + (P(),) * 7,
            out_specs=(grid, grid, weight, weight, weight, weight, P(), P(), P()),
            check_vma=False,
        )(*arrays)
        return outputs

    return step
```

```python
import functools
import math

import jax
import jax.numpy as jnp
from jax import lax
from jax.experimental import pallas as pl
from jax.experimental.pallas import tpu as pltpu
from jax.sharding import Mesh
from jax.sharding import PartitionSpec as P

EPSILON = 1e-06
LON = ("z", "core")
BF16 = jnp.bfloat16
F32 = jnp.float32
MASKED = -1e30
SIDE = 3
BIAS_ROWS = 16
LOG2E = math.log2(math.e)


def inverse_rms(values):
    return lax.rsqrt(jnp.mean(values * values, axis=-1, keepdims=True) + EPSILON)


def norm_back(back_normed, state, inverse, gain):
    scaled = back_normed * gain
    return inverse * scaled - inverse * inverse * inverse * state * jnp.mean(
        scaled * state, axis=-1, keepdims=True
    )


def shifts(count, step, periodic):
    return [(i, (i + step) % count) for i in range(count) if periodic or 0 <= i + step < count]


def from_sides(block, width, dim, axis, periodic):
    count = lax.axis_size(axis)
    size = block.shape[dim]
    low = lax.ppermute(
        lax.slice_in_dim(block, size - width, size, axis=dim), axis, shifts(count, 1, periodic)
    )
    high = lax.ppermute(
        lax.slice_in_dim(block, 0, width, axis=dim), axis, shifts(count, -1, periodic)
    )
    return low, high


def core_swap(values):
    return lax.ppermute(values, "core", [(0, 1), (1, 0)])


def exchange(values, axis):
    return lax.all_to_all(values, axis, 0, 0, tiled=True)


def matmul(left, right):
    return jnp.dot(left, right, preferred_element_type=F32)


def cross_cells(left, right):
    return lax.dot_general(left, right, (((0,), (0,)), ((), ())), preferred_element_type=F32)


def times_transpose(values, weights):
    return lax.dot_general(
        values, weights, (((values.ndim - 1,), (1,)), ((), ())), preferred_element_type=F32
    )


def sigmoid(values):
    return 0.5 + 0.5 * jnp.tanh(0.5 * values)


def silu(values):
    return values * sigmoid(values)


def silu_slope(values):
    gate = sigmoid(values)
    return gate * (1.0 + values * (1.0 - gate))


def call(kernel, name, out_shape, *operands, scratch=(), megabytes=16, flops=0, specs=None):
    return pl.pallas_call(
        kernel,
        out_shape=out_shape,
        scratch_shapes=scratch,
        in_specs=specs or [pl.BlockSpec(memory_space=pltpu.VMEM)] * len(operands),
        compiler_params=pltpu.CompilerParams(vmem_limit_bytes=megabytes * 1024 * 1024),
        cost_estimate=pl.CostEstimate(
            flops=flops,
            bytes_accessed=sum(x.size * x.dtype.itemsize for x in operands),
            transcendentals=0,
        ),
        name=name,
    )(*operands)


def early_kernel(
    groups, cot_ref, bias_ref, out_weight_ref, order_ref, early_ref, framed_ref, bias_frame
):
    row_count, lon_count, channels = cot_ref.shape
    frame = framed_ref.shape[1]
    width = channels // groups
    head_count = bias_ref.shape[2]
    items = head_count // groups
    in_rows = early_ref.shape[2] == width
    framed_ref[...] = jnp.zeros_like(framed_ref)
    bias_frame[...] = jnp.full_like(bias_frame, MASKED)
    for row in range(row_count):
        framed_ref[row, SIDE : SIDE + lon_count, :] = cot_ref[row]
        bias_frame[row, SIDE : SIDE + lon_count, 0:head_count] = bias_ref[row].astype(F32)
    for row in range(row_count):
        back_heads = times_transpose(framed_ref[row], out_weight_ref[...]).astype(BF16)
        bias = bias_frame[row].T if in_rows else bias_frame[row]
        for group in range(groups):
            target = row * groups + group
            early_ref[target, 0:frame, 0:width] = back_heads[:, group * width : (group + 1) * width]
            if in_rows:
                early_ref[target, frame:, :] = bias[
                    group * items : group * items + BIAS_ROWS
                ].astype(BF16)
            else:
                early_ref[target, :, width:] = bias[
                    0:frame, group * items : (group + 1) * items
                ].astype(BF16)


def early_parts(cotangent, key_bias, attention_out, order, groups):
    row_count, lon_count, channels = cotangent.shape
    frame = lon_count + 2 * SIDE
    head_count = key_bias.shape[2]
    width = channels // groups
    if frame <= width and width % 128 == 0:
        shape = (row_count * groups, frame + BIAS_ROWS, width)
        bias_shape = (row_count, width, max(128, head_count + BIAS_ROWS))
    else:
        shape = (row_count * groups, frame, width + head_count // groups)
        bias_shape = (row_count, frame, head_count)
    return call(
        functools.partial(early_kernel, groups),
        "back_heads",
        (
            jax.ShapeDtypeStruct(shape, BF16),
            jax.ShapeDtypeStruct((row_count, frame, channels), BF16),
        ),
        cotangent,
        key_bias,
        attention_out,
        order,
        scratch=[pltpu.VMEM(bias_shape, F32)],
        flops=2 * row_count * frame * channels * channels,
    )


def normalise(values, gain):
    return (values * inverse_rms(values) * gain).astype(BF16)


def convolve(values, kernel, rows, frame):
    size = rows * frame
    total = None
    for b in range(3):
        part = kernel[b : b + 1] * values[0:size]
        for a in range(1, 3):
            part = part + kernel[3 * a + b : 3 * a + b + 1] * values[a * frame : a * frame + size]
        if b != 1:
            part = pltpu.roll(part, 1 if b == 0 else size - 1, 0)
        total = part if total is None else total + part
    return total


def forward_kernel(
    frame, groups, state_ref, gain_ref, expand_ref, kernel_ref, shrink_ref, second_gain_ref, in_ref,
    qkv_ref, inner_ref, normed, total,
):
    step = pl.program_id(0)
    cells, channels = inner_ref.shape
    rows = cells // frame
    width = channels // groups

    @pl.when(step == 0)
    def _():
        near = state_ref[frame : frame + normed.shape[0], :].astype(F32)
        normed[...] = normalise(near, gain_ref[...])
        total[...] = jnp.zeros_like(total)

    activated = silu(matmul(normed[...], expand_ref[...])).astype(BF16).astype(F32)
    mixed = silu(convolve(activated, kernel_ref[...], rows, frame)).astype(BF16)
    total[...] += matmul(mixed, shrink_ref[...])

    @pl.when(step == pl.num_programs(0) - 1)
    def _():
        inner = state_ref[2 * frame : 2 * frame + cells, :].astype(F32)
        inner = (inner + total[...]).astype(BF16)
        inner_ref[...] = inner
        normed_second = normalise(inner.astype(F32), second_gain_ref[...])
        projected = matmul(normed_second, in_ref[...]).astype(BF16)
        for row in range(rows):
            for group in range(groups):
                for kind in range(3):
                    start = kind * channels + group * width
                    qkv_ref[row * groups + group, :, kind * width : (kind + 1) * width] = projected[
                        row * frame : (row + 1) * frame, start : start + width
                    ]


def step_width(wide):
    return 256 if wide % 256 == 0 else wide


def forward(state, input_gain, expand_weight, kernel, shrink_weight, gain, attention_in, groups):
    all_rows, frame, channels = state.shape
    rows = all_rows - 4
    cells = rows * frame
    wide = expand_weight.shape[1]
    part = step_width(wide)
    fixed = lambda shape: pl.BlockSpec(shape, lambda step: (0,) * len(shape))
    return pl.pallas_call(
        functools.partial(forward_kernel, frame, groups),
        grid=(wide // part,),
        out_shape=(
            jax.ShapeDtypeStruct((rows * groups, frame, 3 * channels // groups), BF16),
            jax.ShapeDtypeStruct((cells, channels), BF16),
        ),
        in_specs=[
            fixed((all_rows * frame, channels)),
            fixed((1, channels)),
            pl.BlockSpec((channels, part), lambda step: (0, step)),
            pl.BlockSpec((9, part), lambda step: (0, step)),
            pl.BlockSpec((part, channels), lambda step: (step, 0)),
            fixed((1, channels)),
            fixed(attention_in.shape),
        ],
        out_specs=(
            fixed((rows * groups, frame, 3 * channels // groups)),
            fixed((cells, channels)),
        ),
        scratch_shapes=[
            pltpu.VMEM((cells + 2 * frame, channels), BF16),
            pltpu.VMEM((cells, channels), F32),
        ],
        compiler_params=pltpu.CompilerParams(
            vmem_limit_bytes=16 * 1024 * 1024, dimension_semantics=("arbitrary",)
        ),
        cost_estimate=pl.CostEstimate(
            flops=2 * cells * channels * (3 * wide + 3 * channels),
            bytes_accessed=4 * channels * wide + 6 * channels * channels,
            transcendentals=3 * cells * wide,
        ),
        name="forward",
    )(
        state.reshape(all_rows * frame, channels),
        input_gain,
        expand_weight,
        kernel,
        shrink_weight,
        gain,
        attention_in,
    )


def around_kernel(
    frame, state_ref, gain_ref, expand_ref, kernel_ref, order_ref, activated_ref, slope_ref, mixed_ref,
    expand_slope_ref, normed,
):
    size = activated_ref.shape[1]
    cells = mixed_ref.shape[1]

    @pl.when(pl.program_id(0) == 0)
    def _():
        normed[...] = normalise(state_ref[...].astype(F32), gain_ref[...])

    expanded = matmul(normed[...], expand_ref[...])
    gate = sigmoid(expanded)
    activated = (expanded * gate).astype(BF16)
    activated_ref[0] = activated[frame : frame + size]
    own_gate, own = gate[2 * frame : 2 * frame + cells], expanded[2 * frame : 2 * frame + cells]
    expand_slope_ref[0] = (own_gate * (1.0 + own * (1.0 - own_gate))).astype(BF16)
    convolved = convolve(activated.astype(F32), kernel_ref[...], size // frame, frame)
    gate = sigmoid(convolved)
    slope_ref[0] = (gate * (1.0 + convolved * (1.0 - gate))).astype(BF16)
    mixed_ref[0] = (
        convolved[frame : frame + cells] * gate[frame : frame + cells]
    ).astype(BF16)


def around(state, input_gain, expand_weight, kernel, order):
    all_rows, frame, channels = state.shape
    size, cells = (all_rows - 2) * frame, (all_rows - 4) * frame
    wide = expand_weight.shape[1]
    part = step_width(wide)
    fixed = lambda shape: pl.BlockSpec(shape, lambda step: (0,) * len(shape))
    moving = lambda rows: pl.BlockSpec((rows, part), lambda step: (0, step))
    block = lambda rows: pl.BlockSpec((1, rows, part), lambda step: (step, 0, 0))
    steps = wide // part
    return pl.pallas_call(
        functools.partial(around_kernel, frame),
        grid=(steps,),
        out_shape=(
            jax.ShapeDtypeStruct((steps, size, part), BF16),
            jax.ShapeDtypeStruct((steps, size, part), BF16),
            jax.ShapeDtypeStruct((steps, cells, part), BF16),
            jax.ShapeDtypeStruct((steps, cells, part), BF16),
        ),
        in_specs=[
            fixed((all_rows * frame, channels)),
            fixed((1, channels)),
            moving(channels),
            moving(9),
            pl.BlockSpec(memory_space=pl.ANY),
        ],
        out_specs=(block(size), block(size), block(cells), block(cells)),
        scratch_shapes=[pltpu.VMEM((all_rows * frame, channels), BF16)],
        compiler_params=pltpu.CompilerParams(
            vmem_limit_bytes=16 * 1024 * 1024, dimension_semantics=("arbitrary",)
        ),
        cost_estimate=pl.CostEstimate(
            flops=2 * all_rows * frame * channels * wide,
            bytes_accessed=2 * channels * wide + 14 * size * wide,
            transcendentals=2 * size * wide,
        ),
        name="forward_around",
    )(state.reshape(all_rows * frame, channels), input_gain, expand_weight, kernel, order)


def inner_kernel(
    groups, norm_factor, attended_ref, inner_ref, cot_ref, out_weight_ref, in_weight_ref, gain_ref,
    output_ref, back_inner_ref, unpacked_ref, gain_grad_ref,
):
    targets, frame, width = attended_ref.shape
    width = width // 4
    row_count, lon_count, channels = output_ref.shape
    for target in range(targets):
        row, group = divmod(target, groups)
        for kind in range(4):
            start = kind * channels + group * width
            unpacked_ref[row * frame : (row + 1) * frame, start : start + width] = attended_ref[
                target, :, kind * width : (kind + 1) * width
            ]
    inner = inner_ref[...].astype(F32)
    output = (inner + matmul(unpacked_ref[:, :channels], out_weight_ref[...])).astype(BF16)
    for row in range(row_count):
        start = row * frame + SIDE
        output_ref[row] = output[start : start + lon_count]
    back_second = times_transpose(unpacked_ref[:, channels:], in_weight_ref[...])
    inverse = inverse_rms(inner)
    gain_grad_ref[...] = norm_factor * jnp.sum(back_second * inner * inverse, axis=0, keepdims=True)
    back_inner_ref[...] = (
        cot_ref[...].astype(F32) + norm_back(back_second, inner, inverse, gain_ref[...])
    ).astype(BF16)


def weight_grads_kernel(
    norm_factor, z_size, which_ref, unpacked_ref, inner_ref, gain_ref, cot_ref, back_inner_ref,
    mixed_ref, order_ref, *refs
):
    added_ref = refs[0] if len(refs) == 8 else None
    out_ref, whole_in, whole_out, whole_back, in_t, out_t, back_t = refs[-7:]
    lat_size, _, lane = out_ref.shape
    channels = inner_ref.shape[1]
    blocks, _, part = mixed_ref.shape
    blocks = blocks // lat_size
    in_split, out_split = in_t.shape[0] // z_size, out_t.shape[0] // z_size
    first_rows = out_ref.shape[1] // z_size
    normed_second = normalise(inner_ref[...].astype(F32), gain_ref[...])
    whole_in[...] = unpacked_ref[:, channels:].T
    whole_out[...] = cot_ref[...].T
    whole_back[...] = back_inner_ref[...].T
    for z in range(z_size):
        lon = 2 * z + which_ref[0]
        for source, target, split in (
            (whole_in, in_t, in_split),
            (whole_out, out_t, out_split),
            (whole_back, back_t, out_split),
        ):
            target[z * split : (z + 1) * split, :] = source[
                pl.ds(pl.multiple_of(lon * split, split), split), :
            ]

    def put(lat, start, split, values):
        values = values * norm_factor
        for z in range(z_size):
            rows = slice(z * first_rows + start, z * first_rows + start + split)
            value = values[z * split : (z + 1) * split]
            if added_ref is not None:
                value = value + added_ref[lat, rows, :].astype(F32)
            out_ref[lat, rows, :] = value.astype(BF16)

    for lat in range(lat_size):
        cols = slice(lat * lane, (lat + 1) * lane)
        put(lat, 0, in_split, matmul(in_t[...], normed_second[:, cols]))
        put(lat, in_split, out_split, matmul(out_t[...], unpacked_ref[:, cols]))
        start = in_split + out_split
        for block in range(blocks):
            values = matmul(back_t[...], mixed_ref[lat * blocks + block])
            for piece in range(part // lane):
                put(lat, start, out_split, values[:, piece * lane : (piece + 1) * lane])
                start += out_split


def weight_grads(
    which, unpacked, inner, gain, cot, back_inner, mixed, order, added, norm_factor, lat_size, z_size
):
    own, channels = inner.shape
    lane = channels // lat_size
    wide = mixed.shape[0] * mixed.shape[2]
    rows = 2 * channels + channels // 2 * (wide // channels)
    operands = (unpacked, inner, gain, cot, back_inner, mixed, order)
    if added is not None:
        operands += (added,)
    in_specs = [pl.BlockSpec(memory_space=pltpu.VMEM)] * len(operands)
    in_specs[6] = pl.BlockSpec(memory_space=pl.ANY)
    tall, short = pltpu.VMEM((3 * channels, own), BF16), pltpu.VMEM((channels, own), BF16)
    return pl.pallas_call(
        functools.partial(weight_grads_kernel, norm_factor, z_size),
        out_shape=jax.ShapeDtypeStruct((lat_size, rows, lane), BF16),
        in_specs=[pl.BlockSpec(memory_space=pltpu.SMEM)] + in_specs,
        scratch_shapes=[
            tall,
            short,
            short,
            pltpu.VMEM((3 * channels // 2, own), BF16),
            pltpu.VMEM((channels // 2, own), BF16),
            pltpu.VMEM((channels // 2, own), BF16),
        ],
        compiler_params=pltpu.CompilerParams(vmem_limit_bytes=20 * 1024 * 1024),
        cost_estimate=pl.CostEstimate(
            flops=own * channels * (4 * channels + wide),
            bytes_accessed=2 * channels * (8 * channels + 2 * wide),
            transcendentals=0,
        ),
        name="weight_grads",
    )(which.reshape(1), *operands)


def sum_kernel(parts_ref, out_ref):
    out_ref[...] = summed(parts_ref, slice(None)).astype(BF16)


def sum_parts(parts, steps):
    count, rows, lane = parts.shape
    block = rows // steps
    return pl.pallas_call(
        sum_kernel,
        grid=(steps,),
        out_shape=jax.ShapeDtypeStruct((rows, lane), BF16),
        in_specs=[pl.BlockSpec((count, block, lane), lambda step: (0, step, 0))],
        out_specs=pl.BlockSpec((block, lane), lambda step: (step, 0)),
        name="sum_bands",
    )(parts)


def pack_kernel(
    left_ref, right_ref, mine_ref, theirs_ref, first_gain_ref, second_gain_ref, out_ref
):
    rows, lane = left_ref.shape[1:]
    out_ref[:, 0:rows, :] = (left_ref[...].astype(F32) + right_ref[...].astype(F32)).astype(BF16)
    small = []
    for ref in (mine_ref, theirs_ref):
        for z in range(ref.shape[0]):
            for start in range(0, ref.shape[2], lane):
                small.append(ref[z, :, start : start + lane])
    for ref in (first_gain_ref, second_gain_ref):
        for start in range(0, ref.shape[1], lane):
            small.append(ref[:, start : start + lane])
    small = jnp.concatenate(small, axis=0).astype(BF16)
    for lat in range(out_ref.shape[0]):
        out_ref[lat, rows:, :] = small


def summed(ref, rows):
    total = ref[0, rows, :].astype(F32)
    for part in range(1, ref.shape[0]):
        total = total + ref[part, rows, :].astype(F32)
    return total


def merge_kernel(parts_ref, output_ref, input_ref, out_ref):
    z_size, out_rows, _ = out_ref.shape
    rows = parts_ref.shape[1]
    block = (rows - out_rows) // (z_size - 1)
    small = summed(parts_ref, slice(z_size * block, rows)).astype(BF16)
    for z in range(z_size):
        out_ref[z, 0:block, :] = summed(parts_ref, slice(z * block, (z + 1) * block)).astype(BF16)
        out_ref[z, block:, :] = small


def first_kernel(parts_ref, shrink_ref, in_ref, out_ref):
    lane = parts_ref.shape[1]
    in_split, out_split = in_ref.shape[0], out_ref.shape[0]
    at = in_split + out_split
    in_ref[...] = parts_ref[0:in_split, :].astype(F32)
    out_ref[...] = parts_ref[in_split:at, :].astype(F32)
    for piece in range(shrink_ref.shape[1] // lane):
        shrink_ref[:, piece * lane : (piece + 1) * lane] = parts_ref[at : at + out_split, :].astype(
            F32
        )
        at += out_split


def second_kernel(parts_ref, expand_ref, small_ref):
    block, split = expand_ref.shape
    lane = parts_ref.shape[2]
    at = 0
    for piece in range(split // lane):
        expand_ref[:, piece * lane : (piece + 1) * lane] = summed(parts_ref, slice(at, at + block))
        at += block
    small_ref[...] = summed(parts_ref, slice(at, parts_ref.shape[1]))


def small_kernel(
    split, core_ref, mine_ref, theirs_ref, depth_ref, first_gain_ref, second_gain_ref
):
    lane = mine_ref.shape[1]
    wide = depth_ref.shape[2]
    channels = first_gain_ref.shape[1]
    half_rows = 9 * wide // 2 // lane
    core = core_ref[0]
    pieces = wide // lane
    in_block = split // lane
    for side in range(2):
        which = core if side == 0 else 1 - core
        for piece in range(pieces // 2):
            own_at = side * half_rows + piece * 9
            other_at = (1 - side) * half_rows + piece * 9
            block = mine_ref[own_at : own_at + 9, :] + theirs_ref[other_at : other_at + 9, :]
            z, rest = divmod(piece, in_block)
            start = pl.multiple_of((2 * z + which) * split, lane) + rest * lane
            for a in range(3):
                depth_ref[a, :, pl.ds(pl.multiple_of(start, lane), lane)] = block[3 * a : 3 * a + 3]
    at = 2 * half_rows
    for ref in (first_gain_ref, second_gain_ref):
        for start in range(0, channels, lane):
            ref[:, start : start + lane] = mine_ref[at : at + 1, :] + theirs_ref[at : at + 1, :]
            at += 1


def backward_kernel(
    frame, norm_factor, which_ref, back_ref, state_ref, gain_ref, inside_ref, earlier_ref, order_ref,
    shrink_ref, slope_ref, activated_ref, expand_ref, expand_slope_ref, kernel_ref, part_ref,
    depth_ref, input_ref, gain_grad_ref, back_normed, normed,
):
    step = pl.program_id(0)
    cells, channels = state_ref.shape
    row_count, lon_count, _ = input_ref.shape
    lat_size, _, _, lane = part_ref.shape
    block = channels // lat_size
    inside = inside_ref[...]

    @pl.when(step == 0)
    def _():
        normed[...] = normalise(state_ref[...].astype(F32), gain_ref[...]).T
        back_normed[...] = earlier_ref[...]

    kernel = kernel_ref[...]
    back_convolved = (
        (times_transpose(back_ref[...], shrink_ref[...]) * slope_ref[0].astype(F32))
        .astype(BF16)
        .astype(F32)
    )
    flipped = jnp.concatenate([kernel[8 - i : 9 - i] for i in range(9)], axis=0)
    back_activated = convolve(back_convolved, flipped, row_count, frame)
    back_expanded = jnp.where(inside > 0, back_activated * expand_slope_ref[0].astype(F32), 0.0).astype(BF16)
    expand_grad = (matmul(normed[...], back_expanded) * norm_factor).astype(BF16)
    for lat in range(lat_size):
        for piece in range(expand_grad.shape[1] // lane):
            part_ref[lat, 0, piece * block : (piece + 1) * block, :] = expand_grad[
                lat * block : (lat + 1) * block, piece * lane : (piece + 1) * lane
            ]
    back_normed[...] += times_transpose(back_expanded, expand_ref[...])
    own_back = jnp.where(inside > 0, back_convolved[frame : frame + cells], 0.0)
    activated = activated_ref[0].astype(F32)
    for b in range(3):
        moved = own_back
        if b != 1:
            moved = pltpu.roll(own_back, cells - 1 if b == 0 else 1, 0)
        for a in range(3):
            depth_ref[0, 3 * a + b : 3 * a + b + 1, :] = norm_factor * jnp.sum(
                activated[a * frame : a * frame + cells] * moved, axis=0, keepdims=True
            )

    @pl.when(step == pl.num_programs(0) - 1)
    def _():
        state = state_ref[...].astype(F32)
        inverse = inverse_rms(state)
        grads = back_normed[...]
        gain_grad_ref[...] = norm_factor * jnp.sum(grads * state * inverse, axis=0, keepdims=True)
        result = (
            back_ref[frame : frame + cells, :].astype(F32)
            + norm_back(grads, state, inverse, gain_ref[...])
        ).astype(BF16)
        for row in range(row_count):
            start = row * frame + SIDE
            input_ref[row] = result[start : start + lon_count]


def backward(
    which, back, state, gain, inside, earlier, order, shrink_weight, slope, activated, expand_weight,
    expand_slope, kernel, norm_factor, lat_size, row_count, lon_count,
):
    cells, channels = state.shape
    frame = cells // row_count
    size = activated.shape[1]
    wide = expand_weight.shape[1]
    part = step_width(wide)
    steps = wide // part
    place = lambda step, which: step
    if which is not None:
        steps = steps // 2
        place = lambda step, which: 2 * step + which[0]
    else:
        which = 0
    fixed = lambda shape: pl.BlockSpec(shape, lambda step, which: (0,) * len(shape))
    moving = lambda rows: pl.BlockSpec((rows, part), lambda step, which: (0, place(step, which)))
    whole = lambda rows: pl.BlockSpec((1, rows, part), lambda step, which: (place(step, which), 0, 0))
    block = channels // lat_size
    lane = block
    pieces = part // lane
    return pl.pallas_call(
        functools.partial(backward_kernel, frame, norm_factor),
        grid_spec=pltpu.PrefetchScalarGridSpec(
            num_scalar_prefetch=1,
            grid=(steps,),
            in_specs=[
                fixed((size, channels)),
                fixed((cells, channels)),
                fixed((1, channels)),
                fixed((cells, 1)),
                fixed((cells, channels)),
                pl.BlockSpec(memory_space=pl.ANY),
                pl.BlockSpec((part, channels), lambda step, which: (place(step, which), 0)),
                whole(size),
                whole(size),
                moving(channels),
                whole(cells),
                moving(9),
            ],
            out_specs=(
                pl.BlockSpec((lat_size, 1, pieces * block, lane), lambda step, which: (0, step, 0, 0)),
                pl.BlockSpec((1, 9, part), lambda step, which: (step, 0, 0)),
                fixed((row_count, lon_count, channels)),
                fixed((1, channels)),
                fixed((cells, channels)),
            ),
            scratch_shapes=[pltpu.VMEM((channels, cells), BF16)],
        ),
        out_shape=(
            jax.ShapeDtypeStruct((lat_size, steps, pieces * block, lane), BF16),
            jax.ShapeDtypeStruct((steps, 9, part), F32),
            jax.ShapeDtypeStruct((row_count, lon_count, channels), BF16),
            jax.ShapeDtypeStruct((1, channels), F32),
            jax.ShapeDtypeStruct((cells, channels), F32),
        ),
        compiler_params=pltpu.CompilerParams(
            vmem_limit_bytes=56 * 1024 * 1024, dimension_semantics=("arbitrary",)
        ),
        cost_estimate=pl.CostEstimate(
            flops=8 * cells * channels * part * steps,
            bytes_accessed=(6 * channels + 12 * size) * part * steps,
            transcendentals=0,
        ),
        name="backward",
    )(
        jnp.reshape(which, (1,)).astype(jnp.int32), back, state, gain, inside, earlier, order,
        shrink_weight, slope, activated, expand_weight, expand_slope, kernel,
    )


def attention_kernel(
    head_width, query_block, qkv_ref, early_ref, order_ref, out_ref, heads_t, query_grad_t, key_t,
    value_t, back_ref, bias_ref, key_grad, value_grad, score_ref, back_prob_ref, prob_low_ref, back_score_ref,
):
    head = pl.program_id(0)
    cells = qkv_ref.shape[0]
    width = qkv_ref.shape[1] // 3
    sources = early_ref.shape[0]
    frame = cells // sources
    scale = 1.0 / math.sqrt(head_width)
    keys = qkv_ref[:, width : 2 * width]
    values = qkv_ref[:, 2 * width : 3 * width]
    part = 2 * frame

    @pl.when(head == 0)
    def _():
        key_t[...] = keys.T
        value_t[...] = values.T
        for source in range(sources):
            at = slice(source * frame, (source + 1) * frame)
            back_ref[at, :] = early_ref[source, 0:frame, 0:width]
            if early_ref.shape[1] > frame:
                bias_ref[at, :] = early_ref[source, frame:, :].astype(F32).T[0:frame]
            else:
                bias_ref[at, :] = early_ref[source, :, width:].astype(F32)
        key_grad[...] = jnp.zeros_like(key_grad)
        value_grad[...] = jnp.zeros_like(value_grad)

    lanes = lax.broadcasted_iota(jnp.int32, (1, width), 1) // head_width == head
    zero = jnp.zeros((), BF16)
    heads = lax.broadcasted_iota(jnp.int32, bias_ref.shape, 1)
    bias = LOG2E * jnp.sum(
        jnp.where(heads == head, bias_ref[...], 0.0), axis=1, keepdims=True
    )
    rows = pl.ds(pl.multiple_of(head * head_width, head_width), head_width)
    head_key_t = key_t[rows, :]
    head_value_t = value_t[rows, :]
    last_dims = (((1,), (1,)), ((), ()))

    def fold(values, combine):
        result = values[0:8]
        for start in range(8, values.shape[0], 8):
            result = combine(result, values[start : start + 8])
        return result

    def block(start):
        cols = pl.ds(start, query_block)
        queries = jnp.where(lanes, qkv_ref[cols, 0:width], zero)
        backs = jnp.where(lanes, back_ref[cols, :], zero)
        parts = [slice(i, i + part) for i in range(0, cells, part)]
        highest = jnp.full((8, query_block), -jnp.inf, F32)
        for at in parts:
            scores = lax.dot_general(
                qkv_ref[at, width : 2 * width], queries, last_dims, preferred_element_type=F32
            )
            scores = scores * (scale * LOG2E) + bias[at]
            score_ref[at, :] = scores
            highest = jnp.maximum(highest, fold(scores, jnp.maximum))
        highest = jnp.max(highest, axis=0, keepdims=True)
        total = jnp.zeros((8, query_block), F32)
        centred = jnp.zeros((8, query_block), F32)
        for at in parts:
            back_probs = lax.dot_general(
                qkv_ref[at, 2 * width : 3 * width], backs, last_dims, preferred_element_type=F32
            )
            exponent = jnp.exp2(score_ref[at, :] - highest)
            total = total + fold(exponent, jnp.add)
            centred = centred + fold(exponent * back_probs, jnp.add)
            score_ref[at, :] = exponent
            back_prob_ref[at, :] = back_probs
        inverse = 1.0 / jnp.sum(total, axis=0, keepdims=True)
        centred = jnp.sum(centred, axis=0, keepdims=True) * inverse
        for at in parts:
            probs = score_ref[at, :] * inverse
            probs_low = probs.astype(BF16)
            back_scores = (probs * (back_prob_ref[at, :] - centred)).astype(BF16)
            prob_low_ref[at, :] = probs_low
            back_score_ref[at, :] = back_scores
            value_grad[at, :] += matmul(probs_low, backs)
            key_grad[at, :] += matmul(back_scores, queries)
        heads_t[rows, cols] = matmul(head_value_t, prob_low_ref[...])
        query_grad_t[rows, cols] = matmul(head_key_t, back_score_ref[...])

    block_count = cells // query_block
    if block_count <= 4:
        for index in range(block_count):
            block(index * query_block)
    else:

        def step(index, carry):
            block(pl.multiple_of(index * query_block, query_block))
            return carry

        lax.fori_loop(0, block_count, step, 0)

    @pl.when(head == pl.num_programs(0) - 1)
    def _():
        out_ref[:, 0:width] = heads_t[...].T.astype(BF16)
        out_ref[:, width : 2 * width] = (query_grad_t[...] * scale).T.astype(BF16)
        out_ref[:, 2 * width : 3 * width] = (key_grad[...] * scale).astype(BF16)
        out_ref[:, 3 * width : 4 * width] = value_grad[...].astype(BF16)


def attention(qkv, early, order, head_width):
    cells = qkv.shape[0]
    width = qkv.shape[1] // 3
    items = width // head_width
    bias_columns = BIAS_ROWS if early.shape[2] == width else items
    query_block = cells if cells <= 1024 else 256
    whole = lambda shape: pl.BlockSpec(shape, lambda head: (0,) * len(shape))
    return pl.pallas_call(
        functools.partial(attention_kernel, head_width, query_block),
        grid=(items,),
        out_shape=jax.ShapeDtypeStruct((cells, 4 * width), BF16),
        in_specs=[whole(qkv.shape), whole(early.shape), pl.BlockSpec(memory_space=pl.ANY)],
        out_specs=whole((cells, 4 * width)),
        scratch_shapes=[
            pltpu.VMEM((width, cells), F32),
            pltpu.VMEM((width, cells), F32),
            pltpu.VMEM((width, cells), BF16),
            pltpu.VMEM((width, cells), BF16),
            pltpu.VMEM((cells, width), BF16),
            pltpu.VMEM((cells, bias_columns), F32),
            pltpu.VMEM((cells, width), F32),
            pltpu.VMEM((cells, width), F32),
            pltpu.VMEM((cells, query_block), F32),
            pltpu.VMEM((cells, query_block), F32),
            pltpu.VMEM((cells, query_block), BF16),
            pltpu.VMEM((cells, query_block), BF16),
        ],
        compiler_params=pltpu.CompilerParams(
            vmem_limit_bytes=(20 if cells <= 1024 else 48) * 1024 * 1024, dimension_semantics=("arbitrary",)
        ),
        cost_estimate=pl.CostEstimate(
            flops=items * cells * cells * 32 * 14,
            bytes_accessed=cells * width * 16,
            transcendentals=items * cells * cells,
        ),
        name="attention",
    )(qkv, early, order)


def per_device(
    state_field,
    cotangent,
    key_bias,
    input_gain,
    expand_weight,
    depth_weight,
    shrink_weight,
    attention_gain,
    attention_in,
    attention_out,
):
    row_count, lon_count, channels = state_field.shape
    head_count = key_bias.shape[2]
    head_width = channels // head_count
    wide = expand_weight.shape[1]
    lat_size, z_size = lax.axis_size("lat"), lax.axis_size("z")
    lon_size = 2 * z_size
    core = lax.axis_index("core")
    norm_factor = 1.0 / math.sqrt(row_count * lon_count * lat_size * lon_size)
    items = row_count * head_count // lon_size
    groups = head_count // items
    width = items * head_width
    frame = lon_count + 2 * SIDE
    own = row_count * frame
    kernel = depth_weight.astype(F32).reshape(9, wide)
    input_gain = input_gain.reshape(1, channels)
    attention_gain = attention_gain.reshape(1, channels)

    low, high = from_sides(state_field, SIDE, 1, LON, True)
    state = jnp.concatenate([low, state_field, high], axis=1)
    if row_count == 1:
        below, above = from_sides(state, 1, 0, "lat", False)
        far_below = lax.ppermute(below, "lat", shifts(lat_size, 1, False))
        far_above = lax.ppermute(above, "lat", shifts(lat_size, -1, False))
        all_rows = [far_below, below, state, above, far_above]
    else:
        below, above = from_sides(state, 2, 0, "lat", False)
        all_rows = [below, state, above]
    all_rows = jnp.concatenate(all_rows, axis=0)

    early, cot = early_parts(cotangent, key_bias, attention_out, state, groups)
    early = exchange(early, LON)

    qkv, inner = forward(
        all_rows, input_gain, expand_weight, kernel, shrink_weight, attention_gain, attention_in,
        groups,
    )
    activated, slope, mixed, expand_slope = around(
        all_rows, input_gain, expand_weight, kernel, inner
    )
    qkv = exchange(qkv, LON).reshape(lon_size * frame, 3 * width)

    attended = attention(qkv, early, mixed, head_width)
    attended = exchange(attended.reshape(lon_size, frame, 4 * width), LON)
    cot = cot.reshape(own, channels)
    output_field, back_inner, unpacked, gain_two = call(
        functools.partial(inner_kernel, groups, norm_factor),
        "back_inner",
        (
            jax.ShapeDtypeStruct((row_count, lon_count, channels), BF16),
            jax.ShapeDtypeStruct((own, channels), BF16),
            jax.ShapeDtypeStruct((own, 4 * channels), BF16),
            jax.ShapeDtypeStruct((1, channels), F32),
        ),
        attended,
        inner,
        cot,
        attention_out,
        attention_in,
        attention_gain,
        flops=8 * own * channels * channels,
    )

    back = back_inner.reshape(row_count, frame, channels)
    centre = back[:, SIDE : SIDE + lon_count]
    low, high = from_sides(centre, 1, 1, LON, True)
    edge = jnp.zeros((row_count, SIDE - 1, channels), BF16)
    back_sides = jnp.concatenate([edge, low, centre, high, edge], axis=1)
    below, above = from_sides(back_sides, 1, 0, "lat", False)
    back = jnp.concatenate([below, back_sides, above], axis=0).reshape(-1, channels)

    lane = channels // lat_size
    in_split, out_split, split = 3 * channels // lon_size, channels // lon_size, wide // lon_size
    grads = lambda which, order, added: weight_grads(
        which, unpacked, inner, attention_gain, cot, back_inner, mixed, order, added, norm_factor,
        lat_size, z_size,
    )
    theirs = grads(1 - core, back_sides, None)
    first = grads(core, back, core_swap(theirs))
    first_sums = sum_parts(exchange(first, "lat"), z_size)
    first_sums = lax.psum_scatter(first_sums, "z", scatter_dimension=0, tiled=True)
    flat = lambda parts: parts.reshape(lat_size, -1, lane)

    columns = lax.broadcasted_iota(jnp.int32, (row_count, frame, 1), 1).reshape(own, 1)
    inside = ((columns >= SIDE) & (columns < SIDE + lon_count)).astype(F32)
    state = state.reshape(own, channels)

    def backward_part(which, earlier, order):
        return backward(
            which, back, state, input_gain, inside, earlier, order, shrink_weight, slope, activated,
            expand_weight, expand_slope, kernel, norm_factor, lat_size, row_count, lon_count,
        )

    start = jnp.zeros((own, channels), F32)
    if split == step_width(wide):
        theirs, depth_theirs, _, _, partial = backward_part(1 - core, start, first)
        theirs = core_swap(theirs)
        mine, depth_mine, input_grad, gain_one, _ = backward_part(core, partial, first)
    else:
        parts, depth, input_grad, gain_one, _ = backward_part(None, start, first)
        steps = parts.shape[1]
        parts = parts.reshape(lat_size, steps, -1, split // lane, lane, lane)
        parts = parts.reshape(lat_size, z_size, 2, split // lane * lane, lane)
        theirs = core_swap(lax.dynamic_index_in_dim(parts, 1 - core, 2, False))
        mine = lax.dynamic_index_in_dim(parts, core, 2, False)
        depth = depth.reshape(steps, 9, -1, split).transpose(0, 2, 1, 3)
        depth = depth.reshape(z_size, 2, 9, split)
        depth_theirs = lax.dynamic_index_in_dim(depth, 1 - core, 1, False)
        depth_mine = lax.dynamic_index_in_dim(depth, core, 1, False)

    mine, theirs = flat(mine), flat(theirs)
    block_rows = mine.shape[1] // z_size
    small_rows = (9 * wide + 2 * channels) // lane
    output_field = output_field.transpose(1, 0, 2)
    input_grad = input_grad.transpose(1, 0, 2)
    second = call(
        pack_kernel,
        "pack",
        jax.ShapeDtypeStruct((lat_size, z_size * block_rows + small_rows, lane), BF16),
        mine,
        theirs,
        depth_mine,
        depth_theirs,
        gain_one,
        gain_two,
    )
    second = call(
        merge_kernel,
        "merge",
        jax.ShapeDtypeStruct((z_size, block_rows + small_rows, lane), BF16),
        exchange(second, "lat"),
        output_field,
        input_grad,
        specs=[pl.BlockSpec(memory_space=pltpu.VMEM)] + [pl.BlockSpec(memory_space=pl.ANY)] * 2,
    )
    weight = lambda rows, cols: jax.ShapeDtypeStruct((rows, cols), F32)
    expand_grad, small = call(
        second_kernel,
        "expand_grad",
        (weight(lane, split), weight(small_rows, lane)),
        exchange(second, "z"),
    )
    other = core_swap(small)
    if split % 128 == 0:
        depth_grad, input_gain_grad, attention_gain_grad = pl.pallas_call(
            functools.partial(small_kernel, split),
            out_shape=(
                jax.ShapeDtypeStruct((3, 3, wide), F32),
                weight(1, channels),
                weight(1, channels),
            ),
            in_specs=[
                pl.BlockSpec(memory_space=pltpu.SMEM),
                pl.BlockSpec(memory_space=pltpu.VMEM),
                pl.BlockSpec(memory_space=pltpu.VMEM),
            ],
            name="small_grads",
        )(core.reshape(1), small, other)
    else:
        rows = 9 * wide // 2 // lane
        own_half = small[:rows] + other[rows : 2 * rows]
        other_half = small[rows : 2 * rows] + other[:rows]
        depth_grad = jnp.where(
            core == 0, jnp.stack([own_half, other_half]), jnp.stack([other_half, own_half])
        )
        depth_grad = depth_grad.reshape(2, z_size, split // lane, 9, lane).transpose(3, 1, 0, 2, 4)
        depth_grad = depth_grad.reshape(3, 3, wide)
        gains = (small[2 * rows :] + other[2 * rows :]).reshape(2, channels)
        input_gain_grad, attention_gain_grad = gains[0], gains[1]
    shrink_grad, attention_in_grad, attention_out_grad = call(
        first_kernel,
        "shrink_and_attention_grads",
        (
            weight(out_split, wide // lat_size),
            weight(in_split, lane),
            weight(out_split, lane),
        ),
        first_sums,
    )
    return (
        output_field.transpose(1, 0, 2),
        input_grad.transpose(1, 0, 2),
        expand_grad,
        shrink_grad.T,
        attention_in_grad.T,
        attention_out_grad.T,
        depth_grad,
        input_gain_grad.reshape(channels),
        attention_gain_grad.reshape(channels),
    )


def solution(mesh):
    lat_size, lon_size = mesh.devices.shape
    split = Mesh(mesh.devices.reshape(lat_size, lon_size // 2, 2), ("lat", "z", "core"))
    grid = P("lat", LON, None)
    weight = P("lat", LON)

    def step(*arrays):
        outputs = jax.shard_map(
            per_device,
            mesh=split,
            in_specs=(grid, grid, grid) + (P(),) * 7,
            out_specs=(grid, grid, weight, weight, weight, weight, P(), P(), P()),
            check_vma=False,
        )(*arrays)
        return outputs

    return step
```

```python
import functools
import math

import jax
import jax.numpy as jnp
from jax import lax
from jax.experimental import pallas as pl
from jax.experimental.pallas import tpu as pltpu
from jax.sharding import Mesh
from jax.sharding import PartitionSpec as P

EPSILON = 1e-06
LON = ("z", "core")
BF16 = jnp.bfloat16
F32 = jnp.float32
MASKED = -1e30
SIDE = 3
BIAS_ROWS = 16
FORWARD_WIDTH = 512
LOG2E = math.log2(math.e)


def inverse_rms(values):
    return lax.rsqrt(jnp.mean(values * values, axis=-1, keepdims=True) + EPSILON)


def norm_back(back_normed, state, inverse, gain):
    scaled = back_normed * gain
    return inverse * scaled - inverse * inverse * inverse * state * jnp.mean(
        scaled * state, axis=-1, keepdims=True
    )


def shifts(count, step, periodic):
    return [(i, (i + step) % count) for i in range(count) if periodic or 0 <= i + step < count]


def from_sides(block, width, dim, axis, periodic):
    count = lax.axis_size(axis)
    size = block.shape[dim]
    low = lax.ppermute(
        lax.slice_in_dim(block, size - width, size, axis=dim), axis, shifts(count, 1, periodic)
    )
    high = lax.ppermute(
        lax.slice_in_dim(block, 0, width, axis=dim), axis, shifts(count, -1, periodic)
    )
    return low, high


def core_swap(values):
    return lax.ppermute(values, "core", [(0, 1), (1, 0)])


def exchange(values, axis):
    return lax.all_to_all(values, axis, 0, 0, tiled=True)


def matmul(left, right):
    return jnp.dot(left, right, preferred_element_type=F32)


def times_transpose(values, weights):
    return lax.dot_general(
        values, weights, (((values.ndim - 1,), (1,)), ((), ())), preferred_element_type=F32
    )


def sigmoid(values):
    return 0.5 + 0.5 * jnp.tanh(0.5 * values)


def silu(values):
    return values * sigmoid(values)


def call(kernel, name, out_shape, *operands, scratch=(), megabytes=16, flops=0, specs=None, out_specs=None, aliases=None):
    return pl.pallas_call(
        kernel,
        out_shape=out_shape,
        scratch_shapes=scratch,
        in_specs=specs or [pl.BlockSpec(memory_space=pltpu.VMEM)] * len(operands),
        out_specs=out_specs
        or jax.tree.map(lambda _: pl.BlockSpec(memory_space=pltpu.VMEM), out_shape),
        input_output_aliases=aliases or {},
        compiler_params=pltpu.CompilerParams(vmem_limit_bytes=megabytes * 1024 * 1024),
        cost_estimate=pl.CostEstimate(
            flops=flops,
            bytes_accessed=sum(x.size * x.dtype.itemsize for x in operands),
            transcendentals=0,
        ),
        name=name,
    )(*operands)


def early_kernel(
    groups, cot_ref, bias_ref, out_weight_ref, order_ref, early_ref, framed_ref, bias_frame
):
    row_count, lon_count, channels = cot_ref.shape
    frame = framed_ref.shape[1]
    width = channels // groups
    head_count = bias_ref.shape[2]
    items = head_count // groups
    in_rows = early_ref.shape[2] == width
    framed_ref[...] = jnp.zeros_like(framed_ref)
    bias_frame[...] = jnp.full_like(bias_frame, MASKED)
    for row in range(row_count):
        framed_ref[row, SIDE : SIDE + lon_count, :] = cot_ref[row]
        bias_frame[row, SIDE : SIDE + lon_count, 0:head_count] = bias_ref[row].astype(F32)
    for row in range(row_count):
        back_heads = times_transpose(framed_ref[row], out_weight_ref[...]).astype(BF16)
        bias = bias_frame[row].T if in_rows else bias_frame[row]
        for group in range(groups):
            target = row * groups + group
            early_ref[target, 0:frame, 0:width] = back_heads[:, group * width : (group + 1) * width]
            if in_rows:
                early_ref[target, frame:, :] = bias[
                    group * items : group * items + BIAS_ROWS
                ].astype(BF16)
            else:
                early_ref[target, :, width:] = bias[
                    0:frame, group * items : (group + 1) * items
                ].astype(BF16)


def early_parts(cotangent, key_bias, attention_out, order, groups):
    row_count, lon_count, channels = cotangent.shape
    frame = lon_count + 2 * SIDE
    head_count = key_bias.shape[2]
    width = channels // groups
    if frame <= width and width % 128 == 0:
        shape = (row_count * groups, frame + BIAS_ROWS, width)
        bias_shape = (row_count, width, max(128, head_count + BIAS_ROWS))
    else:
        shape = (row_count * groups, frame, width + head_count // groups)
        bias_shape = (row_count, frame, head_count)
    return call(
        functools.partial(early_kernel, groups),
        "back_heads",
        (
            jax.ShapeDtypeStruct(shape, BF16),
            jax.ShapeDtypeStruct((row_count, frame, channels), BF16),
        ),
        cotangent,
        key_bias,
        attention_out,
        order,
        scratch=[pltpu.VMEM(bias_shape, F32)],
        flops=2 * row_count * frame * channels * channels,
    )


def normalise(values, gain):
    return (values * inverse_rms(values) * gain).astype(BF16)


def convolve(values, kernel, rows, frame):
    size = rows * frame
    total = None
    for b in range(3):
        part = kernel[b : b + 1] * values[0:size]
        for a in range(1, 3):
            part = part + kernel[3 * a + b : 3 * a + b + 1] * values[a * frame : a * frame + size]
        if b != 1:
            part = pltpu.roll(part, 1 if b == 0 else size - 1, 0)
        total = part if total is None else total + part
    return total


def forward_kernel(
    frame, groups, steps, state_ref, gain_ref, kernel_ref, second_gain_ref, expand_hbm, shrink_hbm,
    in_hbm, qkv_ref, inner_ref, expand_ref, shrink_ref, in_ref, normed, total, arrived,
):
    cells, channels = inner_ref.shape
    wide = expand_ref.shape[1]
    rows = cells // frame
    width = channels // groups
    part = wide // steps
    parts = [slice(i * part, (i + 1) * part) for i in range(steps)]
    expand_copies, shrink_copies = [], []
    for i, cols in enumerate(parts):
        expand_copies.append(
            pltpu.make_async_copy(expand_hbm.at[:, cols], expand_ref.at[:, cols], arrived.at[i])
        )
        shrink_copies.append(
            pltpu.make_async_copy(shrink_hbm.at[cols], shrink_ref.at[cols], arrived.at[steps + i])
        )
        expand_copies[i].start()
        shrink_copies[i].start()
    in_copy = pltpu.make_async_copy(in_hbm, in_ref, arrived.at[2 * steps])
    in_copy.start()
    near = state_ref[frame : frame + normed.shape[0], :].astype(F32)
    normed[...] = normalise(near, gain_ref[...])
    for i, cols in enumerate(parts):
        expand_copies[i].wait()
        activated = silu(matmul(normed[...], expand_ref[:, cols])).astype(BF16).astype(F32)
        mixed = silu(convolve(activated, kernel_ref[:, cols], rows, frame)).astype(BF16)
        shrink_copies[i].wait()
        product = matmul(mixed, shrink_ref[cols])
        total[...] = product if i == 0 else total[...] + product
    inner = state_ref[2 * frame : 2 * frame + cells, :].astype(F32)
    inner = (inner + total[...]).astype(BF16)
    inner_ref[...] = inner
    normed_second = normalise(inner.astype(F32), second_gain_ref[...])
    in_copy.wait()
    projected = matmul(normed_second, in_ref[...]).astype(BF16)
    for row in range(rows):
        for group in range(groups):
            for kind in range(3):
                start = kind * channels + group * width
                qkv_ref[row * groups + group, :, kind * width : (kind + 1) * width] = projected[
                    row * frame : (row + 1) * frame, start : start + width
                ]


def step_width(wide):
    return 256 if wide % 256 == 0 else wide


def forward(state, input_gain, expand_weight, kernel, shrink_weight, gain, attention_in, groups):
    all_rows, frame, channels = state.shape
    rows = all_rows - 4
    cells = rows * frame
    wide = expand_weight.shape[1]
    steps = wide // FORWARD_WIDTH
    here, away = pl.BlockSpec(memory_space=pltpu.VMEM), pl.BlockSpec(memory_space=pl.ANY)
    return pl.pallas_call(
        functools.partial(forward_kernel, frame, groups, steps),
        out_shape=(
            jax.ShapeDtypeStruct((rows * groups, frame, 3 * channels // groups), BF16),
            jax.ShapeDtypeStruct((cells, channels), BF16),
        ),
        in_specs=[here] * 4 + [away] * 3,
        scratch_shapes=[
            pltpu.VMEM(expand_weight.shape, BF16),
            pltpu.VMEM(shrink_weight.shape, BF16),
            pltpu.VMEM(attention_in.shape, BF16),
            pltpu.VMEM((cells + 2 * frame, channels), BF16),
            pltpu.VMEM((cells, channels), F32),
            pltpu.SemaphoreType.DMA((2 * steps + 1,)),
        ],
        compiler_params=pltpu.CompilerParams(vmem_limit_bytes=56 * 1024 * 1024),
        cost_estimate=pl.CostEstimate(
            flops=2 * cells * channels * (3 * wide + 3 * channels),
            bytes_accessed=4 * channels * wide + 6 * channels * channels,
            transcendentals=3 * cells * wide,
        ),
        name="forward",
    )(
        state.reshape(all_rows * frame, channels),
        input_gain,
        kernel,
        gain,
        expand_weight,
        shrink_weight,
        attention_in,
    )


def around_kernel(
    frame, state_ref, gain_ref, expand_ref, kernel_ref, order_ref, activated_ref, slope_ref, mixed_ref,
    expand_slope_ref, normed,
):
    size = activated_ref.shape[1]
    cells = mixed_ref.shape[1]

    @pl.when(pl.program_id(0) == 0)
    def _():
        normed[...] = normalise(state_ref[...].astype(F32), gain_ref[...])

    expanded = matmul(normed[...], expand_ref[...])
    gate = sigmoid(expanded)
    activated = (expanded * gate).astype(BF16)
    activated_ref[0] = activated[frame : frame + size]
    own_gate, own = gate[2 * frame : 2 * frame + cells], expanded[2 * frame : 2 * frame + cells]
    expand_slope_ref[0] = (own_gate * (1.0 + own * (1.0 - own_gate))).astype(BF16)
    convolved = convolve(activated.astype(F32), kernel_ref[0], size // frame, frame)
    gate = sigmoid(convolved)
    slope_ref[0] = (gate * (1.0 + convolved * (1.0 - gate))).astype(BF16)
    mixed_ref[0] = (
        convolved[frame : frame + cells] * gate[frame : frame + cells]
    ).astype(BF16)


def around(state, input_gain, expand_weight, kernel, order):
    all_rows, frame, channels = state.shape
    size, cells = (all_rows - 2) * frame, (all_rows - 4) * frame
    wide = expand_weight.shape[1]
    part = step_width(wide)
    fixed = lambda shape: pl.BlockSpec(shape, lambda step: (0,) * len(shape))
    moving = lambda rows: pl.BlockSpec((rows, part), lambda step: (0, step))
    block = lambda rows: pl.BlockSpec((1, rows, part), lambda step: (step, 0, 0))
    steps = wide // part
    return pl.pallas_call(
        functools.partial(around_kernel, frame),
        grid=(steps,),
        out_shape=(
            jax.ShapeDtypeStruct((steps, size, part), BF16),
            jax.ShapeDtypeStruct((steps, size, part), BF16),
            jax.ShapeDtypeStruct((steps, cells, part), BF16),
            jax.ShapeDtypeStruct((steps, cells, part), BF16),
        ),
        in_specs=[
            fixed((all_rows * frame, channels)),
            fixed((1, channels)),
            moving(channels),
            block(9),
            pl.BlockSpec(memory_space=pl.ANY),
        ],
        out_specs=(block(size), block(size), block(cells), block(cells)),
        scratch_shapes=[pltpu.VMEM((all_rows * frame, channels), BF16)],
        compiler_params=pltpu.CompilerParams(
            vmem_limit_bytes=16 * 1024 * 1024, dimension_semantics=("arbitrary",)
        ),
        cost_estimate=pl.CostEstimate(
            flops=2 * all_rows * frame * channels * wide,
            bytes_accessed=2 * channels * wide + 14 * size * wide,
            transcendentals=2 * size * wide,
        ),
        name="forward_around",
    )(state.reshape(all_rows * frame, channels), input_gain, expand_weight, kernel, order)


def inner_kernel(
    groups, norm_factor, attended_ref, inner_ref, cot_ref, out_weight_ref, in_weight_ref, gain_ref,
    output_ref, back_inner_ref, unpacked_ref, gain_grad_ref,
):
    targets, frame, width = attended_ref.shape
    width = width // 4
    row_count, lon_count, channels = output_ref.shape
    for target in range(targets):
        row, group = divmod(target, groups)
        for kind in range(4):
            start = kind * channels + group * width
            unpacked_ref[row * frame : (row + 1) * frame, start : start + width] = attended_ref[
                target, :, kind * width : (kind + 1) * width
            ]
    inner = inner_ref[...].astype(F32)
    output = (inner + matmul(unpacked_ref[:, :channels], out_weight_ref[...])).astype(BF16)
    for row in range(row_count):
        start = row * frame + SIDE
        output_ref[row] = output[start : start + lon_count]
    back_second = times_transpose(unpacked_ref[:, channels:], in_weight_ref[...])
    inverse = inverse_rms(inner)
    gain_grad_ref[...] = norm_factor * jnp.sum(back_second * inner * inverse, axis=0, keepdims=True)
    back_inner_ref[...] = (
        cot_ref[...].astype(F32) + norm_back(back_second, inner, inverse, gain_ref[...])
    ).astype(BF16)


def weight_grads_kernel(
    norm_factor, z_size, which_ref, unpacked_ref, inner_ref, gain_ref, cot_ref, back_inner_ref,
    mixed_ref, order_ref, *refs
):
    added_ref = refs[0] if len(refs) == 8 else None
    out_ref, whole_in, whole_out, whole_back, in_t, out_t, back_t = refs[-7:]
    lat_size, _, lane = out_ref.shape
    channels = inner_ref.shape[1]
    blocks, _, part = mixed_ref.shape
    blocks = blocks // lat_size
    in_split, out_split = in_t.shape[0] // z_size, out_t.shape[0] // z_size
    first_rows = out_ref.shape[1] // z_size
    normed_second = normalise(inner_ref[...].astype(F32), gain_ref[...])
    whole_in[...] = unpacked_ref[:, channels:].T
    whole_out[...] = cot_ref[...].T
    whole_back[...] = back_inner_ref[...].T
    for z in range(z_size):
        lon = 2 * z + which_ref[0]
        for source, target, split in (
            (whole_in, in_t, in_split),
            (whole_out, out_t, out_split),
            (whole_back, back_t, out_split),
        ):
            target[z * split : (z + 1) * split, :] = source[
                pl.ds(pl.multiple_of(lon * split, split), split), :
            ]

    def put(lat, start, split, values):
        values = values * norm_factor
        for z in range(z_size):
            rows = slice(z * first_rows + start, z * first_rows + start + split)
            value = values[z * split : (z + 1) * split]
            if added_ref is not None:
                value = value + added_ref[lat, rows, :].astype(F32)
            out_ref[lat, rows, :] = value.astype(BF16)

    for lat in range(lat_size):
        cols = slice(lat * lane, (lat + 1) * lane)
        put(lat, 0, in_split, matmul(in_t[...], normed_second[:, cols]))
        put(lat, in_split, out_split, matmul(out_t[...], unpacked_ref[:, cols]))
        start = in_split + out_split
        for block in range(blocks):
            values = matmul(back_t[...], mixed_ref[lat * blocks + block])
            for piece in range(part // lane):
                put(lat, start, out_split, values[:, piece * lane : (piece + 1) * lane])
                start += out_split


def weight_grads(
    which, unpacked, inner, gain, cot, back_inner, mixed, order, added, norm_factor, lat_size, z_size
):
    own, channels = inner.shape
    lane = channels // lat_size
    wide = mixed.shape[0] * mixed.shape[2]
    rows = 2 * channels + channels // 2 * (wide // channels)
    operands = (unpacked, inner, gain, cot, back_inner, mixed, order)
    if added is not None:
        operands += (added,)
    in_specs = [pl.BlockSpec(memory_space=pltpu.VMEM)] * len(operands)
    in_specs[6] = pl.BlockSpec(memory_space=pl.ANY)
    tall, short = pltpu.VMEM((3 * channels, own), BF16), pltpu.VMEM((channels, own), BF16)
    return pl.pallas_call(
        functools.partial(weight_grads_kernel, norm_factor, z_size),
        out_shape=jax.ShapeDtypeStruct((lat_size, rows, lane), BF16),
        in_specs=[pl.BlockSpec(memory_space=pltpu.SMEM)] + in_specs,
        scratch_shapes=[
            tall,
            short,
            short,
            pltpu.VMEM((3 * channels // 2, own), BF16),
            pltpu.VMEM((channels // 2, own), BF16),
            pltpu.VMEM((channels // 2, own), BF16),
        ],
        compiler_params=pltpu.CompilerParams(vmem_limit_bytes=20 * 1024 * 1024),
        cost_estimate=pl.CostEstimate(
            flops=own * channels * (4 * channels + wide),
            bytes_accessed=2 * channels * (8 * channels + 2 * wide),
            transcendentals=0,
        ),
        name="weight_grads",
    )(which.reshape(1), *operands)


def after_kernel(*refs):
    pass


def after(values, *others):
    away = pl.BlockSpec(memory_space=pl.ANY)
    return pl.pallas_call(
        after_kernel,
        out_shape=jax.ShapeDtypeStruct(values.shape, values.dtype),
        in_specs=[away] * (1 + len(others)),
        out_specs=away,
        input_output_aliases={0: 0},
        name="after",
    )(values, *others)


def sum_kernel(parts_ref, out_ref):
    out_ref[...] = summed(parts_ref, slice(None)).astype(BF16)


def sum_parts(parts, steps):
    count, rows, lane = parts.shape
    block = rows // steps
    return pl.pallas_call(
        sum_kernel,
        grid=(steps,),
        out_shape=jax.ShapeDtypeStruct((rows, lane), BF16),
        in_specs=[pl.BlockSpec((count, block, lane), lambda step: (0, step, 0))],
        out_specs=pl.BlockSpec((block, lane), lambda step: (step, 0)),
        compiler_params=pltpu.CompilerParams(vmem_limit_bytes=56 * 1024 * 1024),
        name="sum_bands",
    )(parts)


def pack_kernel(
    left_ref, right_ref, mine_ref, theirs_ref, first_gain_ref, second_gain_ref, out_ref
):
    depth = mine_ref[...] + theirs_ref[...]
    rows, lane = left_ref.shape[1:]
    out_ref[:, 0:rows, :] = (left_ref[...].astype(F32) + right_ref[...].astype(F32)).astype(BF16)
    small = []
    for z in range(depth.shape[0]):
        for start in range(0, depth.shape[2], lane):
            small.append(depth[z, :, start : start + lane])
    for ref in (first_gain_ref, second_gain_ref):
        for start in range(0, ref.shape[1], lane):
            small.append(ref[:, start : start + lane])
    small = jnp.concatenate(small, axis=0).astype(BF16)
    for lat in range(out_ref.shape[0]):
        out_ref[lat, rows:, :] = small


def summed(ref, rows):
    total = ref[0, rows, :].astype(F32)
    for part in range(1, ref.shape[0]):
        total = total + ref[part, rows, :].astype(F32)
    return total


def merge_kernel(parts_ref, output_ref, input_ref, out_ref, output_out, input_out):
    z_size, out_rows, _ = out_ref.shape
    rows = parts_ref.shape[1]
    block = (rows - out_rows) // (z_size - 1)
    small = summed(parts_ref, slice(z_size * block, rows)).astype(BF16)
    for z in range(z_size):
        out_ref[z, 0:block, :] = summed(parts_ref, slice(z * block, (z + 1) * block)).astype(BF16)
        out_ref[z, block:, :] = small


def first_kernel(parts_ref, shrink_ref, in_ref, out_ref):
    lane = parts_ref.shape[1]
    in_split, out_split = in_ref.shape[0], out_ref.shape[0]
    at = in_split + out_split
    in_ref[...] = parts_ref[0:in_split, :].astype(F32)
    out_ref[...] = parts_ref[in_split:at, :].astype(F32)
    for piece in range(shrink_ref.shape[1] // lane):
        shrink_ref[:, piece * lane : (piece + 1) * lane] = parts_ref[at : at + out_split, :].astype(
            F32
        )
        at += out_split


def second_kernel(parts_ref, expand_ref, small_ref):
    block, split = expand_ref.shape
    lane = parts_ref.shape[2]
    at = 0
    for piece in range(split // lane):
        expand_ref[:, piece * lane : (piece + 1) * lane] = summed(parts_ref, slice(at, at + block))
        at += block
    small_ref[...] = summed(parts_ref, slice(at, parts_ref.shape[1]))


def small_kernel(
    split, core_ref, mine_ref, theirs_ref, depth_ref, first_gain_ref, second_gain_ref
):
    lane = mine_ref.shape[1]
    wide = depth_ref.shape[2]
    channels = first_gain_ref.shape[1]
    half_rows = 9 * wide // 2 // lane
    core = core_ref[0]
    pieces = wide // lane
    in_block = split // lane
    for side in range(2):
        which = core if side == 0 else 1 - core
        for piece in range(pieces // 2):
            source = mine_ref if side == 0 else theirs_ref
            block = source[piece * 9 : piece * 9 + 9, :]
            z, rest = divmod(piece, in_block)
            start = pl.multiple_of((2 * z + which) * split, lane) + rest * lane
            for a in range(3):
                depth_ref[a, :, pl.ds(pl.multiple_of(start, lane), lane)] = block[3 * a : 3 * a + 3]
    at = half_rows
    for ref in (first_gain_ref, second_gain_ref):
        for start in range(0, channels, lane):
            ref[:, start : start + lane] = mine_ref[at : at + 1, :] + theirs_ref[at : at + 1, :]
            at += 1


def backward_kernel(
    frame, norm_factor, stride, which_ref, *refs
):
    earlier_ref = refs[0] if len(refs) == 25 else None
    (
        back_ref, state_ref, gain_ref, kernel_ref, order_ref, shrink_hbm, slope_hbm,
        expand_slope_hbm, expand_hbm, activated_hbm, part_hbm, depth_ref, input_ref, gain_grad_ref,
        back_normed, shrink_all, slope_all, expand_slope_all, expand_all, activated_all, part_ref,
        normed, arrived, sent,
    ) = refs[-24:]
    cells, channels = state_ref.shape
    row_count, lon_count, _ = input_ref.shape
    lat_size, steps, _, lane = part_ref.shape
    part = slope_all.shape[2]
    block = channels // lat_size
    copies = []
    for step in range(steps):
        place = stride * step + which_ref[0]
        here = pl.ds(pl.multiple_of(place * part, part), part)
        pairs = (
            (shrink_hbm.at[here], shrink_all.at[step]),
            (slope_hbm.at[place], slope_all.at[step]),
            (expand_slope_hbm.at[place], expand_slope_all.at[step]),
            (expand_hbm.at[:, here], expand_all.at[step]),
            (activated_hbm.at[place], activated_all.at[step]),
        )
        copies.append(
            [
                pltpu.make_async_copy(source, target, arrived.at[step, i])
                for i, (source, target) in enumerate(pairs)
            ]
        )
        for copy in copies[step]:
            copy.start()
    column = lax.broadcasted_iota(jnp.int32, (frame, part), 0)
    outside = (column < SIDE) | (column >= SIDE + lon_count)
    outside = jnp.concatenate([outside] * row_count, axis=0)
    normed[...] = normalise(state_ref[...].astype(F32), gain_ref[...]).T
    sends = []
    for step in range(steps):
        place = stride * step + which_ref[0]
        kernel = kernel_ref[place]
        copies[step][0].wait()
        copies[step][1].wait()
        back_convolved = times_transpose(back_ref[...], shrink_all[step])
        back_convolved = (back_convolved * slope_all[step].astype(F32)).astype(BF16).astype(F32)
        flipped = jnp.concatenate([kernel[8 - i : 9 - i] for i in range(9)], axis=0)
        back_activated = convolve(back_convolved, flipped, row_count, frame)
        copies[step][2].wait()
        back_expanded = back_activated * expand_slope_all[step].astype(F32)
        back_expanded = jnp.where(outside, 0.0, back_expanded).astype(BF16)
        expand_grad = (matmul(normed[...], back_expanded) * norm_factor).astype(BF16)
        for lat in range(lat_size):
            for piece in range(part // lane):
                part_ref[lat, step, piece * block : (piece + 1) * block, :] = expand_grad[
                    lat * block : (lat + 1) * block, piece * lane : (piece + 1) * lane
                ]
        sends.append(
            pltpu.make_async_copy(part_ref.at[:, step], part_hbm.at[:, step], sent.at[step])
        )
        sends[step].start()
        copies[step][3].wait()
        product = times_transpose(back_expanded, expand_all[step])
        if step > 0:
            product = product + back_normed[...]
        elif earlier_ref is not None:
            product = product + earlier_ref[...]
        back_normed[...] = product
        own_back = jnp.where(outside, 0.0, back_convolved[frame : frame + cells])
        copies[step][4].wait()
        activated = activated_all[step].astype(F32)
        for b in range(3):
            moved = own_back
            if b != 1:
                moved = pltpu.roll(own_back, cells - 1 if b == 0 else 1, 0)
            for a in range(3):
                depth_ref[step, 3 * a + b : 3 * a + b + 1, :] = norm_factor * jnp.sum(
                    activated[a * frame : a * frame + cells] * moved, axis=0, keepdims=True
                )
    state = state_ref[...].astype(F32)
    inverse = inverse_rms(state)
    grads = back_normed[...]
    gain_grad_ref[...] = norm_factor * jnp.sum(grads * state * inverse, axis=0, keepdims=True)
    result = (
        back_ref[frame : frame + cells, :].astype(F32)
        + norm_back(grads, state, inverse, gain_ref[...])
    ).astype(BF16)
    for row in range(row_count):
        start = row * frame + SIDE
        input_ref[row] = result[start : start + lon_count]
    for send in sends:
        send.wait()


def backward(
    which, back, state, gain, earlier, order, shrink_weight, slope, activated, expand_weight,
    expand_slope, kernel, norm_factor, lat_size, row_count, lon_count,
):
    cells, channels = state.shape
    frame = cells // row_count
    steps, size, part = activated.shape
    stride = 1
    if which is None:
        which = 0
    else:
        steps, stride = steps // 2, 2
    block = channels // lat_size
    lane = block
    part_shape = (lat_size, steps, part // lane * block, lane)
    here, away = pl.BlockSpec(memory_space=pltpu.VMEM), pl.BlockSpec(memory_space=pl.ANY)
    operands = (back, state, gain, kernel)
    if earlier is not None:
        operands = (earlier,) + operands
    return pl.pallas_call(
        functools.partial(backward_kernel, frame, norm_factor, stride),
        in_specs=[pl.BlockSpec(memory_space=pltpu.SMEM)] + [here] * len(operands) + [away] * 6,
        out_specs=(away,) + (here,) * 4,
        scratch_shapes=[
            pltpu.VMEM((steps, part, channels), BF16),
            pltpu.VMEM((steps, size, part), BF16),
            pltpu.VMEM((steps, cells, part), BF16),
            pltpu.VMEM((steps, channels, part), BF16),
            pltpu.VMEM((steps, size, part), BF16),
            pltpu.VMEM(part_shape, BF16),
            pltpu.VMEM((channels, cells), BF16),
            pltpu.SemaphoreType.DMA((steps, 5)),
            pltpu.SemaphoreType.DMA((steps,)),
        ],
        out_shape=(
            jax.ShapeDtypeStruct(part_shape, BF16),
            jax.ShapeDtypeStruct((steps, 9, part), F32),
            jax.ShapeDtypeStruct((row_count, lon_count, channels), BF16),
            jax.ShapeDtypeStruct((1, channels), F32),
            jax.ShapeDtypeStruct((cells, channels), F32),
        ),
        compiler_params=pltpu.CompilerParams(vmem_limit_bytes=56 * 1024 * 1024),
        cost_estimate=pl.CostEstimate(
            flops=8 * cells * channels * part * steps,
            bytes_accessed=(6 * channels + 12 * size) * part * steps,
            transcendentals=0,
        ),
        name="backward",
    )(
        jnp.reshape(which, (1,)).astype(jnp.int32), *operands, order, shrink_weight, slope,
        expand_slope, expand_weight, activated,
    )


def attention_kernel(
    head_width, query_block, qkv_ref, early_ref, order_ref, out_ref, heads_t, query_grad_t, key_t,
    value_t, back_ref, bias_ref, key_grad, value_grad, score_ref, back_prob_ref, prob_low_ref, back_score_ref,
):
    head = pl.program_id(0)
    cells = qkv_ref.shape[0]
    width = qkv_ref.shape[1] // 3
    sources = early_ref.shape[0]
    frame = cells // sources
    scale = 1.0 / math.sqrt(head_width)
    keys = qkv_ref[:, width : 2 * width]
    values = qkv_ref[:, 2 * width : 3 * width]
    part = 2 * frame

    @pl.when(head == 0)
    def _():
        key_t[...] = keys.T
        value_t[...] = values.T
        for source in range(sources):
            at = slice(source * frame, (source + 1) * frame)
            back_ref[at, :] = early_ref[source, 0:frame, 0:width]
            if early_ref.shape[1] > frame:
                bias_ref[at, :] = early_ref[source, frame:, :].astype(F32).T[0:frame]
            else:
                bias_ref[at, :] = early_ref[source, :, width:].astype(F32)
        key_grad[...] = jnp.zeros_like(key_grad)
        value_grad[...] = jnp.zeros_like(value_grad)

    lanes = lax.broadcasted_iota(jnp.int32, (1, width), 1) // head_width == head
    zero = jnp.zeros((), BF16)
    heads = lax.broadcasted_iota(jnp.int32, bias_ref.shape, 1)
    bias = LOG2E * jnp.sum(
        jnp.where(heads == head, bias_ref[...], 0.0), axis=1, keepdims=True
    )
    rows = pl.ds(pl.multiple_of(head * head_width, head_width), head_width)
    head_key_t = key_t[rows, :]
    head_value_t = value_t[rows, :]
    last_dims = (((1,), (1,)), ((), ()))

    def fold(values, combine):
        result = values[0:8]
        for start in range(8, values.shape[0], 8):
            result = combine(result, values[start : start + 8])
        return result

    def block(start):
        cols = pl.ds(start, query_block)
        queries = jnp.where(lanes, qkv_ref[cols, 0:width], zero)
        backs = jnp.where(lanes, back_ref[cols, :], zero)
        parts = [slice(i, i + part) for i in range(0, cells, part)]
        highest = jnp.full((8, query_block), -jnp.inf, F32)
        for at in parts:
            scores = lax.dot_general(
                qkv_ref[at, width : 2 * width], queries, last_dims, preferred_element_type=F32
            )
            scores = scores * (scale * LOG2E) + bias[at]
            score_ref[at, :] = scores
            highest = jnp.maximum(highest, fold(scores, jnp.maximum))
        highest = jnp.max(highest, axis=0, keepdims=True)
        total = jnp.zeros((8, query_block), F32)
        centred = jnp.zeros((8, query_block), F32)
        for at in parts:
            back_probs = lax.dot_general(
                qkv_ref[at, 2 * width : 3 * width], backs, last_dims, preferred_element_type=F32
            )
            exponent = jnp.exp2(score_ref[at, :] - highest)
            total = total + fold(exponent, jnp.add)
            centred = centred + fold(exponent * back_probs, jnp.add)
            score_ref[at, :] = exponent
            back_prob_ref[at, :] = back_probs
        inverse = 1.0 / jnp.sum(total, axis=0, keepdims=True)
        centred = jnp.sum(centred, axis=0, keepdims=True) * inverse
        for at in parts:
            probs = score_ref[at, :] * inverse
            probs_low = probs.astype(BF16)
            back_scores = (probs * (back_prob_ref[at, :] - centred)).astype(BF16)
            prob_low_ref[at, :] = probs_low
            back_score_ref[at, :] = back_scores
            value_grad[at, :] += matmul(probs_low, backs)
            key_grad[at, :] += matmul(back_scores, queries)
        heads_t[rows, cols] = matmul(head_value_t, prob_low_ref[...])
        query_grad_t[rows, cols] = matmul(head_key_t, back_score_ref[...])

    block_count = cells // query_block
    if block_count <= 4:
        for index in range(block_count):
            block(index * query_block)
    else:

        def step(index, carry):
            block(pl.multiple_of(index * query_block, query_block))
            return carry

        lax.fori_loop(0, block_count, step, 0)

    @pl.when(head == pl.num_programs(0) - 1)
    def _():
        out_ref[:, 0:width] = heads_t[...].T.astype(BF16)
        out_ref[:, width : 2 * width] = (query_grad_t[...] * scale).T.astype(BF16)
        out_ref[:, 2 * width : 3 * width] = (key_grad[...] * scale).astype(BF16)
        out_ref[:, 3 * width : 4 * width] = value_grad[...].astype(BF16)


def attention(qkv, early, order, head_width):
    cells = qkv.shape[0]
    width = qkv.shape[1] // 3
    items = width // head_width
    bias_columns = BIAS_ROWS if early.shape[2] == width else items
    query_block = cells if cells <= 1024 else 256
    whole = lambda shape: pl.BlockSpec(shape, lambda head: (0,) * len(shape))
    return pl.pallas_call(
        functools.partial(attention_kernel, head_width, query_block),
        grid=(items,),
        out_shape=jax.ShapeDtypeStruct((cells, 4 * width), BF16),
        in_specs=[whole(qkv.shape), whole(early.shape), pl.BlockSpec(memory_space=pl.ANY)],
        out_specs=whole((cells, 4 * width)),
        scratch_shapes=[
            pltpu.VMEM((width, cells), F32),
            pltpu.VMEM((width, cells), F32),
            pltpu.VMEM((width, cells), BF16),
            pltpu.VMEM((width, cells), BF16),
            pltpu.VMEM((cells, width), BF16),
            pltpu.VMEM((cells, bias_columns), F32),
            pltpu.VMEM((cells, width), F32),
            pltpu.VMEM((cells, width), F32),
            pltpu.VMEM((cells, query_block), F32),
            pltpu.VMEM((cells, query_block), F32),
            pltpu.VMEM((cells, query_block), BF16),
            pltpu.VMEM((cells, query_block), BF16),
        ],
        compiler_params=pltpu.CompilerParams(
            vmem_limit_bytes=(20 if cells <= 1024 else 48) * 1024 * 1024, dimension_semantics=("arbitrary",)
        ),
        cost_estimate=pl.CostEstimate(
            flops=items * cells * cells * 32 * 14,
            bytes_accessed=cells * width * 16,
            transcendentals=items * cells * cells,
        ),
        name="attention",
    )(qkv, early, order)


def per_device(
    state_field,
    cotangent,
    key_bias,
    input_gain,
    expand_weight,
    depth_weight,
    shrink_weight,
    attention_gain,
    attention_in,
    attention_out,
):
    row_count, lon_count, channels = state_field.shape
    head_count = key_bias.shape[2]
    head_width = channels // head_count
    wide = expand_weight.shape[1]
    lat_size, z_size = lax.axis_size("lat"), lax.axis_size("z")
    lon_size = 2 * z_size
    core = lax.axis_index("core")
    norm_factor = 1.0 / math.sqrt(row_count * lon_count * lat_size * lon_size)
    items = row_count * head_count // lon_size
    groups = head_count // items
    width = items * head_width
    frame = lon_count + 2 * SIDE
    own = row_count * frame
    kernel = depth_weight.astype(F32).reshape(9, wide)
    kernel_blocks = kernel.reshape(9, -1, step_width(wide)).transpose(1, 0, 2)
    input_gain = input_gain.reshape(1, channels)
    attention_gain = attention_gain.reshape(1, channels)

    low, high = from_sides(state_field, SIDE, 1, LON, True)
    state = jnp.concatenate([low, state_field, high], axis=1)
    if row_count == 1:
        below, above = from_sides(state, 1, 0, "lat", False)
        far_below = lax.ppermute(below, "lat", shifts(lat_size, 1, False))
        far_above = lax.ppermute(above, "lat", shifts(lat_size, -1, False))
        all_rows = [far_below, below, state, above, far_above]
    else:
        below, above = from_sides(state, 2, 0, "lat", False)
        all_rows = [below, state, above]
    all_rows = jnp.concatenate(all_rows, axis=0)

    early, cot = early_parts(cotangent, key_bias, attention_out, state, groups)
    early = exchange(early, LON)

    qkv, inner = forward(
        all_rows, input_gain, expand_weight, kernel, shrink_weight, attention_gain, attention_in,
        groups,
    )
    activated, slope, mixed, expand_slope = around(
        all_rows, input_gain, expand_weight, kernel_blocks, inner
    )
    qkv = exchange(qkv, LON).reshape(lon_size * frame, 3 * width)

    attended = attention(qkv, early, mixed, head_width)
    attended = exchange(attended.reshape(lon_size, frame, 4 * width), LON)
    cot = cot.reshape(own, channels)
    output_field, back_inner, unpacked, gain_two = call(
        functools.partial(inner_kernel, groups, norm_factor),
        "back_inner",
        (
            jax.ShapeDtypeStruct((row_count, lon_count, channels), BF16),
            jax.ShapeDtypeStruct((own, channels), BF16),
            jax.ShapeDtypeStruct((own, 4 * channels), BF16),
            jax.ShapeDtypeStruct((1, channels), F32),
        ),
        attended,
        inner,
        cot,
        attention_out,
        attention_in,
        attention_gain,
        flops=8 * own * channels * channels,
    )

    back = back_inner.reshape(row_count, frame, channels)
    centre = back[:, SIDE : SIDE + lon_count]
    low, high = from_sides(centre, 1, 1, LON, True)
    edge = jnp.zeros((row_count, SIDE - 1, channels), BF16)
    back_sides = jnp.concatenate([edge, low, centre, high, edge], axis=1)
    below, above = from_sides(back_sides, 1, 0, "lat", False)
    back = jnp.concatenate([below, back_sides, above], axis=0).reshape(-1, channels)

    lane = channels // lat_size
    in_split, out_split, split = 3 * channels // lon_size, channels // lon_size, wide // lon_size
    grads = lambda which, order, added: weight_grads(
        which, unpacked, inner, attention_gain, cot, back_inner, mixed, order, added, norm_factor,
        lat_size, z_size,
    )
    theirs = grads(1 - core, back_sides, None)
    first = after(grads(core, back_sides, core_swap(theirs)), below, above)
    first_sums = sum_parts(exchange(first, "lat"), 2)
    first_sums = lax.psum_scatter(first_sums, "z", scatter_dimension=0, tiled=True)
    flat = lambda parts: parts.reshape(lat_size, -1, lane)

    state = state.reshape(own, channels)

    def backward_part(which, earlier, order):
        return backward(
            which, back, state, input_gain, earlier, order, shrink_weight, slope, activated,
            expand_weight, expand_slope, kernel_blocks, norm_factor, lat_size, row_count, lon_count,
        )

    if split == step_width(wide):
        theirs, depth_theirs, _, _, partial = backward_part(1 - core, None, first)
        theirs = core_swap(theirs)
        depth_theirs = core_swap(depth_theirs)
        mine, depth_mine, input_grad, gain_one, _ = backward_part(core, partial, first)
    else:
        parts, depth, input_grad, gain_one, _ = backward_part(None, None, first)
        steps = parts.shape[1]
        parts = parts.reshape(lat_size, steps, -1, split // lane, lane, lane)
        parts = parts.reshape(lat_size, z_size, 2, split // lane * lane, lane)
        theirs = core_swap(lax.dynamic_index_in_dim(parts, 1 - core, 2, False))
        mine = lax.dynamic_index_in_dim(parts, core, 2, False)
        depth = depth.reshape(steps, 9, -1, split).transpose(0, 2, 1, 3)
        depth = depth.reshape(z_size, 2, 9, split)
        depth_theirs = core_swap(lax.dynamic_index_in_dim(depth, 1 - core, 1, False))
        depth_mine = lax.dynamic_index_in_dim(depth, core, 1, False)

    mine, theirs = flat(mine), flat(theirs)
    block_rows = mine.shape[1] // z_size
    small_rows = (9 * wide // 2 + 2 * channels) // lane
    output_field = output_field.transpose(1, 0, 2)
    input_grad = input_grad.transpose(1, 0, 2)
    second = call(
        pack_kernel,
        "pack",
        jax.ShapeDtypeStruct((lat_size, z_size * block_rows + small_rows, lane), BF16),
        mine,
        theirs,
        depth_mine,
        depth_theirs,
        gain_one,
        gain_two,
    )
    field = jax.ShapeDtypeStruct(output_field.shape, BF16)
    second, output_field, input_grad = call(
        merge_kernel,
        "merge",
        (jax.ShapeDtypeStruct((z_size, block_rows + small_rows, lane), BF16), field, field),
        exchange(second, "lat"),
        output_field,
        input_grad,
        specs=[pl.BlockSpec(memory_space=pltpu.VMEM)] + [pl.BlockSpec(memory_space=pl.ANY)] * 2,
        out_specs=(pl.BlockSpec(memory_space=pltpu.VMEM),)
        + (pl.BlockSpec(memory_space=pl.ANY),) * 2,
        aliases={1: 1, 2: 2},
    )
    weight = lambda rows, cols: jax.ShapeDtypeStruct((rows, cols), F32)
    expand_grad, small = call(
        second_kernel,
        "expand_grad",
        (weight(lane, split), weight(small_rows, lane)),
        exchange(second, "z"),
    )
    other = core_swap(small)
    if split % 128 == 0:
        depth_grad, input_gain_grad, attention_gain_grad = pl.pallas_call(
            functools.partial(small_kernel, split),
            out_shape=(
                jax.ShapeDtypeStruct((3, 3, wide), F32),
                weight(1, channels),
                weight(1, channels),
            ),
            in_specs=[
                pl.BlockSpec(memory_space=pltpu.SMEM),
                pl.BlockSpec(memory_space=pltpu.VMEM),
                pl.BlockSpec(memory_space=pltpu.VMEM),
            ],
            compiler_params=pltpu.CompilerParams(vmem_limit_bytes=56 * 1024 * 1024),
        name="small_grads",
        )(core.reshape(1), small, other)
    else:
        rows = 9 * wide // 2 // lane
        own_half, other_half = small[:rows], other[:rows]
        depth_grad = jnp.where(
            core == 0, jnp.stack([own_half, other_half]), jnp.stack([other_half, own_half])
        )
        depth_grad = depth_grad.reshape(2, z_size, split // lane, 9, lane).transpose(3, 1, 0, 2, 4)
        depth_grad = depth_grad.reshape(3, 3, wide)
        gains = (small[rows:] + other[rows:]).reshape(2, channels)
        input_gain_grad, attention_gain_grad = gains[0], gains[1]
    shrink_grad, attention_in_grad, attention_out_grad = call(
        first_kernel,
        "shrink_and_attention_grads",
        (
            weight(out_split, wide // lat_size),
            weight(in_split, lane),
            weight(out_split, lane),
        ),
        first_sums,
        megabytes=56,
    )
    return (
        output_field.transpose(1, 0, 2),
        input_grad.transpose(1, 0, 2),
        expand_grad,
        shrink_grad.T,
        attention_in_grad.T,
        attention_out_grad.T,
        depth_grad,
        input_gain_grad.reshape(channels),
        attention_gain_grad.reshape(channels),
    )


def solution(mesh):
    lat_size, lon_size = mesh.devices.shape
    split = Mesh(mesh.devices.reshape(lat_size, lon_size // 2, 2), ("lat", "z", "core"))
    grid = P("lat", LON, None)
    weight = P("lat", LON)

    def step(*arrays):
        outputs = jax.shard_map(
            per_device,
            mesh=split,
            in_specs=(grid, grid, grid) + (P(),) * 7,
            out_specs=(grid, grid, weight, weight, weight, weight, P(), P(), P()),
            check_vma=False,
        )(*arrays)
        return outputs

    return step
```

```python
import functools
import math

import jax
import jax.numpy as jnp
from jax import lax
from jax.experimental import pallas as pl
from jax.experimental.pallas import tpu as pltpu
from jax.sharding import Mesh
from jax.sharding import PartitionSpec as P

EPSILON = 1e-06
LON = ("z", "core")
BF16 = jnp.bfloat16
F32 = jnp.float32
MASKED = -1e30
SIDE = 3
BIAS_ROWS = 16
FORWARD_WIDTH = 1024
LOG2E = math.log2(math.e)


def inverse_rms(values):
    return lax.rsqrt(jnp.mean(values * values, axis=-1, keepdims=True) + EPSILON)


def norm_back(back_normed, state, inverse, gain):
    scaled = back_normed * gain
    return inverse * scaled - inverse * inverse * inverse * state * jnp.mean(
        scaled * state, axis=-1, keepdims=True
    )


def shifts(count, step, periodic):
    return [(i, (i + step) % count) for i in range(count) if periodic or 0 <= i + step < count]


def from_sides(block, width, dim, axis, periodic):
    count = lax.axis_size(axis)
    size = block.shape[dim]
    low = lax.ppermute(
        lax.slice_in_dim(block, size - width, size, axis=dim), axis, shifts(count, 1, periodic)
    )
    high = lax.ppermute(
        lax.slice_in_dim(block, 0, width, axis=dim), axis, shifts(count, -1, periodic)
    )
    return low, high


def core_swap(values):
    return lax.ppermute(values, "core", [(0, 1), (1, 0)])


def exchange(values, axis):
    return lax.all_to_all(values, axis, 0, 0, tiled=True)


def matmul(left, right):
    return jnp.dot(left, right, preferred_element_type=F32)


def times_transpose(values, weights):
    return lax.dot_general(
        values, weights, (((values.ndim - 1,), (1,)), ((), ())), preferred_element_type=F32
    )


def sigmoid(values):
    return 0.5 + 0.5 * jnp.tanh(0.5 * values)


def silu(values):
    return values * sigmoid(values)


def call(kernel, name, out_shape, *operands, scratch=(), megabytes=16, flops=0, specs=None, out_specs=None, aliases=None):
    return pl.pallas_call(
        kernel,
        out_shape=out_shape,
        scratch_shapes=scratch,
        in_specs=specs or [pl.BlockSpec(memory_space=pltpu.VMEM)] * len(operands),
        out_specs=out_specs
        or jax.tree.map(lambda _: pl.BlockSpec(memory_space=pltpu.VMEM), out_shape),
        input_output_aliases=aliases or {},
        compiler_params=pltpu.CompilerParams(vmem_limit_bytes=megabytes * 1024 * 1024),
        cost_estimate=pl.CostEstimate(
            flops=flops,
            bytes_accessed=sum(x.size * x.dtype.itemsize for x in operands),
            transcendentals=0,
        ),
        name=name,
    )(*operands)


def early_kernel(
    groups, cot_ref, bias_ref, out_weight_ref, order_ref, early_ref, framed_ref, bias_frame
):
    row_count, lon_count, channels = cot_ref.shape
    frame = framed_ref.shape[1]
    width = channels // groups
    head_count = bias_ref.shape[2]
    items = head_count // groups
    in_rows = early_ref.shape[2] == width
    framed_ref[...] = jnp.zeros_like(framed_ref)
    bias_frame[...] = jnp.full_like(bias_frame, MASKED)
    for row in range(row_count):
        framed_ref[row, SIDE : SIDE + lon_count, :] = cot_ref[row]
        bias_frame[row, SIDE : SIDE + lon_count, 0:head_count] = bias_ref[row].astype(F32)
    for row in range(row_count):
        back_heads = times_transpose(framed_ref[row], out_weight_ref[...]).astype(BF16)
        bias = bias_frame[row].T if in_rows else bias_frame[row]
        for group in range(groups):
            target = row * groups + group
            early_ref[target, 0:frame, 0:width] = back_heads[:, group * width : (group + 1) * width]
            if in_rows:
                early_ref[target, frame:, :] = bias[
                    group * items : group * items + BIAS_ROWS
                ].astype(BF16)
            else:
                early_ref[target, :, width:] = bias[
                    0:frame, group * items : (group + 1) * items
                ].astype(BF16)


def early_parts(cotangent, key_bias, attention_out, order, groups):
    row_count, lon_count, channels = cotangent.shape
    frame = lon_count + 2 * SIDE
    head_count = key_bias.shape[2]
    width = channels // groups
    if frame <= width and width % 128 == 0:
        shape = (row_count * groups, frame + BIAS_ROWS, width)
        bias_shape = (row_count, width, max(128, head_count + BIAS_ROWS))
    else:
        shape = (row_count * groups, frame, width + head_count // groups)
        bias_shape = (row_count, frame, head_count)
    return call(
        functools.partial(early_kernel, groups),
        "back_heads",
        (
            jax.ShapeDtypeStruct(shape, BF16),
            jax.ShapeDtypeStruct((row_count, frame, channels), BF16),
        ),
        cotangent,
        key_bias,
        attention_out,
        order,
        scratch=[pltpu.VMEM(bias_shape, F32)],
        flops=2 * row_count * frame * channels * channels,
    )


def normalise(values, gain):
    return (values * inverse_rms(values) * gain).astype(BF16)


def convolve(values, kernel, rows, frame):
    size = rows * frame
    total = None
    for b in range(3):
        part = kernel[b : b + 1] * values[0:size]
        for a in range(1, 3):
            part = part + kernel[3 * a + b : 3 * a + b + 1] * values[a * frame : a * frame + size]
        if b != 1:
            part = pltpu.roll(part, 1 if b == 0 else size - 1, 0)
        total = part if total is None else total + part
    return total


def forward_kernel(
    frame, groups, steps, state_ref, gain_ref, kernel_ref, second_gain_ref, expand_hbm, shrink_hbm,
    in_hbm, qkv_ref, inner_ref, expand_ref, shrink_ref, in_ref, normed, total, arrived,
):
    cells, channels = inner_ref.shape
    wide = expand_ref.shape[1]
    rows = cells // frame
    width = channels // groups
    part = wide // steps
    parts = [slice(i * part, (i + 1) * part) for i in range(steps)]
    expand_copies, shrink_copies = [], []
    for i, cols in enumerate(parts):
        expand_copies.append(
            pltpu.make_async_copy(expand_hbm.at[:, cols], expand_ref.at[:, cols], arrived.at[i])
        )
        shrink_copies.append(
            pltpu.make_async_copy(shrink_hbm.at[cols], shrink_ref.at[cols], arrived.at[steps + i])
        )
        expand_copies[i].start()
        shrink_copies[i].start()
    in_copy = pltpu.make_async_copy(in_hbm, in_ref, arrived.at[2 * steps])
    in_copy.start()
    near = state_ref[frame : frame + normed.shape[0], :].astype(F32)
    normed[...] = normalise(near, gain_ref[...])
    for i, cols in enumerate(parts):
        expand_copies[i].wait()
        activated = silu(matmul(normed[...], expand_ref[:, cols])).astype(BF16).astype(F32)
        kernel = jnp.concatenate([kernel_ref[a, :, cols] for a in range(3)], axis=0).astype(F32)
        mixed = silu(convolve(activated, kernel, rows, frame)).astype(BF16)
        shrink_copies[i].wait()
        product = matmul(mixed, shrink_ref[cols])
        total[...] = product if i == 0 else total[...] + product
    inner = state_ref[2 * frame : 2 * frame + cells, :].astype(F32)
    inner = (inner + total[...]).astype(BF16)
    inner_ref[...] = inner
    normed_second = normalise(inner.astype(F32), second_gain_ref[...])
    in_copy.wait()
    projected = matmul(normed_second, in_ref[...]).astype(BF16)
    for row in range(rows):
        for group in range(groups):
            for kind in range(3):
                start = kind * channels + group * width
                qkv_ref[row * groups + group, :, kind * width : (kind + 1) * width] = projected[
                    row * frame : (row + 1) * frame, start : start + width
                ]


def step_width(wide):
    return 256 if wide % 256 == 0 else wide


def forward(state, input_gain, expand_weight, kernel, shrink_weight, gain, attention_in, groups):
    all_rows, frame, channels = state.shape
    rows = all_rows - 4
    cells = rows * frame
    wide = expand_weight.shape[1]
    steps = wide // FORWARD_WIDTH
    here, away = pl.BlockSpec(memory_space=pltpu.VMEM), pl.BlockSpec(memory_space=pl.ANY)
    return pl.pallas_call(
        functools.partial(forward_kernel, frame, groups, steps),
        out_shape=(
            jax.ShapeDtypeStruct((rows * groups, frame, 3 * channels // groups), BF16),
            jax.ShapeDtypeStruct((cells, channels), BF16),
        ),
        in_specs=[here] * 4 + [away] * 3,
        scratch_shapes=[
            pltpu.VMEM(expand_weight.shape, BF16),
            pltpu.VMEM(shrink_weight.shape, BF16),
            pltpu.VMEM(attention_in.shape, BF16),
            pltpu.VMEM((cells + 2 * frame, channels), BF16),
            pltpu.VMEM((cells, channels), F32),
            pltpu.SemaphoreType.DMA((2 * steps + 1,)),
        ],
        compiler_params=pltpu.CompilerParams(vmem_limit_bytes=56 * 1024 * 1024),
        cost_estimate=pl.CostEstimate(
            flops=2 * cells * channels * (3 * wide + 3 * channels),
            bytes_accessed=4 * channels * wide + 6 * channels * channels,
            transcendentals=3 * cells * wide,
        ),
        name="forward",
    )(
        state.reshape(all_rows * frame, channels),
        input_gain,
        kernel,
        gain,
        expand_weight,
        shrink_weight,
        attention_in,
    )


def around_kernel(
    frame, state_ref, gain_ref, expand_ref, kernel_ref, order_ref, activated_ref, slope_ref, mixed_ref,
    expand_slope_ref, normed,
):
    size = activated_ref.shape[1]
    cells = mixed_ref.shape[1]

    @pl.when(pl.program_id(0) == 0)
    def _():
        normed[...] = normalise(state_ref[...].astype(F32), gain_ref[...])

    expanded = matmul(normed[...], expand_ref[...])
    gate = sigmoid(expanded)
    activated = (expanded * gate).astype(BF16)
    activated_ref[0] = activated[frame : frame + size]
    own_gate, own = gate[2 * frame : 2 * frame + cells], expanded[2 * frame : 2 * frame + cells]
    expand_slope_ref[0] = (own_gate * (1.0 + own * (1.0 - own_gate))).astype(BF16)
    convolved = convolve(activated.astype(F32), kernel_ref[0], size // frame, frame)
    gate = sigmoid(convolved)
    slope_ref[0] = (gate * (1.0 + convolved * (1.0 - gate))).astype(BF16)
    mixed_ref[0] = (
        convolved[frame : frame + cells] * gate[frame : frame + cells]
    ).astype(BF16)


def around(state, input_gain, expand_weight, kernel, order):
    all_rows, frame, channels = state.shape
    size, cells = (all_rows - 2) * frame, (all_rows - 4) * frame
    wide = expand_weight.shape[1]
    part = step_width(wide)
    fixed = lambda shape: pl.BlockSpec(shape, lambda step: (0,) * len(shape))
    moving = lambda rows: pl.BlockSpec((rows, part), lambda step: (0, step))
    block = lambda rows: pl.BlockSpec((1, rows, part), lambda step: (step, 0, 0))
    steps = wide // part
    return pl.pallas_call(
        functools.partial(around_kernel, frame),
        grid=(steps,),
        out_shape=(
            jax.ShapeDtypeStruct((steps, size, part), BF16),
            jax.ShapeDtypeStruct((steps, size, part), BF16),
            jax.ShapeDtypeStruct((steps, cells, part), BF16),
            jax.ShapeDtypeStruct((steps, cells, part), BF16),
        ),
        in_specs=[
            fixed((all_rows * frame, channels)),
            fixed((1, channels)),
            moving(channels),
            block(9),
            pl.BlockSpec(memory_space=pl.ANY),
        ],
        out_specs=(block(size), block(size), block(cells), block(cells)),
        scratch_shapes=[pltpu.VMEM((all_rows * frame, channels), BF16)],
        compiler_params=pltpu.CompilerParams(
            vmem_limit_bytes=16 * 1024 * 1024, dimension_semantics=("arbitrary",)
        ),
        cost_estimate=pl.CostEstimate(
            flops=2 * all_rows * frame * channels * wide,
            bytes_accessed=2 * channels * wide + 14 * size * wide,
            transcendentals=2 * size * wide,
        ),
        name="forward_around",
    )(state.reshape(all_rows * frame, channels), input_gain, expand_weight, kernel, order)


def inner_kernel(
    groups, norm_factor, attended_ref, inner_ref, cot_ref, out_weight_ref, in_weight_ref, gain_ref,
    output_ref, back_inner_ref, unpacked_ref, gain_grad_ref,
):
    targets, frame, width = attended_ref.shape
    width = width // 4
    row_count, lon_count, channels = output_ref.shape
    for target in range(targets):
        row, group = divmod(target, groups)
        for kind in range(4):
            start = kind * channels + group * width
            unpacked_ref[row * frame : (row + 1) * frame, start : start + width] = attended_ref[
                target, :, kind * width : (kind + 1) * width
            ]
    inner = inner_ref[...].astype(F32)
    output = (inner + matmul(unpacked_ref[:, :channels], out_weight_ref[...])).astype(BF16)
    for row in range(row_count):
        start = row * frame + SIDE
        output_ref[row] = output[start : start + lon_count]
    back_second = times_transpose(unpacked_ref[:, channels:], in_weight_ref[...])
    inverse = inverse_rms(inner)
    gain_grad_ref[...] = norm_factor * jnp.sum(back_second * inner * inverse, axis=0, keepdims=True)
    back_inner_ref[...] = (
        cot_ref[...].astype(F32) + norm_back(back_second, inner, inverse, gain_ref[...])
    ).astype(BF16)


def weight_grads_kernel(
    norm_factor, z_size, which_ref, unpacked_ref, inner_ref, gain_ref, cot_ref, back_inner_ref,
    mixed_ref, order_ref, *refs
):
    added_ref = refs[0] if len(refs) == 8 else None
    out_ref, whole_in, whole_out, whole_back, in_t, out_t, back_t = refs[-7:]
    lat_size, _, lane = out_ref.shape
    channels = inner_ref.shape[1]
    blocks, _, part = mixed_ref.shape
    blocks = blocks // lat_size
    in_split, out_split = in_t.shape[0] // z_size, out_t.shape[0] // z_size
    first_rows = out_ref.shape[1] // z_size
    normed_second = normalise(inner_ref[...].astype(F32), gain_ref[...])
    whole_in[...] = unpacked_ref[:, channels:].T
    whole_out[...] = cot_ref[...].T
    whole_back[...] = back_inner_ref[...].T
    for z in range(z_size):
        lon = 2 * z + which_ref[0]
        for source, target, split in (
            (whole_in, in_t, in_split),
            (whole_out, out_t, out_split),
            (whole_back, back_t, out_split),
        ):
            target[z * split : (z + 1) * split, :] = source[
                pl.ds(pl.multiple_of(lon * split, split), split), :
            ]

    def put(lat, start, split, values):
        values = values * norm_factor
        for z in range(z_size):
            rows = slice(z * first_rows + start, z * first_rows + start + split)
            value = values[z * split : (z + 1) * split]
            if added_ref is not None:
                value = value + added_ref[lat, rows, :].astype(F32)
            out_ref[lat, rows, :] = value.astype(BF16)

    for lat in range(lat_size):
        cols = slice(lat * lane, (lat + 1) * lane)
        put(lat, 0, in_split, matmul(in_t[...], normed_second[:, cols]))
        put(lat, in_split, out_split, matmul(out_t[...], unpacked_ref[:, cols]))
        start = in_split + out_split
        for block in range(blocks):
            values = matmul(back_t[...], mixed_ref[lat * blocks + block])
            for piece in range(part // lane):
                put(lat, start, out_split, values[:, piece * lane : (piece + 1) * lane])
                start += out_split


def weight_grads(
    which, unpacked, inner, gain, cot, back_inner, mixed, order, added, norm_factor, lat_size, z_size
):
    own, channels = inner.shape
    lane = channels // lat_size
    wide = mixed.shape[0] * mixed.shape[2]
    rows = 2 * channels + channels // 2 * (wide // channels)
    operands = (unpacked, inner, gain, cot, back_inner, mixed, order)
    if added is not None:
        operands += (added,)
    in_specs = [pl.BlockSpec(memory_space=pltpu.VMEM)] * len(operands)
    in_specs[6] = pl.BlockSpec(memory_space=pl.ANY)
    tall, short = pltpu.VMEM((3 * channels, own), BF16), pltpu.VMEM((channels, own), BF16)
    return pl.pallas_call(
        functools.partial(weight_grads_kernel, norm_factor, z_size),
        out_shape=jax.ShapeDtypeStruct((lat_size, rows, lane), BF16),
        in_specs=[pl.BlockSpec(memory_space=pltpu.SMEM)] + in_specs,
        scratch_shapes=[
            tall,
            short,
            short,
            pltpu.VMEM((3 * channels // 2, own), BF16),
            pltpu.VMEM((channels // 2, own), BF16),
            pltpu.VMEM((channels // 2, own), BF16),
        ],
        compiler_params=pltpu.CompilerParams(vmem_limit_bytes=20 * 1024 * 1024),
        cost_estimate=pl.CostEstimate(
            flops=own * channels * (4 * channels + wide),
            bytes_accessed=2 * channels * (8 * channels + 2 * wide),
            transcendentals=0,
        ),
        name="weight_grads",
    )(which.reshape(1), *operands)


def after_kernel(*refs):
    pass


def after(values, *others):
    away = pl.BlockSpec(memory_space=pl.ANY)
    return pl.pallas_call(
        after_kernel,
        out_shape=jax.ShapeDtypeStruct(values.shape, values.dtype),
        in_specs=[away] * (1 + len(others)),
        out_specs=away,
        input_output_aliases={0: 0},
        name="after",
    )(values, *others)


def sum_kernel(parts_ref, out_ref):
    out_ref[...] = summed(parts_ref, slice(None)).astype(BF16)


def sum_parts(parts):
    return call(sum_kernel, "sum_bands", jax.ShapeDtypeStruct(parts.shape[1:], BF16), parts, megabytes=8)


def pack_kernel(
    left_ref, right_ref, mine_ref, theirs_ref, first_gain_ref, second_gain_ref, out_ref
):
    depth = mine_ref[...] + theirs_ref[...]
    rows, lane = left_ref.shape[1:]
    out_ref[:, 0:rows, :] = (left_ref[...].astype(F32) + right_ref[...].astype(F32)).astype(BF16)
    small = []
    for z in range(depth.shape[0]):
        for start in range(0, depth.shape[2], lane):
            small.append(depth[z, :, start : start + lane])
    for ref in (first_gain_ref, second_gain_ref):
        for start in range(0, ref.shape[1], lane):
            small.append(ref[:, start : start + lane])
    small = jnp.concatenate(small, axis=0).astype(BF16)
    for lat in range(out_ref.shape[0]):
        out_ref[lat, rows:, :] = small


def summed(ref, rows):
    total = ref[0, rows, :].astype(F32)
    for part in range(1, ref.shape[0]):
        total = total + ref[part, rows, :].astype(F32)
    return total


def merge_kernel(parts_ref, output_ref, input_ref, out_ref, output_out, input_out):
    z_size, out_rows, _ = out_ref.shape
    rows = parts_ref.shape[1]
    block = (rows - out_rows) // (z_size - 1)
    small = summed(parts_ref, slice(z_size * block, rows)).astype(BF16)
    for z in range(z_size):
        out_ref[z, 0:block, :] = summed(parts_ref, slice(z * block, (z + 1) * block)).astype(BF16)
        out_ref[z, block:, :] = small


def small_sum_kernel(parts_ref, small_ref):
    rows = parts_ref.shape[1] - small_ref.shape[0]
    small_ref[...] = summed(parts_ref, slice(rows, parts_ref.shape[1]))


def finish_kernel(parts_ref, first_ref, expand_ref, shrink_ref, in_ref, out_ref):
    block, split = expand_ref.shape
    lane = parts_ref.shape[2]
    for piece in range(split // lane):
        expand_ref[:, piece * lane : (piece + 1) * lane] = summed(
            parts_ref, slice(piece * block, (piece + 1) * block)
        )
    in_split, out_split = in_ref.shape[0], out_ref.shape[0]
    at = in_split + out_split
    in_ref[...] = first_ref[0:in_split, :].astype(F32)
    out_ref[...] = first_ref[in_split:at, :].astype(F32)
    for piece in range(shrink_ref.shape[1] // lane):
        shrink_ref[:, piece * lane : (piece + 1) * lane] = first_ref[at : at + out_split, :].astype(
            F32
        )
        at += out_split


def small_kernel(
    split, core_ref, mine_ref, theirs_ref, order_ref, depth_ref, first_gain_ref, second_gain_ref
):
    lane = mine_ref.shape[1]
    wide = depth_ref.shape[2]
    channels = first_gain_ref.shape[1]
    half_rows = 9 * wide // 2 // lane
    core = core_ref[0]
    pieces = wide // lane
    in_block = split // lane
    for side in range(2):
        which = core if side == 0 else 1 - core
        for piece in range(pieces // 2):
            source = mine_ref if side == 0 else theirs_ref
            block = source[piece * 9 : piece * 9 + 9, :]
            z, rest = divmod(piece, in_block)
            start = pl.multiple_of((2 * z + which) * split, lane) + rest * lane
            for a in range(3):
                depth_ref[a, :, pl.ds(pl.multiple_of(start, lane), lane)] = block[3 * a : 3 * a + 3]
    at = half_rows
    for ref in (first_gain_ref, second_gain_ref):
        for start in range(0, channels, lane):
            ref[:, start : start + lane] = mine_ref[at : at + 1, :] + theirs_ref[at : at + 1, :]
            at += 1


def backward_kernel(
    frame, norm_factor, stride, which_ref, *refs
):
    earlier_ref = refs[0] if len(refs) == 25 else None
    (
        back_ref, state_ref, gain_ref, kernel_ref, order_ref, shrink_hbm, slope_hbm,
        expand_slope_hbm, expand_hbm, activated_hbm, part_hbm, depth_ref, input_ref, gain_grad_ref,
        back_normed, shrink_all, slope_all, expand_slope_all, expand_all, activated_all, part_ref,
        normed, arrived, sent,
    ) = refs[-24:]
    cells, channels = state_ref.shape
    row_count, lon_count, _ = input_ref.shape
    lat_size, steps, _, lane = part_ref.shape
    part = slope_all.shape[2]
    block = channels // lat_size
    copies = []
    for step in range(steps):
        place = stride * step + which_ref[0]
        here = pl.ds(pl.multiple_of(place * part, part), part)
        pairs = (
            (shrink_hbm.at[here], shrink_all.at[step]),
            (slope_hbm.at[place], slope_all.at[step]),
            (expand_slope_hbm.at[place], expand_slope_all.at[step]),
            (expand_hbm.at[:, here], expand_all.at[step]),
            (activated_hbm.at[place], activated_all.at[step]),
        )
        copies.append(
            [
                pltpu.make_async_copy(source, target, arrived.at[step, i])
                for i, (source, target) in enumerate(pairs)
            ]
        )
        for copy in copies[step]:
            copy.start()
    column = lax.broadcasted_iota(jnp.int32, (frame, part), 0)
    outside = (column < SIDE) | (column >= SIDE + lon_count)
    outside = jnp.concatenate([outside] * row_count, axis=0)
    normed[...] = normalise(state_ref[...].astype(F32), gain_ref[...]).T
    sends = []
    for step in range(steps):
        place = stride * step + which_ref[0]
        kernel = kernel_ref[place]
        copies[step][0].wait()
        copies[step][1].wait()
        back_convolved = times_transpose(back_ref[...], shrink_all[step])
        back_convolved = (back_convolved * slope_all[step].astype(F32)).astype(BF16).astype(F32)
        flipped = jnp.concatenate([kernel[8 - i : 9 - i] for i in range(9)], axis=0)
        back_activated = convolve(back_convolved, flipped, row_count, frame)
        copies[step][2].wait()
        back_expanded = back_activated * expand_slope_all[step].astype(F32)
        back_expanded = jnp.where(outside, 0.0, back_expanded).astype(BF16)
        expand_grad = (matmul(normed[...], back_expanded) * norm_factor).astype(BF16)
        for lat in range(lat_size):
            for piece in range(part // lane):
                part_ref[lat, step, piece * block : (piece + 1) * block, :] = expand_grad[
                    lat * block : (lat + 1) * block, piece * lane : (piece + 1) * lane
                ]
        sends.append(
            pltpu.make_async_copy(part_ref.at[:, step], part_hbm.at[:, step], sent.at[step])
        )
        sends[step].start()
        copies[step][3].wait()
        product = times_transpose(back_expanded, expand_all[step])
        if step > 0:
            product = product + back_normed[...]
        elif earlier_ref is not None:
            product = product + earlier_ref[...]
        back_normed[...] = product
        own_back = jnp.where(outside, 0.0, back_convolved[frame : frame + cells])
        copies[step][4].wait()
        activated = activated_all[step].astype(F32)
        for b in range(3):
            moved = own_back
            if b != 1:
                moved = pltpu.roll(own_back, cells - 1 if b == 0 else 1, 0)
            for a in range(3):
                depth_ref[step, 3 * a + b : 3 * a + b + 1, :] = norm_factor * jnp.sum(
                    activated[a * frame : a * frame + cells] * moved, axis=0, keepdims=True
                )
    state = state_ref[...].astype(F32)
    inverse = inverse_rms(state)
    grads = back_normed[...]
    gain_grad_ref[...] = norm_factor * jnp.sum(grads * state * inverse, axis=0, keepdims=True)
    result = (
        back_ref[frame : frame + cells, :].astype(F32)
        + norm_back(grads, state, inverse, gain_ref[...])
    ).astype(BF16)
    for row in range(row_count):
        start = row * frame + SIDE
        input_ref[row] = result[start : start + lon_count]
    for send in sends:
        send.wait()


def backward(
    which, back, state, gain, earlier, order, shrink_weight, slope, activated, expand_weight,
    expand_slope, kernel, norm_factor, lat_size, row_count, lon_count,
):
    cells, channels = state.shape
    frame = cells // row_count
    steps, size, part = activated.shape
    stride = 1
    if which is None:
        which = 0
    else:
        steps, stride = steps // 2, 2
    block = channels // lat_size
    lane = block
    part_shape = (lat_size, steps, part // lane * block, lane)
    here, away = pl.BlockSpec(memory_space=pltpu.VMEM), pl.BlockSpec(memory_space=pl.ANY)
    operands = (back, state, gain, kernel)
    if earlier is not None:
        operands = (earlier,) + operands
    return pl.pallas_call(
        functools.partial(backward_kernel, frame, norm_factor, stride),
        in_specs=[pl.BlockSpec(memory_space=pltpu.SMEM)] + [here] * len(operands) + [away] * 6,
        out_specs=(away,) + (here,) * 4,
        scratch_shapes=[
            pltpu.VMEM((steps, part, channels), BF16),
            pltpu.VMEM((steps, size, part), BF16),
            pltpu.VMEM((steps, cells, part), BF16),
            pltpu.VMEM((steps, channels, part), BF16),
            pltpu.VMEM((steps, size, part), BF16),
            pltpu.VMEM(part_shape, BF16),
            pltpu.VMEM((channels, cells), BF16),
            pltpu.SemaphoreType.DMA((steps, 5)),
            pltpu.SemaphoreType.DMA((steps,)),
        ],
        out_shape=(
            jax.ShapeDtypeStruct(part_shape, BF16),
            jax.ShapeDtypeStruct((steps, 9, part), F32),
            jax.ShapeDtypeStruct((row_count, lon_count, channels), BF16),
            jax.ShapeDtypeStruct((1, channels), F32),
            jax.ShapeDtypeStruct((cells, channels), F32),
        ),
        compiler_params=pltpu.CompilerParams(vmem_limit_bytes=56 * 1024 * 1024),
        cost_estimate=pl.CostEstimate(
            flops=8 * cells * channels * part * steps,
            bytes_accessed=(6 * channels + 12 * size) * part * steps,
            transcendentals=0,
        ),
        name="backward",
    )(
        jnp.reshape(which, (1,)).astype(jnp.int32), *operands, order, shrink_weight, slope,
        expand_slope, expand_weight, activated,
    )


def attention_kernel(
    head_width, query_block, qkv_ref, early_ref, order_ref, out_ref, heads_t, query_grad_t, key_t,
    value_t, back_ref, bias_ref, key_grad, value_grad, score_ref, back_prob_ref, prob_low_ref, back_score_ref,
):
    head = pl.program_id(0)
    cells = qkv_ref.shape[0]
    width = qkv_ref.shape[1] // 3
    sources = early_ref.shape[0]
    frame = cells // sources
    scale = 1.0 / math.sqrt(head_width)
    keys = qkv_ref[:, width : 2 * width]
    values = qkv_ref[:, 2 * width : 3 * width]
    part = 2 * frame

    @pl.when(head == 0)
    def _():
        key_t[...] = keys.T
        value_t[...] = values.T
        for source in range(sources):
            at = slice(source * frame, (source + 1) * frame)
            back_ref[at, :] = early_ref[source, 0:frame, 0:width]
            if early_ref.shape[1] > frame:
                bias_ref[at, :] = early_ref[source, frame:, :].astype(F32).T[0:frame]
            else:
                bias_ref[at, :] = early_ref[source, :, width:].astype(F32)
        key_grad[...] = jnp.zeros_like(key_grad)
        value_grad[...] = jnp.zeros_like(value_grad)

    lanes = lax.broadcasted_iota(jnp.int32, (1, width), 1) // head_width == head
    zero = jnp.zeros((), BF16)
    heads = lax.broadcasted_iota(jnp.int32, bias_ref.shape, 1)
    bias = LOG2E * jnp.sum(
        jnp.where(heads == head, bias_ref[...], 0.0), axis=1, keepdims=True
    )
    rows = pl.ds(pl.multiple_of(head * head_width, head_width), head_width)
    head_key_t = key_t[rows, :]
    head_value_t = value_t[rows, :]
    last_dims = (((1,), (1,)), ((), ()))

    def fold(values, combine):
        result = values[0:8]
        for start in range(8, values.shape[0], 8):
            result = combine(result, values[start : start + 8])
        return result

    def block(start):
        cols = pl.ds(start, query_block)
        queries = jnp.where(lanes, qkv_ref[cols, 0:width], zero)
        backs = jnp.where(lanes, back_ref[cols, :], zero)
        parts = [slice(i, i + part) for i in range(0, cells, part)]
        highest = jnp.full((8, query_block), -jnp.inf, F32)
        for at in parts:
            scores = lax.dot_general(
                qkv_ref[at, width : 2 * width], queries, last_dims, preferred_element_type=F32
            )
            scores = scores * (scale * LOG2E) + bias[at]
            score_ref[at, :] = scores
            highest = jnp.maximum(highest, fold(scores, jnp.maximum))
        highest = jnp.max(highest, axis=0, keepdims=True)
        total = jnp.zeros((8, query_block), F32)
        centred = jnp.zeros((8, query_block), F32)
        for at in parts:
            back_probs = lax.dot_general(
                qkv_ref[at, 2 * width : 3 * width], backs, last_dims, preferred_element_type=F32
            )
            exponent = jnp.exp2(score_ref[at, :] - highest)
            total = total + fold(exponent, jnp.add)
            centred = centred + fold(exponent * back_probs, jnp.add)
            score_ref[at, :] = exponent
            back_prob_ref[at, :] = back_probs
        inverse = 1.0 / jnp.sum(total, axis=0, keepdims=True)
        centred = jnp.sum(centred, axis=0, keepdims=True) * inverse
        for at in parts:
            probs = score_ref[at, :] * inverse
            probs_low = probs.astype(BF16)
            back_scores = (probs * (back_prob_ref[at, :] - centred)).astype(BF16)
            prob_low_ref[at, :] = probs_low
            back_score_ref[at, :] = back_scores
            value_grad[at, :] += matmul(probs_low, backs)
            key_grad[at, :] += matmul(back_scores, queries)
        heads_t[rows, cols] = matmul(head_value_t, prob_low_ref[...])
        query_grad_t[rows, cols] = matmul(head_key_t, back_score_ref[...])

    block_count = cells // query_block
    if block_count <= 4:
        for index in range(block_count):
            block(index * query_block)
    else:

        def step(index, carry):
            block(pl.multiple_of(index * query_block, query_block))
            return carry

        lax.fori_loop(0, block_count, step, 0)

    @pl.when(head == pl.num_programs(0) - 1)
    def _():
        out_ref[:, 0:width] = heads_t[...].T.astype(BF16)
        out_ref[:, width : 2 * width] = (query_grad_t[...] * scale).T.astype(BF16)
        out_ref[:, 2 * width : 3 * width] = (key_grad[...] * scale).astype(BF16)
        out_ref[:, 3 * width : 4 * width] = value_grad[...].astype(BF16)


def attention(qkv, early, order, head_width):
    cells = qkv.shape[0]
    width = qkv.shape[1] // 3
    items = width // head_width
    bias_columns = BIAS_ROWS if early.shape[2] == width else items
    query_block = cells if cells <= 1024 else 256
    whole = lambda shape: pl.BlockSpec(shape, lambda head: (0,) * len(shape))
    return pl.pallas_call(
        functools.partial(attention_kernel, head_width, query_block),
        grid=(items,),
        out_shape=jax.ShapeDtypeStruct((cells, 4 * width), BF16),
        in_specs=[whole(qkv.shape), whole(early.shape), pl.BlockSpec(memory_space=pl.ANY)],
        out_specs=whole((cells, 4 * width)),
        scratch_shapes=[
            pltpu.VMEM((width, cells), F32),
            pltpu.VMEM((width, cells), F32),
            pltpu.VMEM((width, cells), BF16),
            pltpu.VMEM((width, cells), BF16),
            pltpu.VMEM((cells, width), BF16),
            pltpu.VMEM((cells, bias_columns), F32),
            pltpu.VMEM((cells, width), F32),
            pltpu.VMEM((cells, width), F32),
            pltpu.VMEM((cells, query_block), F32),
            pltpu.VMEM((cells, query_block), F32),
            pltpu.VMEM((cells, query_block), BF16),
            pltpu.VMEM((cells, query_block), BF16),
        ],
        compiler_params=pltpu.CompilerParams(
            vmem_limit_bytes=(20 if cells <= 1024 else 48) * 1024 * 1024, dimension_semantics=("arbitrary",)
        ),
        cost_estimate=pl.CostEstimate(
            flops=items * cells * cells * 32 * 14,
            bytes_accessed=cells * width * 16,
            transcendentals=items * cells * cells,
        ),
        name="attention",
    )(qkv, early, order)


def per_device(
    state_field,
    cotangent,
    key_bias,
    input_gain,
    expand_weight,
    depth_weight,
    shrink_weight,
    attention_gain,
    attention_in,
    attention_out,
):
    row_count, lon_count, channels = state_field.shape
    head_count = key_bias.shape[2]
    head_width = channels // head_count
    wide = expand_weight.shape[1]
    lat_size, z_size = lax.axis_size("lat"), lax.axis_size("z")
    lon_size = 2 * z_size
    core = lax.axis_index("core")
    norm_factor = 1.0 / math.sqrt(row_count * lon_count * lat_size * lon_size)
    items = row_count * head_count // lon_size
    groups = head_count // items
    width = items * head_width
    frame = lon_count + 2 * SIDE
    own = row_count * frame
    kernel = depth_weight.astype(F32).reshape(9, wide)
    kernel_blocks = kernel.reshape(9, -1, step_width(wide)).transpose(1, 0, 2)
    input_gain = input_gain.reshape(1, channels)
    attention_gain = attention_gain.reshape(1, channels)

    low, high = from_sides(state_field, SIDE, 1, LON, True)
    state = jnp.concatenate([low, state_field, high], axis=1)
    if row_count == 1:
        below, above = from_sides(state, 1, 0, "lat", False)
        far_below = lax.ppermute(below, "lat", shifts(lat_size, 1, False))
        far_above = lax.ppermute(above, "lat", shifts(lat_size, -1, False))
        all_rows = [far_below, below, state, above, far_above]
    else:
        below, above = from_sides(state, 2, 0, "lat", False)
        all_rows = [below, state, above]
    all_rows = jnp.concatenate(all_rows, axis=0)

    early, cot = early_parts(cotangent, key_bias, attention_out, state, groups)
    early = exchange(early, LON)

    qkv, inner = forward(
        all_rows, input_gain, expand_weight, depth_weight, shrink_weight, attention_gain,
        attention_in,
        groups,
    )
    activated, slope, mixed, expand_slope = around(
        all_rows, input_gain, expand_weight, kernel_blocks, inner
    )
    qkv = exchange(qkv, LON).reshape(lon_size * frame, 3 * width)

    attended = attention(qkv, early, mixed, head_width)
    attended = exchange(attended.reshape(lon_size, frame, 4 * width), LON)
    cot = cot.reshape(own, channels)
    output_field, back_inner, unpacked, gain_two = call(
        functools.partial(inner_kernel, groups, norm_factor),
        "back_inner",
        (
            jax.ShapeDtypeStruct((row_count, lon_count, channels), BF16),
            jax.ShapeDtypeStruct((own, channels), BF16),
            jax.ShapeDtypeStruct((own, 4 * channels), BF16),
            jax.ShapeDtypeStruct((1, channels), F32),
        ),
        attended,
        inner,
        cot,
        attention_out,
        attention_in,
        attention_gain,
        flops=8 * own * channels * channels,
    )

    back = back_inner.reshape(row_count, frame, channels)
    centre = back[:, SIDE : SIDE + lon_count]
    low, high = from_sides(centre, 1, 1, LON, True)
    edge = jnp.zeros((row_count, SIDE - 1, channels), BF16)
    back_sides = jnp.concatenate([edge, low, centre, high, edge], axis=1)
    below, above = from_sides(back_sides, 1, 0, "lat", False)
    back = jnp.concatenate([below, back_sides, above], axis=0).reshape(-1, channels)

    lane = channels // lat_size
    in_split, out_split, split = 3 * channels // lon_size, channels // lon_size, wide // lon_size
    grads = lambda which, order, added: weight_grads(
        which, unpacked, inner, attention_gain, cot, back_inner, mixed, order, added, norm_factor,
        lat_size, z_size,
    )
    theirs = grads(1 - core, back_sides, None)
    first = after(grads(core, back_sides, core_swap(theirs)), below, above)
    first_sums = sum_parts(exchange(first, "lat"))
    first_sums = lax.psum_scatter(first_sums, "z", scatter_dimension=0, tiled=True)
    flat = lambda parts: parts.reshape(lat_size, -1, lane)

    state = state.reshape(own, channels)

    def backward_part(which, earlier, order):
        return backward(
            which, back, state, input_gain, earlier, order, shrink_weight, slope, activated,
            expand_weight, expand_slope, kernel_blocks, norm_factor, lat_size, row_count, lon_count,
        )

    if split == step_width(wide):
        theirs, depth_theirs, _, _, partial = backward_part(1 - core, None, first)
        theirs = core_swap(theirs)
        depth_theirs = core_swap(depth_theirs)
        mine, depth_mine, input_grad, gain_one, _ = backward_part(core, partial, first)
    else:
        parts, depth, input_grad, gain_one, _ = backward_part(None, None, first)
        steps = parts.shape[1]
        parts = parts.reshape(lat_size, steps, -1, split // lane, lane, lane)
        parts = parts.reshape(lat_size, z_size, 2, split // lane * lane, lane)
        theirs = core_swap(lax.dynamic_index_in_dim(parts, 1 - core, 2, False))
        mine = lax.dynamic_index_in_dim(parts, core, 2, False)
        depth = depth.reshape(steps, 9, -1, split).transpose(0, 2, 1, 3)
        depth = depth.reshape(z_size, 2, 9, split)
        depth_theirs = core_swap(lax.dynamic_index_in_dim(depth, 1 - core, 1, False))
        depth_mine = lax.dynamic_index_in_dim(depth, core, 1, False)

    mine, theirs = flat(mine), flat(theirs)
    block_rows = mine.shape[1] // z_size
    small_rows = (9 * wide // 2 + 2 * channels) // lane
    output_field = output_field.transpose(1, 0, 2)
    input_grad = input_grad.transpose(1, 0, 2)
    second = call(
        pack_kernel,
        "pack",
        jax.ShapeDtypeStruct((lat_size, z_size * block_rows + small_rows, lane), BF16),
        mine,
        theirs,
        depth_mine,
        depth_theirs,
        gain_one,
        gain_two,
        megabytes=56,
    )
    field = jax.ShapeDtypeStruct(output_field.shape, BF16)
    second, output_field, input_grad = call(
        merge_kernel,
        "merge",
        (jax.ShapeDtypeStruct((z_size, block_rows + small_rows, lane), BF16), field, field),
        exchange(second, "lat"),
        output_field,
        input_grad,
        specs=[pl.BlockSpec(memory_space=pltpu.VMEM)] + [pl.BlockSpec(memory_space=pl.ANY)] * 2,
        out_specs=(pl.BlockSpec(memory_space=pltpu.VMEM),)
        + (pl.BlockSpec(memory_space=pl.ANY),) * 2,
        aliases={1: 1, 2: 2},
    )
    weight = lambda rows, cols: jax.ShapeDtypeStruct((rows, cols), F32)
    second = exchange(second, "z")
    small = call(small_sum_kernel, "small_sums", weight(small_rows, lane), second)
    expand_grad, shrink_grad, attention_in_grad, attention_out_grad = call(
        finish_kernel,
        "finish",
        (
            weight(lane, split),
            weight(out_split, wide // lat_size),
            weight(in_split, lane),
            weight(out_split, lane),
        ),
        second,
        first_sums,
    )
    other = core_swap(small)
    if split % 128 == 0:
        depth_grad, input_gain_grad, attention_gain_grad = pl.pallas_call(
            functools.partial(small_kernel, split),
            out_shape=(
                jax.ShapeDtypeStruct((3, 3, wide), F32),
                weight(1, channels),
                weight(1, channels),
            ),
            in_specs=[
                pl.BlockSpec(memory_space=pltpu.SMEM),
                pl.BlockSpec(memory_space=pltpu.VMEM),
                pl.BlockSpec(memory_space=pltpu.VMEM),
                pl.BlockSpec(memory_space=pl.ANY),
            ],
        name="small_grads",
        )(core.reshape(1), small, other, attention_out_grad)
    else:
        rows = 9 * wide // 2 // lane
        own_half, other_half = small[:rows], other[:rows]
        depth_grad = jnp.where(
            core == 0, jnp.stack([own_half, other_half]), jnp.stack([other_half, own_half])
        )
        depth_grad = depth_grad.reshape(2, z_size, split // lane, 9, lane).transpose(3, 1, 0, 2, 4)
        depth_grad = depth_grad.reshape(3, 3, wide)
        gains = (small[rows:] + other[rows:]).reshape(2, channels)
        input_gain_grad, attention_gain_grad = gains[0], gains[1]
    return (
        output_field.transpose(1, 0, 2),
        input_grad.transpose(1, 0, 2),
        expand_grad,
        shrink_grad.T,
        attention_in_grad.T,
        attention_out_grad.T,
        depth_grad,
        input_gain_grad.reshape(channels),
        attention_gain_grad.reshape(channels),
    )


def solution(mesh):
    lat_size, lon_size = mesh.devices.shape
    split = Mesh(mesh.devices.reshape(lat_size, lon_size // 2, 2), ("lat", "z", "core"))
    grid = P("lat", LON, None)
    weight = P("lat", LON)

    def step(*arrays):
        outputs = jax.shard_map(
            per_device,
            mesh=split,
            in_specs=(grid, grid, grid) + (P(),) * 7,
            out_specs=(grid, grid, weight, weight, weight, weight, P(), P(), P()),
            check_vma=False,
        )(*arrays)
        return outputs

    return step
```

```python
import functools
import math

import jax
import jax.numpy as jnp
from jax import lax
from jax.experimental import pallas as pl
from jax.experimental.pallas import tpu as pltpu
from jax.sharding import Mesh
from jax.sharding import PartitionSpec as P

EPSILON = 1e-06
LON = ("z", "core")
BF16 = jnp.bfloat16
F32 = jnp.float32
MASKED = -1e30
SIDE = 3
BIAS_ROWS = 16
FORWARD_WIDTH = 1024
LOG2E = math.log2(math.e)


def inverse_rms(values):
    return lax.rsqrt(jnp.mean(values * values, axis=-1, keepdims=True) + EPSILON)


def norm_back(back_normed, state, inverse, gain):
    scaled = back_normed * gain
    return inverse * scaled - inverse * inverse * inverse * state * jnp.mean(
        scaled * state, axis=-1, keepdims=True
    )


def shifts(count, step, periodic):
    return [(i, (i + step) % count) for i in range(count) if periodic or 0 <= i + step < count]


def from_sides(block, width, dim, axis, periodic):
    count = lax.axis_size(axis)
    size = block.shape[dim]
    low = lax.ppermute(
        lax.slice_in_dim(block, size - width, size, axis=dim), axis, shifts(count, 1, periodic)
    )
    high = lax.ppermute(
        lax.slice_in_dim(block, 0, width, axis=dim), axis, shifts(count, -1, periodic)
    )
    return low, high


def core_swap(values):
    return lax.ppermute(values, "core", [(0, 1), (1, 0)])


def exchange(values, axis):
    return lax.all_to_all(values, axis, 0, 0, tiled=True)


def matmul(left, right):
    return jnp.dot(left, right, preferred_element_type=F32)


def times_transpose(values, weights):
    return lax.dot_general(
        values, weights, (((values.ndim - 1,), (1,)), ((), ())), preferred_element_type=F32
    )


def sigmoid(values):
    return 0.5 + 0.5 * jnp.tanh(0.5 * values)


def silu(values):
    return values * sigmoid(values)


def call(kernel, name, out_shape, *operands, scratch=(), megabytes=16, flops=0, specs=None, out_specs=None, aliases=None):
    return pl.pallas_call(
        kernel,
        out_shape=out_shape,
        scratch_shapes=scratch,
        in_specs=specs or [pl.BlockSpec(memory_space=pltpu.VMEM)] * len(operands),
        out_specs=out_specs
        or jax.tree.map(lambda _: pl.BlockSpec(memory_space=pltpu.VMEM), out_shape),
        input_output_aliases=aliases or {},
        compiler_params=pltpu.CompilerParams(vmem_limit_bytes=megabytes * 1024 * 1024),
        cost_estimate=pl.CostEstimate(
            flops=flops,
            bytes_accessed=sum(x.size * x.dtype.itemsize for x in operands),
            transcendentals=0,
        ),
        name=name,
    )(*operands)


def early_kernel(
    groups, cot_ref, bias_ref, out_weight_ref, order_ref, early_ref, framed_ref, bias_frame, wide_frame
):
    row_count, lon_count, channels = cot_ref.shape
    frame = framed_ref.shape[1]
    width = channels // groups
    head_count = bias_ref.shape[2]
    items = head_count // groups
    in_rows = early_ref.shape[2] == width
    wide_frame[...] = jnp.zeros_like(wide_frame)
    bias_frame[...] = jnp.full_like(bias_frame, MASKED)
    for row in range(row_count):
        wide_frame[row, SIDE : SIDE + lon_count, :] = cot_ref[row].astype(F32)
        framed_ref[row] = wide_frame[row].astype(BF16)
        bias_frame[row, SIDE : SIDE + lon_count, 0:head_count] = bias_ref[row].astype(F32)
    for row in range(row_count):
        back_heads = times_transpose(framed_ref[row], out_weight_ref[...]).astype(BF16)
        bias = bias_frame[row].T if in_rows else bias_frame[row]
        for group in range(groups):
            target = row * groups + group
            early_ref[target, 0:frame, 0:width] = back_heads[:, group * width : (group + 1) * width]
            if in_rows:
                early_ref[target, frame:, :] = bias[
                    group * items : group * items + BIAS_ROWS
                ].astype(BF16)
            else:
                early_ref[target, :, width:] = bias[
                    0:frame, group * items : (group + 1) * items
                ].astype(BF16)


def early_parts(cotangent, key_bias, attention_out, order, groups):
    row_count, lon_count, channels = cotangent.shape
    frame = lon_count + 2 * SIDE
    head_count = key_bias.shape[2]
    width = channels // groups
    if frame <= width and width % 128 == 0:
        shape = (row_count * groups, frame + BIAS_ROWS, width)
        bias_shape = (row_count, width, max(128, head_count + BIAS_ROWS))
    else:
        shape = (row_count * groups, frame, width + head_count // groups)
        bias_shape = (row_count, frame, head_count)
    return call(
        functools.partial(early_kernel, groups),
        "back_heads",
        (
            jax.ShapeDtypeStruct(shape, BF16),
            jax.ShapeDtypeStruct((row_count, frame, channels), BF16),
        ),
        cotangent,
        key_bias,
        attention_out,
        order,
        scratch=[pltpu.VMEM(bias_shape, F32), pltpu.VMEM((row_count, frame, channels), F32)],
        flops=2 * row_count * frame * channels * channels,
    )


def normalise(values, gain):
    return (values * inverse_rms(values) * gain).astype(BF16)


def convolve(values, kernel, rows, frame):
    size = rows * frame
    total = None
    for b in range(3):
        part = kernel[b : b + 1] * values[0:size]
        for a in range(1, 3):
            part = part + kernel[3 * a + b : 3 * a + b + 1] * values[a * frame : a * frame + size]
        if b != 1:
            part = pltpu.roll(part, 1 if b == 0 else size - 1, 0)
        total = part if total is None else total + part
    return total


def forward_kernel(
    frame, groups, steps, state_ref, gain_ref, kernel_ref, second_gain_ref, expand_hbm, shrink_hbm,
    in_hbm, qkv_ref, inner_ref, expand_ref, shrink_ref, in_ref, normed, total, arrived,
):
    cells, channels = inner_ref.shape
    wide = expand_ref.shape[1]
    rows = cells // frame
    width = channels // groups
    part = wide // steps
    parts = [slice(i * part, (i + 1) * part) for i in range(steps)]
    expand_copies, shrink_copies = [], []
    for i, cols in enumerate(parts):
        expand_copies.append(
            pltpu.make_async_copy(expand_hbm.at[:, cols], expand_ref.at[:, cols], arrived.at[i])
        )
        shrink_copies.append(
            pltpu.make_async_copy(shrink_hbm.at[cols], shrink_ref.at[cols], arrived.at[steps + i])
        )
        expand_copies[i].start()
        shrink_copies[i].start()
    in_copy = pltpu.make_async_copy(in_hbm, in_ref, arrived.at[2 * steps])
    in_copy.start()
    near = state_ref[frame : frame + normed.shape[0], :].astype(F32)
    normed[...] = normalise(near, gain_ref[...])
    for i, cols in enumerate(parts):
        expand_copies[i].wait()
        activated = silu(matmul(normed[...], expand_ref[:, cols])).astype(BF16).astype(F32)
        kernel = jnp.concatenate([kernel_ref[a, :, cols] for a in range(3)], axis=0).astype(F32)
        mixed = silu(convolve(activated, kernel, rows, frame)).astype(BF16)
        shrink_copies[i].wait()
        product = matmul(mixed, shrink_ref[cols])
        total[...] = product if i == 0 else total[...] + product
    inner = state_ref[2 * frame : 2 * frame + cells, :].astype(F32)
    inner = (inner + total[...]).astype(BF16)
    inner_ref[...] = inner
    normed_second = normalise(inner.astype(F32), second_gain_ref[...])
    in_copy.wait()
    projected = matmul(normed_second, in_ref[...]).astype(BF16)
    for row in range(rows):
        for group in range(groups):
            for kind in range(3):
                start = kind * channels + group * width
                qkv_ref[row * groups + group, :, kind * width : (kind + 1) * width] = projected[
                    row * frame : (row + 1) * frame, start : start + width
                ]


def step_width(wide):
    return 256 if wide % 256 == 0 else wide


def forward(state, input_gain, expand_weight, kernel, shrink_weight, gain, attention_in, groups):
    all_rows, frame, channels = state.shape
    rows = all_rows - 4
    cells = rows * frame
    wide = expand_weight.shape[1]
    steps = wide // FORWARD_WIDTH
    here, away = pl.BlockSpec(memory_space=pltpu.VMEM), pl.BlockSpec(memory_space=pl.ANY)
    return pl.pallas_call(
        functools.partial(forward_kernel, frame, groups, steps),
        out_shape=(
            jax.ShapeDtypeStruct((rows * groups, frame, 3 * channels // groups), BF16),
            jax.ShapeDtypeStruct((cells, channels), BF16),
        ),
        in_specs=[here] * 4 + [away] * 3,
        scratch_shapes=[
            pltpu.VMEM(expand_weight.shape, BF16),
            pltpu.VMEM(shrink_weight.shape, BF16),
            pltpu.VMEM(attention_in.shape, BF16),
            pltpu.VMEM((cells + 2 * frame, channels), BF16),
            pltpu.VMEM((cells, channels), F32),
            pltpu.SemaphoreType.DMA((2 * steps + 1,)),
        ],
        compiler_params=pltpu.CompilerParams(vmem_limit_bytes=56 * 1024 * 1024),
        cost_estimate=pl.CostEstimate(
            flops=2 * cells * channels * (3 * wide + 3 * channels),
            bytes_accessed=4 * channels * wide + 6 * channels * channels,
            transcendentals=3 * cells * wide,
        ),
        name="forward",
    )(
        state.reshape(all_rows * frame, channels),
        input_gain,
        kernel,
        gain,
        expand_weight,
        shrink_weight,
        attention_in,
    )


def around_kernel(
    frame, state_ref, gain_ref, expand_ref, kernel_ref, order_ref, activated_ref, slope_ref, mixed_ref,
    expand_slope_ref, normed,
):
    size = activated_ref.shape[1]
    cells = mixed_ref.shape[1]

    @pl.when(pl.program_id(0) == 0)
    def _():
        normed[...] = normalise(state_ref[...].astype(F32), gain_ref[...])

    expanded = matmul(normed[...], expand_ref[...])
    gate = sigmoid(expanded)
    activated = (expanded * gate).astype(BF16)
    activated_ref[0] = activated[frame : frame + size]
    own_gate, own = gate[2 * frame : 2 * frame + cells], expanded[2 * frame : 2 * frame + cells]
    expand_slope_ref[0] = (own_gate * (1.0 + own * (1.0 - own_gate))).astype(BF16)
    convolved = convolve(activated.astype(F32), kernel_ref[0], size // frame, frame)
    gate = sigmoid(convolved)
    slope_ref[0] = (gate * (1.0 + convolved * (1.0 - gate))).astype(BF16)
    mixed_ref[0] = (
        convolved[frame : frame + cells] * gate[frame : frame + cells]
    ).astype(BF16)


def around(state, input_gain, expand_weight, kernel, order):
    all_rows, frame, channels = state.shape
    size, cells = (all_rows - 2) * frame, (all_rows - 4) * frame
    wide = expand_weight.shape[1]
    part = step_width(wide)
    fixed = lambda shape: pl.BlockSpec(shape, lambda step: (0,) * len(shape))
    moving = lambda rows: pl.BlockSpec((rows, part), lambda step: (0, step))
    block = lambda rows: pl.BlockSpec((1, rows, part), lambda step: (step, 0, 0))
    steps = wide // part
    return pl.pallas_call(
        functools.partial(around_kernel, frame),
        grid=(steps,),
        out_shape=(
            jax.ShapeDtypeStruct((steps, size, part), BF16),
            jax.ShapeDtypeStruct((steps, size, part), BF16),
            jax.ShapeDtypeStruct((steps, cells, part), BF16),
            jax.ShapeDtypeStruct((steps, cells, part), BF16),
        ),
        in_specs=[
            fixed((all_rows * frame, channels)),
            fixed((1, channels)),
            moving(channels),
            block(9),
            pl.BlockSpec(memory_space=pl.ANY),
        ],
        out_specs=(block(size), block(size), block(cells), block(cells)),
        scratch_shapes=[pltpu.VMEM((all_rows * frame, channels), BF16)],
        compiler_params=pltpu.CompilerParams(
            vmem_limit_bytes=16 * 1024 * 1024, dimension_semantics=("arbitrary",)
        ),
        cost_estimate=pl.CostEstimate(
            flops=2 * all_rows * frame * channels * wide,
            bytes_accessed=2 * channels * wide + 14 * size * wide,
            transcendentals=2 * size * wide,
        ),
        name="forward_around",
    )(state.reshape(all_rows * frame, channels), input_gain, expand_weight, kernel, order)


def inner_kernel(
    groups, norm_factor, attended_ref, inner_ref, cot_ref, out_weight_ref, in_weight_ref, gain_ref,
    output_ref, back_inner_ref, unpacked_ref, gain_grad_ref,
):
    targets, frame, width = attended_ref.shape
    width = width // 4
    row_count, lon_count, channels = output_ref.shape
    for target in range(targets):
        row, group = divmod(target, groups)
        for kind in range(4):
            start = kind * channels + group * width
            unpacked_ref[row * frame : (row + 1) * frame, start : start + width] = attended_ref[
                target, :, kind * width : (kind + 1) * width
            ]
    inner = inner_ref[...].astype(F32)
    output = inner + matmul(unpacked_ref[:, :channels], out_weight_ref[...])
    for row in range(row_count):
        start = row * frame + SIDE
        output_ref[row] = output[start : start + lon_count].astype(BF16)
    back_second = times_transpose(unpacked_ref[:, channels:], in_weight_ref[...])
    inverse = inverse_rms(inner)
    gain_grad_ref[...] = norm_factor * jnp.sum(back_second * inner * inverse, axis=0, keepdims=True)
    back_inner_ref[...] = (
        cot_ref[...].astype(F32) + norm_back(back_second, inner, inverse, gain_ref[...])
    ).astype(BF16)


def weight_grads_kernel(
    norm_factor, z_size, which_ref, unpacked_ref, inner_ref, gain_ref, cot_ref, back_inner_ref,
    mixed_ref, order_ref, *refs
):
    added_ref = refs[0] if len(refs) == 8 else None
    out_ref, whole_in, whole_out, whole_back, in_t, out_t, back_t = refs[-7:]
    lat_size, _, lane = out_ref.shape
    channels = inner_ref.shape[1]
    blocks, _, part = mixed_ref.shape
    blocks = blocks // lat_size
    in_split, out_split = in_t.shape[0] // z_size, out_t.shape[0] // z_size
    first_rows = out_ref.shape[1] // z_size
    normed_second = normalise(inner_ref[...].astype(F32), gain_ref[...])
    whole_in[...] = unpacked_ref[:, channels:].T
    whole_out[...] = cot_ref[...].T
    whole_back[...] = back_inner_ref[...].T
    for z in range(z_size):
        lon = 2 * z + which_ref[0]
        for source, target, split in (
            (whole_in, in_t, in_split),
            (whole_out, out_t, out_split),
            (whole_back, back_t, out_split),
        ):
            target[z * split : (z + 1) * split, :] = source[
                pl.ds(pl.multiple_of(lon * split, split), split), :
            ]

    def put(lat, start, split, values):
        values = values * norm_factor
        for z in range(z_size):
            rows = slice(z * first_rows + start, z * first_rows + start + split)
            value = values[z * split : (z + 1) * split]
            if added_ref is not None:
                value = value + added_ref[lat, rows, :].astype(F32)
            out_ref[lat, rows, :] = value.astype(BF16)

    for lat in range(lat_size):
        cols = slice(lat * lane, (lat + 1) * lane)
        put(lat, 0, in_split, matmul(in_t[...], normed_second[:, cols]))
        put(lat, in_split, out_split, matmul(out_t[...], unpacked_ref[:, cols]))
        start = in_split + out_split
        for block in range(blocks):
            values = matmul(back_t[...], mixed_ref[lat * blocks + block])
            for piece in range(part // lane):
                put(lat, start, out_split, values[:, piece * lane : (piece + 1) * lane])
                start += out_split


def weight_grads(
    which, unpacked, inner, gain, cot, back_inner, mixed, order, added, norm_factor, lat_size, z_size
):
    own, channels = inner.shape
    lane = channels // lat_size
    wide = mixed.shape[0] * mixed.shape[2]
    rows = 2 * channels + channels // 2 * (wide // channels)
    operands = (unpacked, inner, gain, cot, back_inner, mixed, order)
    if added is not None:
        operands += (added,)
    in_specs = [pl.BlockSpec(memory_space=pltpu.VMEM)] * len(operands)
    in_specs[6] = pl.BlockSpec(memory_space=pl.ANY)
    tall, short = pltpu.VMEM((3 * channels, own), BF16), pltpu.VMEM((channels, own), BF16)
    return pl.pallas_call(
        functools.partial(weight_grads_kernel, norm_factor, z_size),
        out_shape=jax.ShapeDtypeStruct((lat_size, rows, lane), BF16),
        in_specs=[pl.BlockSpec(memory_space=pltpu.SMEM)] + in_specs,
        scratch_shapes=[
            tall,
            short,
            short,
            pltpu.VMEM((3 * channels // 2, own), BF16),
            pltpu.VMEM((channels // 2, own), BF16),
            pltpu.VMEM((channels // 2, own), BF16),
        ],
        compiler_params=pltpu.CompilerParams(vmem_limit_bytes=20 * 1024 * 1024),
        cost_estimate=pl.CostEstimate(
            flops=own * channels * (4 * channels + wide),
            bytes_accessed=2 * channels * (8 * channels + 2 * wide),
            transcendentals=0,
        ),
        name="weight_grads",
    )(which.reshape(1), *operands)


def after_kernel(*refs):
    pass


def after(values, *others):
    away = pl.BlockSpec(memory_space=pl.ANY)
    return pl.pallas_call(
        after_kernel,
        out_shape=jax.ShapeDtypeStruct(values.shape, values.dtype),
        in_specs=[away] * (1 + len(others)),
        out_specs=away,
        input_output_aliases={0: 0},
        name="after",
    )(values, *others)


def sum_kernel(parts_ref, out_ref):
    out_ref[...] = summed(parts_ref, slice(None)).astype(BF16)


def sum_parts(parts):
    return call(sum_kernel, "sum_bands", jax.ShapeDtypeStruct(parts.shape[1:], BF16), parts, megabytes=8)


def pack_kernel(
    left_ref, right_ref, mine_ref, theirs_ref, first_gain_ref, second_gain_ref, out_ref
):
    depth = mine_ref[...] + theirs_ref[...]
    rows, lane = left_ref.shape[1:]
    out_ref[:, 0:rows, :] = (left_ref[...].astype(F32) + right_ref[...].astype(F32)).astype(BF16)
    small = []
    for z in range(depth.shape[0]):
        for start in range(0, depth.shape[2], lane):
            small.append(depth[z, :, start : start + lane])
    for ref in (first_gain_ref, second_gain_ref):
        for start in range(0, ref.shape[1], lane):
            small.append(ref[:, start : start + lane])
    small = jnp.concatenate(small, axis=0).astype(BF16)
    for lat in range(out_ref.shape[0]):
        out_ref[lat, rows:, :] = small


def summed(ref, rows):
    total = ref[0, rows, :].astype(F32)
    for part in range(1, ref.shape[0]):
        total = total + ref[part, rows, :].astype(F32)
    return total


def merge_kernel(parts_ref, output_ref, input_ref, out_ref, output_out, input_out):
    z_size, out_rows, _ = out_ref.shape
    rows = parts_ref.shape[1]
    block = (rows - out_rows) // (z_size - 1)
    small = summed(parts_ref, slice(z_size * block, rows)).astype(BF16)
    for z in range(z_size):
        out_ref[z, 0:block, :] = summed(parts_ref, slice(z * block, (z + 1) * block)).astype(BF16)
        out_ref[z, block:, :] = small


def small_sum_kernel(parts_ref, small_ref):
    rows = parts_ref.shape[1] - small_ref.shape[0]
    small_ref[...] = summed(parts_ref, slice(rows, parts_ref.shape[1]))


def finish_kernel(parts_ref, first_ref, expand_ref, shrink_ref, in_ref, out_ref):
    block, split = expand_ref.shape
    lane = parts_ref.shape[2]
    for piece in range(split // lane):
        expand_ref[:, piece * lane : (piece + 1) * lane] = summed(
            parts_ref, slice(piece * block, (piece + 1) * block)
        )
    in_split, out_split = in_ref.shape[0], out_ref.shape[0]
    at = in_split + out_split
    in_ref[...] = first_ref[0:in_split, :].astype(F32)
    out_ref[...] = first_ref[in_split:at, :].astype(F32)
    for piece in range(shrink_ref.shape[1] // lane):
        shrink_ref[:, piece * lane : (piece + 1) * lane] = first_ref[at : at + out_split, :].astype(
            F32
        )
        at += out_split


def small_kernel(
    split, core_ref, mine_ref, theirs_ref, order_ref, depth_ref, first_gain_ref, second_gain_ref
):
    lane = mine_ref.shape[1]
    wide = depth_ref.shape[2]
    channels = first_gain_ref.shape[1]
    half_rows = 9 * wide // 2 // lane
    core = core_ref[0]
    pieces = wide // lane
    in_block = split // lane
    for side in range(2):
        which = core if side == 0 else 1 - core
        for piece in range(pieces // 2):
            source = mine_ref if side == 0 else theirs_ref
            block = source[piece * 9 : piece * 9 + 9, :]
            z, rest = divmod(piece, in_block)
            start = pl.multiple_of((2 * z + which) * split, lane) + rest * lane
            for a in range(3):
                depth_ref[a, :, pl.ds(pl.multiple_of(start, lane), lane)] = block[3 * a : 3 * a + 3]
    at = half_rows
    for ref in (first_gain_ref, second_gain_ref):
        for start in range(0, channels, lane):
            ref[:, start : start + lane] = mine_ref[at : at + 1, :] + theirs_ref[at : at + 1, :]
            at += 1


def backward_kernel(
    frame, norm_factor, stride, which_ref, *refs
):
    earlier_ref = refs[0] if len(refs) == 25 else None
    (
        back_ref, state_ref, gain_ref, kernel_ref, order_ref, shrink_hbm, slope_hbm,
        expand_slope_hbm, expand_hbm, activated_hbm, part_hbm, depth_ref, input_ref, gain_grad_ref,
        back_normed, shrink_all, slope_all, expand_slope_all, expand_all, activated_all, part_ref,
        normed, arrived, sent,
    ) = refs[-24:]
    cells, channels = state_ref.shape
    row_count, lon_count, _ = input_ref.shape
    lat_size, steps, _, lane = part_ref.shape
    part = slope_all.shape[2]
    block = channels // lat_size
    copies = []
    for step in range(steps):
        place = stride * step + which_ref[0]
        here = pl.ds(pl.multiple_of(place * part, part), part)
        pairs = (
            (shrink_hbm.at[here], shrink_all.at[step]),
            (slope_hbm.at[place], slope_all.at[step]),
            (expand_slope_hbm.at[place], expand_slope_all.at[step]),
            (expand_hbm.at[:, here], expand_all.at[step]),
            (activated_hbm.at[place], activated_all.at[step]),
        )
        copies.append(
            [
                pltpu.make_async_copy(source, target, arrived.at[step, i])
                for i, (source, target) in enumerate(pairs)
            ]
        )
        for copy in copies[step]:
            copy.start()
    column = lax.broadcasted_iota(jnp.int32, (frame, part), 0)
    outside = (column < SIDE) | (column >= SIDE + lon_count)
    outside = jnp.concatenate([outside] * row_count, axis=0)
    normed[...] = normalise(state_ref[...].astype(F32), gain_ref[...]).T
    sends = []
    for step in range(steps):
        place = stride * step + which_ref[0]
        kernel = kernel_ref[place]
        copies[step][0].wait()
        copies[step][1].wait()
        back_convolved = times_transpose(back_ref[...], shrink_all[step])
        back_convolved = (back_convolved * slope_all[step].astype(F32)).astype(BF16).astype(F32)
        flipped = jnp.concatenate([kernel[8 - i : 9 - i] for i in range(9)], axis=0)
        back_activated = convolve(back_convolved, flipped, row_count, frame)
        copies[step][2].wait()
        back_expanded = back_activated * expand_slope_all[step].astype(F32)
        back_expanded = jnp.where(outside, 0.0, back_expanded).astype(BF16)
        expand_grad = (matmul(normed[...], back_expanded) * norm_factor).astype(BF16)
        for lat in range(lat_size):
            for piece in range(part // lane):
                part_ref[lat, step, piece * block : (piece + 1) * block, :] = expand_grad[
                    lat * block : (lat + 1) * block, piece * lane : (piece + 1) * lane
                ]
        sends.append(
            pltpu.make_async_copy(part_ref.at[:, step], part_hbm.at[:, step], sent.at[step])
        )
        sends[step].start()
        copies[step][3].wait()
        product = times_transpose(back_expanded, expand_all[step])
        if step > 0:
            product = product + back_normed[...]
        elif earlier_ref is not None:
            product = product + earlier_ref[...]
        back_normed[...] = product
        own_back = jnp.where(outside, 0.0, back_convolved[frame : frame + cells])
        copies[step][4].wait()
        activated = activated_all[step].astype(F32)
        for b in range(3):
            moved = own_back
            if b != 1:
                moved = pltpu.roll(own_back, cells - 1 if b == 0 else 1, 0)
            for a in range(3):
                depth_ref[step, 3 * a + b : 3 * a + b + 1, :] = norm_factor * jnp.sum(
                    activated[a * frame : a * frame + cells] * moved, axis=0, keepdims=True
                )
    state = state_ref[...].astype(F32)
    inverse = inverse_rms(state)
    grads = back_normed[...]
    gain_grad_ref[...] = norm_factor * jnp.sum(grads * state * inverse, axis=0, keepdims=True)
    result = back_ref[frame : frame + cells, :].astype(F32) + norm_back(
        grads, state, inverse, gain_ref[...]
    )
    for row in range(row_count):
        start = row * frame + SIDE
        input_ref[row] = result[start : start + lon_count].astype(BF16)
    for send in sends:
        send.wait()


def backward(
    which, back, state, gain, earlier, order, shrink_weight, slope, activated, expand_weight,
    expand_slope, kernel, norm_factor, lat_size, row_count, lon_count,
):
    cells, channels = state.shape
    frame = cells // row_count
    steps, size, part = activated.shape
    stride = 1
    if which is None:
        which = 0
    else:
        steps, stride = steps // 2, 2
    block = channels // lat_size
    lane = block
    part_shape = (lat_size, steps, part // lane * block, lane)
    here, away = pl.BlockSpec(memory_space=pltpu.VMEM), pl.BlockSpec(memory_space=pl.ANY)
    operands = (back, state, gain, kernel)
    if earlier is not None:
        operands = (earlier,) + operands
    return pl.pallas_call(
        functools.partial(backward_kernel, frame, norm_factor, stride),
        in_specs=[pl.BlockSpec(memory_space=pltpu.SMEM)] + [here] * len(operands) + [away] * 6,
        out_specs=(away,) + (here,) * 4,
        scratch_shapes=[
            pltpu.VMEM((steps, part, channels), BF16),
            pltpu.VMEM((steps, size, part), BF16),
            pltpu.VMEM((steps, cells, part), BF16),
            pltpu.VMEM((steps, channels, part), BF16),
            pltpu.VMEM((steps, size, part), BF16),
            pltpu.VMEM(part_shape, BF16),
            pltpu.VMEM((channels, cells), BF16),
            pltpu.SemaphoreType.DMA((steps, 5)),
            pltpu.SemaphoreType.DMA((steps,)),
        ],
        out_shape=(
            jax.ShapeDtypeStruct(part_shape, BF16),
            jax.ShapeDtypeStruct((steps, 9, part), F32),
            jax.ShapeDtypeStruct((row_count, lon_count, channels), BF16),
            jax.ShapeDtypeStruct((1, channels), F32),
            jax.ShapeDtypeStruct((cells, channels), F32),
        ),
        compiler_params=pltpu.CompilerParams(vmem_limit_bytes=56 * 1024 * 1024),
        cost_estimate=pl.CostEstimate(
            flops=8 * cells * channels * part * steps,
            bytes_accessed=(6 * channels + 12 * size) * part * steps,
            transcendentals=0,
        ),
        name="backward",
    )(
        jnp.reshape(which, (1,)).astype(jnp.int32), *operands, order, shrink_weight, slope,
        expand_slope, expand_weight, activated,
    )


def attention_kernel(
    head_width, query_block, qkv_ref, early_ref, order_ref, out_ref, heads_t, query_grad_t, key_t,
    value_t, back_ref, bias_ref, key_grad, value_grad, score_ref, back_prob_ref, prob_low_ref, back_score_ref,
):
    head = pl.program_id(0)
    cells = qkv_ref.shape[0]
    width = qkv_ref.shape[1] // 3
    sources = early_ref.shape[0]
    frame = cells // sources
    scale = 1.0 / math.sqrt(head_width)
    keys = qkv_ref[:, width : 2 * width]
    values = qkv_ref[:, 2 * width : 3 * width]
    part = 2 * frame

    @pl.when(head == 0)
    def _():
        key_t[...] = keys.T
        value_t[...] = values.T
        for source in range(sources):
            at = slice(source * frame, (source + 1) * frame)
            back_ref[at, :] = early_ref[source, 0:frame, 0:width]
            if early_ref.shape[1] > frame:
                bias_ref[at, :] = early_ref[source, frame:, :].astype(F32).T[0:frame]
            else:
                bias_ref[at, :] = early_ref[source, :, width:].astype(F32)
        key_grad[...] = jnp.zeros_like(key_grad)
        value_grad[...] = jnp.zeros_like(value_grad)

    lanes = lax.broadcasted_iota(jnp.int32, (1, width), 1) // head_width == head
    zero = jnp.zeros((), BF16)
    heads = lax.broadcasted_iota(jnp.int32, bias_ref.shape, 1)
    bias = LOG2E * jnp.sum(
        jnp.where(heads == head, bias_ref[...], 0.0), axis=1, keepdims=True
    )
    rows = pl.ds(pl.multiple_of(head * head_width, head_width), head_width)
    head_key_t = key_t[rows, :]
    head_value_t = value_t[rows, :]
    last_dims = (((1,), (1,)), ((), ()))

    def fold(values, combine):
        result = values[0:8]
        for start in range(8, values.shape[0], 8):
            result = combine(result, values[start : start + 8])
        return result

    def block(start):
        cols = pl.ds(start, query_block)
        queries = jnp.where(lanes, qkv_ref[cols, 0:width], zero)
        backs = jnp.where(lanes, back_ref[cols, :], zero)
        parts = [slice(i, i + part) for i in range(0, cells, part)]
        highest = jnp.full((8, query_block), -jnp.inf, F32)
        for at in parts:
            scores = lax.dot_general(
                qkv_ref[at, width : 2 * width], queries, last_dims, preferred_element_type=F32
            )
            scores = scores * (scale * LOG2E) + bias[at]
            score_ref[at, :] = scores
            highest = jnp.maximum(highest, fold(scores, jnp.maximum))
        highest = jnp.max(highest, axis=0, keepdims=True)
        total = jnp.zeros((8, query_block), F32)
        centred = jnp.zeros((8, query_block), F32)
        for at in parts:
            back_probs = lax.dot_general(
                qkv_ref[at, 2 * width : 3 * width], backs, last_dims, preferred_element_type=F32
            )
            exponent = jnp.exp2(score_ref[at, :] - highest)
            total = total + fold(exponent, jnp.add)
            centred = centred + fold(exponent * back_probs, jnp.add)
            score_ref[at, :] = exponent
            back_prob_ref[at, :] = back_probs
        inverse = 1.0 / jnp.sum(total, axis=0, keepdims=True)
        centred = jnp.sum(centred, axis=0, keepdims=True) * inverse
        for at in parts:
            probs = score_ref[at, :] * inverse
            probs_low = probs.astype(BF16)
            back_scores = (probs * (back_prob_ref[at, :] - centred)).astype(BF16)
            prob_low_ref[at, :] = probs_low
            back_score_ref[at, :] = back_scores
            value_grad[at, :] += matmul(probs_low, backs)
            key_grad[at, :] += matmul(back_scores, queries)
        heads_t[rows, cols] = matmul(head_value_t, prob_low_ref[...])
        query_grad_t[rows, cols] = matmul(head_key_t, back_score_ref[...])

    block_count = cells // query_block
    if block_count <= 4:
        for index in range(block_count):
            block(index * query_block)
    else:

        def step(index, carry):
            block(pl.multiple_of(index * query_block, query_block))
            return carry

        lax.fori_loop(0, block_count, step, 0)

    @pl.when(head == pl.num_programs(0) - 1)
    def _():
        out_ref[:, 0:width] = heads_t[...].T.astype(BF16)
        out_ref[:, width : 2 * width] = (query_grad_t[...] * scale).T.astype(BF16)
        out_ref[:, 2 * width : 3 * width] = (key_grad[...] * scale).astype(BF16)
        out_ref[:, 3 * width : 4 * width] = value_grad[...].astype(BF16)


def attention(qkv, early, order, head_width):
    cells = qkv.shape[0]
    width = qkv.shape[1] // 3
    items = width // head_width
    bias_columns = BIAS_ROWS if early.shape[2] == width else items
    query_block = cells if cells <= 1024 else 256
    whole = lambda shape: pl.BlockSpec(shape, lambda head: (0,) * len(shape))
    return pl.pallas_call(
        functools.partial(attention_kernel, head_width, query_block),
        grid=(items,),
        out_shape=jax.ShapeDtypeStruct((cells, 4 * width), BF16),
        in_specs=[whole(qkv.shape), whole(early.shape), pl.BlockSpec(memory_space=pl.ANY)],
        out_specs=whole((cells, 4 * width)),
        scratch_shapes=[
            pltpu.VMEM((width, cells), F32),
            pltpu.VMEM((width, cells), F32),
            pltpu.VMEM((width, cells), BF16),
            pltpu.VMEM((width, cells), BF16),
            pltpu.VMEM((cells, width), BF16),
            pltpu.VMEM((cells, bias_columns), F32),
            pltpu.VMEM((cells, width), F32),
            pltpu.VMEM((cells, width), F32),
            pltpu.VMEM((cells, query_block), F32),
            pltpu.VMEM((cells, query_block), F32),
            pltpu.VMEM((cells, query_block), BF16),
            pltpu.VMEM((cells, query_block), BF16),
        ],
        compiler_params=pltpu.CompilerParams(
            vmem_limit_bytes=(20 if cells <= 1024 else 48) * 1024 * 1024, dimension_semantics=("arbitrary",)
        ),
        cost_estimate=pl.CostEstimate(
            flops=items * cells * cells * 32 * 14,
            bytes_accessed=cells * width * 16,
            transcendentals=items * cells * cells,
        ),
        name="attention",
    )(qkv, early, order)


def per_device(
    state_field,
    cotangent,
    key_bias,
    input_gain,
    expand_weight,
    depth_weight,
    shrink_weight,
    attention_gain,
    attention_in,
    attention_out,
):
    row_count, lon_count, channels = state_field.shape
    head_count = key_bias.shape[2]
    head_width = channels // head_count
    wide = expand_weight.shape[1]
    lat_size, z_size = lax.axis_size("lat"), lax.axis_size("z")
    lon_size = 2 * z_size
    core = lax.axis_index("core")
    norm_factor = 1.0 / math.sqrt(row_count * lon_count * lat_size * lon_size)
    items = row_count * head_count // lon_size
    groups = head_count // items
    width = items * head_width
    frame = lon_count + 2 * SIDE
    own = row_count * frame
    kernel = depth_weight.astype(F32).reshape(9, wide)
    kernel_blocks = kernel.reshape(9, -1, step_width(wide)).transpose(1, 0, 2)
    input_gain = input_gain.reshape(1, channels)
    attention_gain = attention_gain.reshape(1, channels)

    low, high = from_sides(state_field, SIDE, 1, LON, True)
    state = jnp.concatenate([low, state_field, high], axis=1)
    if row_count == 1:
        below, above = from_sides(state, 1, 0, "lat", False)
        far_below = lax.ppermute(below, "lat", shifts(lat_size, 1, False))
        far_above = lax.ppermute(above, "lat", shifts(lat_size, -1, False))
        all_rows = [far_below, below, state, above, far_above]
    else:
        below, above = from_sides(state, 2, 0, "lat", False)
        all_rows = [below, state, above]
    all_rows = jnp.concatenate(all_rows, axis=0)

    early, cot = early_parts(cotangent, key_bias, attention_out, state, groups)
    early = exchange(early, LON)

    qkv, inner = forward(
        all_rows, input_gain, expand_weight, depth_weight, shrink_weight, attention_gain,
        attention_in,
        groups,
    )
    activated, slope, mixed, expand_slope = around(
        all_rows, input_gain, expand_weight, kernel_blocks, inner
    )
    qkv = exchange(qkv, LON).reshape(lon_size * frame, 3 * width)

    attended = attention(qkv, early, mixed, head_width)
    attended = exchange(attended.reshape(lon_size, frame, 4 * width), LON)
    cot = cot.reshape(own, channels)
    output_field, back_inner, unpacked, gain_two = call(
        functools.partial(inner_kernel, groups, norm_factor),
        "back_inner",
        (
            jax.ShapeDtypeStruct((row_count, lon_count, channels), BF16),
            jax.ShapeDtypeStruct((own, channels), BF16),
            jax.ShapeDtypeStruct((own, 4 * channels), BF16),
            jax.ShapeDtypeStruct((1, channels), F32),
        ),
        attended,
        inner,
        cot,
        attention_out,
        attention_in,
        attention_gain,
        flops=8 * own * channels * channels,
    )

    back = back_inner.reshape(row_count, frame, channels)
    centre = back[:, SIDE : SIDE + lon_count]
    low, high = from_sides(centre, 1, 1, LON, True)
    edge = jnp.zeros((row_count, SIDE - 1, channels), BF16)
    back_sides = jnp.concatenate([edge, low, centre, high, edge], axis=1)
    below, above = from_sides(back_sides, 1, 0, "lat", False)
    back = jnp.concatenate([below, back_sides, above], axis=0).reshape(-1, channels)

    lane = channels // lat_size
    in_split, out_split, split = 3 * channels // lon_size, channels // lon_size, wide // lon_size
    grads = lambda which, order, added: weight_grads(
        which, unpacked, inner, attention_gain, cot, back_inner, mixed, order, added, norm_factor,
        lat_size, z_size,
    )
    theirs = grads(1 - core, back_sides, None)
    first = after(grads(core, back_sides, core_swap(theirs)), below, above)
    first_sums = sum_parts(exchange(first, "lat"))
    first_sums = lax.psum_scatter(first_sums, "z", scatter_dimension=0, tiled=True)
    flat = lambda parts: parts.reshape(lat_size, -1, lane)

    state = state.reshape(own, channels)

    def backward_part(which, earlier, order):
        return backward(
            which, back, state, input_gain, earlier, order, shrink_weight, slope, activated,
            expand_weight, expand_slope, kernel_blocks, norm_factor, lat_size, row_count, lon_count,
        )

    if split == step_width(wide):
        theirs, depth_theirs, _, _, partial = backward_part(1 - core, None, first)
        theirs = core_swap(theirs)
        depth_theirs = core_swap(depth_theirs)
        mine, depth_mine, input_grad, gain_one, _ = backward_part(core, partial, first)
    else:
        parts, depth, input_grad, gain_one, _ = backward_part(None, None, first)
        steps = parts.shape[1]
        parts = parts.reshape(lat_size, steps, -1, split // lane, lane, lane)
        parts = parts.reshape(lat_size, z_size, 2, split // lane * lane, lane)
        theirs = core_swap(lax.dynamic_index_in_dim(parts, 1 - core, 2, False))
        mine = lax.dynamic_index_in_dim(parts, core, 2, False)
        depth = depth.reshape(steps, 9, -1, split).transpose(0, 2, 1, 3)
        depth = depth.reshape(z_size, 2, 9, split)
        depth_theirs = core_swap(lax.dynamic_index_in_dim(depth, 1 - core, 1, False))
        depth_mine = lax.dynamic_index_in_dim(depth, core, 1, False)

    mine, theirs = flat(mine), flat(theirs)
    block_rows = mine.shape[1] // z_size
    small_rows = (9 * wide // 2 + 2 * channels) // lane
    output_field = output_field.transpose(1, 0, 2)
    input_grad = input_grad.transpose(1, 0, 2)
    second = call(
        pack_kernel,
        "pack",
        jax.ShapeDtypeStruct((lat_size, z_size * block_rows + small_rows, lane), BF16),
        mine,
        theirs,
        depth_mine,
        depth_theirs,
        gain_one,
        gain_two,
        megabytes=56,
    )
    field = jax.ShapeDtypeStruct(output_field.shape, BF16)
    second, output_field, input_grad = call(
        merge_kernel,
        "merge",
        (jax.ShapeDtypeStruct((z_size, block_rows + small_rows, lane), BF16), field, field),
        exchange(second, "lat"),
        output_field,
        input_grad,
        specs=[pl.BlockSpec(memory_space=pltpu.VMEM)] + [pl.BlockSpec(memory_space=pl.ANY)] * 2,
        out_specs=(pl.BlockSpec(memory_space=pltpu.VMEM),)
        + (pl.BlockSpec(memory_space=pl.ANY),) * 2,
        aliases={1: 1, 2: 2},
    )
    weight = lambda rows, cols: jax.ShapeDtypeStruct((rows, cols), F32)
    second = exchange(second, "z")
    small = call(small_sum_kernel, "small_sums", weight(small_rows, lane), second)
    expand_grad, shrink_grad, attention_in_grad, attention_out_grad = call(
        finish_kernel,
        "finish",
        (
            weight(lane, split),
            weight(out_split, wide // lat_size),
            weight(in_split, lane),
            weight(out_split, lane),
        ),
        second,
        first_sums,
    )
    other = core_swap(small)
    if split % 128 == 0:
        depth_grad, input_gain_grad, attention_gain_grad = pl.pallas_call(
            functools.partial(small_kernel, split),
            out_shape=(
                jax.ShapeDtypeStruct((3, 3, wide), F32),
                weight(1, channels),
                weight(1, channels),
            ),
            in_specs=[
                pl.BlockSpec(memory_space=pltpu.SMEM),
                pl.BlockSpec(memory_space=pltpu.VMEM),
                pl.BlockSpec(memory_space=pltpu.VMEM),
                pl.BlockSpec(memory_space=pl.ANY),
            ],
        name="small_grads",
        )(core.reshape(1), small, other, attention_out_grad)
    else:
        rows = 9 * wide // 2 // lane
        own_half, other_half = small[:rows], other[:rows]
        depth_grad = jnp.where(
            core == 0, jnp.stack([own_half, other_half]), jnp.stack([other_half, own_half])
        )
        depth_grad = depth_grad.reshape(2, z_size, split // lane, 9, lane).transpose(3, 1, 0, 2, 4)
        depth_grad = depth_grad.reshape(3, 3, wide)
        gains = (small[rows:] + other[rows:]).reshape(2, channels)
        input_gain_grad, attention_gain_grad = gains[0], gains[1]
    return (
        output_field.transpose(1, 0, 2),
        input_grad.transpose(1, 0, 2),
        expand_grad,
        shrink_grad.T,
        attention_in_grad.T,
        attention_out_grad.T,
        depth_grad,
        input_gain_grad.reshape(channels),
        attention_gain_grad.reshape(channels),
    )


def solution(mesh):
    lat_size, lon_size = mesh.devices.shape
    split = Mesh(mesh.devices.reshape(lat_size, lon_size // 2, 2), ("lat", "z", "core"))
    grid = P("lat", LON, None)
    weight = P("lat", LON)

    def step(*arrays):
        outputs = jax.shard_map(
            per_device,
            mesh=split,
            in_specs=(grid, grid, grid) + (P(),) * 7,
            out_specs=(grid, grid, weight, weight, weight, weight, P(), P(), P()),
            check_vma=False,
        )(*arrays)
        return outputs

    return step
```

```python
import functools
import math

import jax
import jax.numpy as jnp
from jax import lax
from jax.experimental import pallas as pl
from jax.experimental.pallas import tpu as pltpu
from jax.sharding import Mesh
from jax.sharding import PartitionSpec as P

EPSILON = 1e-06
LON = ("z", "core")
BF16 = jnp.bfloat16
F32 = jnp.float32
MASKED = -1e30
SIDE = 3
BIAS_ROWS = 16
FORWARD_WIDTH = 1024
LOG2E = math.log2(math.e)


def inverse_rms(values):
    return lax.rsqrt(jnp.mean(values * values, axis=-1, keepdims=True) + EPSILON)


def norm_back(back_normed, state, inverse, gain):
    scaled = back_normed * gain
    return inverse * scaled - inverse * inverse * inverse * state * jnp.mean(
        scaled * state, axis=-1, keepdims=True
    )


def shifts(count, step, periodic):
    return [(i, (i + step) % count) for i in range(count) if periodic or 0 <= i + step < count]


def from_sides(block, width, dim, axis, periodic):
    count = lax.axis_size(axis)
    size = block.shape[dim]
    low = lax.ppermute(
        lax.slice_in_dim(block, size - width, size, axis=dim), axis, shifts(count, 1, periodic)
    )
    high = lax.ppermute(
        lax.slice_in_dim(block, 0, width, axis=dim), axis, shifts(count, -1, periodic)
    )
    return low, high


def core_swap(values):
    return lax.ppermute(values, "core", [(0, 1), (1, 0)])


def exchange(values, axis):
    return lax.all_to_all(values, axis, 0, 0, tiled=True)


def matmul(left, right):
    return jnp.dot(left, right, preferred_element_type=F32)


def times_transpose(values, weights):
    return lax.dot_general(
        values, weights, (((values.ndim - 1,), (1,)), ((), ())), preferred_element_type=F32
    )


def sigmoid(values):
    return 0.5 + 0.5 * jnp.tanh(0.5 * values)


def silu(values):
    return values * sigmoid(values)


def call(kernel, name, out_shape, *operands, scratch=(), megabytes=16, flops=0, specs=None, out_specs=None, aliases=None):
    return pl.pallas_call(
        kernel,
        out_shape=out_shape,
        scratch_shapes=scratch,
        in_specs=specs or [pl.BlockSpec(memory_space=pltpu.VMEM)] * len(operands),
        out_specs=out_specs
        or jax.tree.map(lambda _: pl.BlockSpec(memory_space=pltpu.VMEM), out_shape),
        input_output_aliases=aliases or {},
        compiler_params=pltpu.CompilerParams(vmem_limit_bytes=megabytes * 1024 * 1024),
        cost_estimate=pl.CostEstimate(
            flops=flops,
            bytes_accessed=sum(x.size * x.dtype.itemsize for x in operands),
            transcendentals=0,
        ),
        name=name,
    )(*operands)


def early_kernel(
    groups, cot_ref, bias_ref, out_weight_ref, order_ref, early_ref, framed_ref, bias_frame, wide_frame
):
    row_count, lon_count, channels = cot_ref.shape
    frame = framed_ref.shape[1]
    width = channels // groups
    head_count = bias_ref.shape[2]
    items = head_count // groups
    in_rows = early_ref.shape[2] == width
    wide_frame[...] = jnp.zeros_like(wide_frame)
    bias_frame[...] = jnp.full_like(bias_frame, MASKED)
    for row in range(row_count):
        wide_frame[row, SIDE : SIDE + lon_count, :] = cot_ref[row].astype(F32)
        framed_ref[row] = wide_frame[row].astype(BF16)
        bias_frame[row, SIDE : SIDE + lon_count, 0:head_count] = bias_ref[row].astype(F32)
    for row in range(row_count):
        back_heads = times_transpose(framed_ref[row], out_weight_ref[...]).astype(BF16)
        bias = bias_frame[row].T if in_rows else bias_frame[row]
        for group in range(groups):
            target = row * groups + group
            early_ref[target, 0:frame, 0:width] = back_heads[:, group * width : (group + 1) * width]
            if in_rows:
                early_ref[target, frame:, :] = bias[
                    group * items : group * items + BIAS_ROWS
                ].astype(BF16)
            else:
                early_ref[target, :, width:] = bias[
                    0:frame, group * items : (group + 1) * items
                ].astype(BF16)


def early_parts(cotangent, key_bias, attention_out, order, groups):
    row_count, lon_count, channels = cotangent.shape
    frame = lon_count + 2 * SIDE
    head_count = key_bias.shape[2]
    width = channels // groups
    if frame <= width and width % 128 == 0:
        shape = (row_count * groups, frame + BIAS_ROWS, width)
        bias_shape = (row_count, width, max(128, head_count + BIAS_ROWS))
    else:
        shape = (row_count * groups, frame, width + head_count // groups)
        bias_shape = (row_count, frame, head_count)
    return call(
        functools.partial(early_kernel, groups),
        "back_heads",
        (
            jax.ShapeDtypeStruct(shape, BF16),
            jax.ShapeDtypeStruct((row_count, frame, channels), BF16),
        ),
        cotangent,
        key_bias,
        attention_out,
        order,
        scratch=[pltpu.VMEM(bias_shape, F32), pltpu.VMEM((row_count, frame, channels), F32)],
        flops=2 * row_count * frame * channels * channels,
    )


def normalise(values, gain):
    return (values * inverse_rms(values) * gain).astype(BF16)


def convolve(values, kernel, rows, frame):
    size = rows * frame
    total = None
    for b in range(3):
        part = kernel[b : b + 1] * values[0:size]
        for a in range(1, 3):
            part = part + kernel[3 * a + b : 3 * a + b + 1] * values[a * frame : a * frame + size]
        if b != 1:
            part = pltpu.roll(part, 1 if b == 0 else size - 1, 0)
        total = part if total is None else total + part
    return total


def forward_kernel(
    frame, groups, steps, state_ref, gain_ref, kernel_ref, second_gain_ref, expand_hbm, shrink_hbm,
    in_hbm, qkv_ref, inner_ref, expand_ref, shrink_ref, in_ref, normed, total, arrived,
):
    cells, channels = inner_ref.shape
    wide = expand_ref.shape[1]
    rows = cells // frame
    width = channels // groups
    part = wide // steps
    parts = [slice(i * part, (i + 1) * part) for i in range(steps)]
    expand_copies, shrink_copies = [], []
    for i, cols in enumerate(parts):
        expand_copies.append(
            pltpu.make_async_copy(expand_hbm.at[:, cols], expand_ref.at[:, cols], arrived.at[i])
        )
        shrink_copies.append(
            pltpu.make_async_copy(shrink_hbm.at[cols], shrink_ref.at[cols], arrived.at[steps + i])
        )
        expand_copies[i].start()
        shrink_copies[i].start()
    in_copy = pltpu.make_async_copy(in_hbm, in_ref, arrived.at[2 * steps])
    in_copy.start()
    near = state_ref[frame : frame + normed.shape[0], :].astype(F32)
    normed[...] = normalise(near, gain_ref[...])
    for i, cols in enumerate(parts):
        expand_copies[i].wait()
        activated = silu(matmul(normed[...], expand_ref[:, cols])).astype(BF16).astype(F32)
        kernel = jnp.concatenate([kernel_ref[a, :, cols] for a in range(3)], axis=0).astype(F32)
        mixed = silu(convolve(activated, kernel, rows, frame)).astype(BF16)
        shrink_copies[i].wait()
        product = matmul(mixed, shrink_ref[cols])
        total[...] = product if i == 0 else total[...] + product
    inner = state_ref[2 * frame : 2 * frame + cells, :].astype(F32)
    inner = (inner + total[...]).astype(BF16)
    inner_ref[...] = inner
    normed_second = normalise(inner.astype(F32), second_gain_ref[...])
    in_copy.wait()
    projected = matmul(normed_second, in_ref[...]).astype(BF16)
    for row in range(rows):
        for group in range(groups):
            for kind in range(3):
                start = kind * channels + group * width
                qkv_ref[row * groups + group, :, kind * width : (kind + 1) * width] = projected[
                    row * frame : (row + 1) * frame, start : start + width
                ]


def step_width(wide):
    return 256 if wide % 256 == 0 else wide


def forward(state, input_gain, expand_weight, kernel, shrink_weight, gain, attention_in, groups):
    all_rows, frame, channels = state.shape
    rows = all_rows - 4
    cells = rows * frame
    wide = expand_weight.shape[1]
    steps = wide // FORWARD_WIDTH
    here, away = pl.BlockSpec(memory_space=pltpu.VMEM), pl.BlockSpec(memory_space=pl.ANY)
    return pl.pallas_call(
        functools.partial(forward_kernel, frame, groups, steps),
        out_shape=(
            jax.ShapeDtypeStruct((rows * groups, frame, 3 * channels // groups), BF16),
            jax.ShapeDtypeStruct((cells, channels), BF16),
        ),
        in_specs=[here] * 4 + [away] * 3,
        scratch_shapes=[
            pltpu.VMEM(expand_weight.shape, BF16),
            pltpu.VMEM(shrink_weight.shape, BF16),
            pltpu.VMEM(attention_in.shape, BF16),
            pltpu.VMEM((cells + 2 * frame, channels), BF16),
            pltpu.VMEM((cells, channels), F32),
            pltpu.SemaphoreType.DMA((2 * steps + 1,)),
        ],
        compiler_params=pltpu.CompilerParams(vmem_limit_bytes=56 * 1024 * 1024),
        cost_estimate=pl.CostEstimate(
            flops=2 * cells * channels * (3 * wide + 3 * channels),
            bytes_accessed=4 * channels * wide + 6 * channels * channels,
            transcendentals=3 * cells * wide,
        ),
        name="forward",
    )(
        state.reshape(all_rows * frame, channels),
        input_gain,
        kernel,
        gain,
        expand_weight,
        shrink_weight,
        attention_in,
    )


def around_kernel(
    frame, state_ref, gain_ref, expand_ref, kernel_ref, order_ref, activated_ref, slope_ref, mixed_ref,
    expand_slope_ref, normed,
):
    size = activated_ref.shape[1]
    cells = mixed_ref.shape[1]

    @pl.when(pl.program_id(0) == 0)
    def _():
        normed[...] = normalise(state_ref[...].astype(F32), gain_ref[...])

    expanded = matmul(normed[...], expand_ref[...])
    gate = sigmoid(expanded)
    activated = (expanded * gate).astype(BF16)
    activated_ref[0] = activated[frame : frame + size]
    own_gate, own = gate[2 * frame : 2 * frame + cells], expanded[2 * frame : 2 * frame + cells]
    expand_slope_ref[0] = (own_gate * (1.0 + own * (1.0 - own_gate))).astype(BF16)
    convolved = convolve(activated.astype(F32), kernel_ref[0], size // frame, frame)
    gate = sigmoid(convolved)
    slope_ref[0] = (gate * (1.0 + convolved * (1.0 - gate))).astype(BF16)
    mixed_ref[0] = (
        convolved[frame : frame + cells] * gate[frame : frame + cells]
    ).astype(BF16)


def around(state, input_gain, expand_weight, kernel, order):
    all_rows, frame, channels = state.shape
    size, cells = (all_rows - 2) * frame, (all_rows - 4) * frame
    wide = expand_weight.shape[1]
    part = step_width(wide)
    fixed = lambda shape: pl.BlockSpec(shape, lambda step: (0,) * len(shape))
    moving = lambda rows: pl.BlockSpec((rows, part), lambda step: (0, step))
    block = lambda rows: pl.BlockSpec((1, rows, part), lambda step: (step, 0, 0))
    steps = wide // part
    return pl.pallas_call(
        functools.partial(around_kernel, frame),
        grid=(steps,),
        out_shape=(
            jax.ShapeDtypeStruct((steps, size, part), BF16),
            jax.ShapeDtypeStruct((steps, size, part), BF16),
            jax.ShapeDtypeStruct((steps, cells, part), BF16),
            jax.ShapeDtypeStruct((steps, cells, part), BF16),
        ),
        in_specs=[
            fixed((all_rows * frame, channels)),
            fixed((1, channels)),
            moving(channels),
            block(9),
            pl.BlockSpec(memory_space=pl.ANY),
        ],
        out_specs=(block(size), block(size), block(cells), block(cells)),
        scratch_shapes=[pltpu.VMEM((all_rows * frame, channels), BF16)],
        compiler_params=pltpu.CompilerParams(
            vmem_limit_bytes=16 * 1024 * 1024, dimension_semantics=("arbitrary",)
        ),
        cost_estimate=pl.CostEstimate(
            flops=2 * all_rows * frame * channels * wide,
            bytes_accessed=2 * channels * wide + 14 * size * wide,
            transcendentals=2 * size * wide,
        ),
        name="forward_around",
    )(state.reshape(all_rows * frame, channels), input_gain, expand_weight, kernel, order)


def inner_kernel(
    groups, norm_factor, attended_ref, inner_ref, cot_ref, out_weight_ref, in_weight_ref, gain_ref,
    output_ref, back_inner_ref, unpacked_ref, gain_grad_ref,
):
    targets, frame, width = attended_ref.shape
    width = width // 4
    row_count, lon_count, channels = output_ref.shape
    for target in range(targets):
        row, group = divmod(target, groups)
        for kind in range(4):
            start = kind * channels + group * width
            unpacked_ref[row * frame : (row + 1) * frame, start : start + width] = attended_ref[
                target, :, kind * width : (kind + 1) * width
            ]
    inner = inner_ref[...].astype(F32)
    output = inner + matmul(unpacked_ref[:, :channels], out_weight_ref[...])
    for row in range(row_count):
        start = row * frame + SIDE
        output_ref[row] = output[start : start + lon_count].astype(BF16)
    back_second = times_transpose(unpacked_ref[:, channels:], in_weight_ref[...])
    inverse = inverse_rms(inner)
    gain_grad_ref[...] = norm_factor * jnp.sum(back_second * inner * inverse, axis=0, keepdims=True)
    back_inner_ref[...] = (
        cot_ref[...].astype(F32) + norm_back(back_second, inner, inverse, gain_ref[...])
    ).astype(BF16)


def weight_grads_kernel(
    norm_factor, z_size, which_ref, unpacked_ref, inner_ref, gain_ref, cot_ref, back_inner_ref,
    mixed_ref, order_ref, *refs
):
    added_ref = out_hbm = None
    if len(refs) == 10:
        added_ref, out_hbm, *refs, sent = refs
    out_ref, whole_in, whole_out, whole_back, in_t, out_t, back_t = refs
    sends = []
    lat_size, _, lane = out_ref.shape
    channels = inner_ref.shape[1]
    blocks, _, part = mixed_ref.shape
    blocks = blocks // lat_size
    in_split, out_split = in_t.shape[0] // z_size, out_t.shape[0] // z_size
    first_rows = out_ref.shape[1] // z_size
    normed_second = normalise(inner_ref[...].astype(F32), gain_ref[...])
    whole_in[...] = unpacked_ref[:, channels:].T
    whole_out[...] = cot_ref[...].T
    whole_back[...] = back_inner_ref[...].T
    for z in range(z_size):
        lon = 2 * z + which_ref[0]
        for source, target, split in (
            (whole_in, in_t, in_split),
            (whole_out, out_t, out_split),
            (whole_back, back_t, out_split),
        ):
            target[z * split : (z + 1) * split, :] = source[
                pl.ds(pl.multiple_of(lon * split, split), split), :
            ]

    def put(lat, start, split, values):
        values = values * norm_factor
        for z in range(z_size):
            rows = slice(z * first_rows + start, z * first_rows + start + split)
            value = values[z * split : (z + 1) * split]
            if added_ref is not None:
                value = value + added_ref[lat, rows, :].astype(F32)
            out_ref[lat, rows, :] = value.astype(BF16)

    for lat in range(lat_size):
        cols = slice(lat * lane, (lat + 1) * lane)
        put(lat, 0, in_split, matmul(in_t[...], normed_second[:, cols]))
        put(lat, in_split, out_split, matmul(out_t[...], unpacked_ref[:, cols]))
        start = in_split + out_split
        for block in range(blocks):
            values = matmul(back_t[...], mixed_ref[lat * blocks + block])
            for piece in range(part // lane):
                put(lat, start, out_split, values[:, piece * lane : (piece + 1) * lane])
                start += out_split
        if out_hbm is not None:
            sends.append(
                pltpu.make_async_copy(out_ref.at[lat], out_hbm.at[lat], sent.at[lat])
            )
            sends[lat].start()
    for send in sends:
        send.wait()


def weight_grads(
    which, unpacked, inner, gain, cot, back_inner, mixed, order, added, norm_factor, lat_size, z_size
):
    own, channels = inner.shape
    lane = channels // lat_size
    wide = mixed.shape[0] * mixed.shape[2]
    rows = 2 * channels + channels // 2 * (wide // channels)
    operands = (unpacked, inner, gain, cot, back_inner, mixed, order)
    if added is not None:
        operands += (added,)
    in_specs = [pl.BlockSpec(memory_space=pltpu.VMEM)] * len(operands)
    in_specs[6] = pl.BlockSpec(memory_space=pl.ANY)
    out_spec, first_scratch, last_scratch = pl.BlockSpec(memory_space=pltpu.VMEM), [], []
    if added is not None:
        out_spec = pl.BlockSpec(memory_space=pl.ANY)
        first_scratch = [pltpu.VMEM((lat_size, rows, lane), BF16)]
        last_scratch = [pltpu.SemaphoreType.DMA((lat_size,))]
    tall, short = pltpu.VMEM((3 * channels, own), BF16), pltpu.VMEM((channels, own), BF16)
    return pl.pallas_call(
        functools.partial(weight_grads_kernel, norm_factor, z_size),
        out_shape=jax.ShapeDtypeStruct((lat_size, rows, lane), BF16),
        in_specs=[pl.BlockSpec(memory_space=pltpu.SMEM)] + in_specs,
        out_specs=out_spec,
        scratch_shapes=first_scratch
        + [
            tall,
            short,
            short,
            pltpu.VMEM((3 * channels // 2, own), BF16),
            pltpu.VMEM((channels // 2, own), BF16),
            pltpu.VMEM((channels // 2, own), BF16),
        ]
        + last_scratch,
        compiler_params=pltpu.CompilerParams(vmem_limit_bytes=20 * 1024 * 1024),
        cost_estimate=pl.CostEstimate(
            flops=own * channels * (4 * channels + wide),
            bytes_accessed=2 * channels * (8 * channels + 2 * wide),
            transcendentals=0,
        ),
        name="weight_grads",
    )(which.reshape(1), *operands)


def after_kernel(*refs):
    pass


def after(values, *others):
    away = pl.BlockSpec(memory_space=pl.ANY)
    return pl.pallas_call(
        after_kernel,
        out_shape=jax.ShapeDtypeStruct(values.shape, values.dtype),
        in_specs=[away] * (1 + len(others)),
        out_specs=away,
        input_output_aliases={0: 0},
        name="after",
    )(values, *others)


def sum_kernel(parts_ref, out_ref):
    out_ref[...] = summed(parts_ref, slice(None)).astype(BF16)


def sum_parts(parts):
    return call(sum_kernel, "sum_bands", jax.ShapeDtypeStruct(parts.shape[1:], BF16), parts, megabytes=8)


def pack_kernel(
    left_ref, right_ref, mine_ref, theirs_ref, first_gain_ref, second_gain_ref, out_ref
):
    depth = mine_ref[...] + theirs_ref[...]
    rows, lane = left_ref.shape[1:]
    out_ref[:, 0:rows, :] = (left_ref[...].astype(F32) + right_ref[...].astype(F32)).astype(BF16)
    small = []
    for z in range(depth.shape[0]):
        for start in range(0, depth.shape[2], lane):
            small.append(depth[z, :, start : start + lane])
    for ref in (first_gain_ref, second_gain_ref):
        for start in range(0, ref.shape[1], lane):
            small.append(ref[:, start : start + lane])
    small = jnp.concatenate(small, axis=0).astype(BF16)
    for lat in range(out_ref.shape[0]):
        out_ref[lat, rows:, :] = small


def summed(ref, rows):
    total = ref[0, rows, :].astype(F32)
    for part in range(1, ref.shape[0]):
        total = total + ref[part, rows, :].astype(F32)
    return total


def merge_kernel(parts_ref, output_ref, input_ref, out_ref, output_out, input_out):
    z_size, out_rows, _ = out_ref.shape
    rows = parts_ref.shape[1]
    block = (rows - out_rows) // (z_size - 1)
    small = summed(parts_ref, slice(z_size * block, rows)).astype(BF16)
    for z in range(z_size):
        out_ref[z, 0:block, :] = summed(parts_ref, slice(z * block, (z + 1) * block)).astype(BF16)
        out_ref[z, block:, :] = small


def small_sum_kernel(parts_ref, small_ref):
    rows = parts_ref.shape[1] - small_ref.shape[0]
    small_ref[...] = summed(parts_ref, slice(rows, parts_ref.shape[1]))


def finish_kernel(parts_ref, first_ref, expand_ref, shrink_ref, in_ref, out_ref):
    block, split = expand_ref.shape
    lane = parts_ref.shape[2]
    for piece in range(split // lane):
        expand_ref[:, piece * lane : (piece + 1) * lane] = summed(
            parts_ref, slice(piece * block, (piece + 1) * block)
        )
    in_split, out_split = in_ref.shape[0], out_ref.shape[0]
    at = in_split + out_split
    in_ref[...] = first_ref[0:in_split, :].astype(F32)
    out_ref[...] = first_ref[in_split:at, :].astype(F32)
    for piece in range(shrink_ref.shape[1] // lane):
        shrink_ref[:, piece * lane : (piece + 1) * lane] = first_ref[at : at + out_split, :].astype(
            F32
        )
        at += out_split


def small_kernel(
    split, core_ref, mine_ref, theirs_ref, order_ref, depth_ref, first_gain_ref, second_gain_ref
):
    lane = mine_ref.shape[1]
    wide = depth_ref.shape[2]
    channels = first_gain_ref.shape[1]
    half_rows = 9 * wide // 2 // lane
    core = core_ref[0]
    pieces = wide // lane
    in_block = split // lane
    for side in range(2):
        which = core if side == 0 else 1 - core
        for piece in range(pieces // 2):
            source = mine_ref if side == 0 else theirs_ref
            block = source[piece * 9 : piece * 9 + 9, :]
            z, rest = divmod(piece, in_block)
            start = pl.multiple_of((2 * z + which) * split, lane) + rest * lane
            for a in range(3):
                depth_ref[a, :, pl.ds(pl.multiple_of(start, lane), lane)] = block[3 * a : 3 * a + 3]
    at = half_rows
    for ref in (first_gain_ref, second_gain_ref):
        for start in range(0, channels, lane):
            ref[:, start : start + lane] = mine_ref[at : at + 1, :] + theirs_ref[at : at + 1, :]
            at += 1


def backward_kernel(
    frame, norm_factor, stride, which_ref, *refs
):
    earlier_ref = refs[0] if len(refs) == 25 else None
    (
        back_ref, state_ref, gain_ref, kernel_ref, order_ref, shrink_hbm, slope_hbm,
        expand_slope_hbm, expand_hbm, activated_hbm, part_hbm, depth_ref, input_ref, gain_grad_ref,
        back_normed, shrink_all, slope_all, expand_slope_all, expand_all, activated_all, part_ref,
        normed, arrived, sent,
    ) = refs[-24:]
    cells, channels = state_ref.shape
    row_count, lon_count, _ = input_ref.shape
    lat_size, steps, _, lane = part_ref.shape
    part = slope_all.shape[2]
    block = channels // lat_size
    copies = []
    for step in range(steps):
        place = stride * step + which_ref[0]
        here = pl.ds(pl.multiple_of(place * part, part), part)
        pairs = (
            (shrink_hbm.at[here], shrink_all.at[step]),
            (slope_hbm.at[place], slope_all.at[step]),
            (expand_slope_hbm.at[place], expand_slope_all.at[step]),
            (expand_hbm.at[:, here], expand_all.at[step]),
            (activated_hbm.at[place], activated_all.at[step]),
        )
        copies.append(
            [
                pltpu.make_async_copy(source, target, arrived.at[step, i])
                for i, (source, target) in enumerate(pairs)
            ]
        )
        for copy in copies[step]:
            copy.start()
    column = lax.broadcasted_iota(jnp.int32, (frame, part), 0)
    outside = (column < SIDE) | (column >= SIDE + lon_count)
    outside = jnp.concatenate([outside] * row_count, axis=0)
    normed[...] = normalise(state_ref[...].astype(F32), gain_ref[...]).T
    sends = []
    for step in range(steps):
        place = stride * step + which_ref[0]
        kernel = kernel_ref[place]
        copies[step][0].wait()
        copies[step][1].wait()
        back_convolved = times_transpose(back_ref[...], shrink_all[step])
        back_convolved = (back_convolved * slope_all[step].astype(F32)).astype(BF16).astype(F32)
        flipped = jnp.concatenate([kernel[8 - i : 9 - i] for i in range(9)], axis=0)
        back_activated = convolve(back_convolved, flipped, row_count, frame)
        copies[step][2].wait()
        back_expanded = back_activated * expand_slope_all[step].astype(F32)
        back_expanded = jnp.where(outside, 0.0, back_expanded).astype(BF16)
        expand_grad = (matmul(normed[...], back_expanded) * norm_factor).astype(BF16)
        for lat in range(lat_size):
            for piece in range(part // lane):
                part_ref[lat, step, piece * block : (piece + 1) * block, :] = expand_grad[
                    lat * block : (lat + 1) * block, piece * lane : (piece + 1) * lane
                ]
        sends.append(
            pltpu.make_async_copy(part_ref.at[:, step], part_hbm.at[:, step], sent.at[step])
        )
        sends[step].start()
        copies[step][3].wait()
        product = times_transpose(back_expanded, expand_all[step])
        if step > 0:
            product = product + back_normed[...]
        elif earlier_ref is not None:
            product = product + earlier_ref[...]
        back_normed[...] = product
        own_back = jnp.where(outside, 0.0, back_convolved[frame : frame + cells])
        copies[step][4].wait()
        activated = activated_all[step].astype(F32)
        for b in range(3):
            moved = own_back
            if b != 1:
                moved = pltpu.roll(own_back, cells - 1 if b == 0 else 1, 0)
            for a in range(3):
                depth_ref[step, 3 * a + b : 3 * a + b + 1, :] = norm_factor * jnp.sum(
                    activated[a * frame : a * frame + cells] * moved, axis=0, keepdims=True
                )
    state = state_ref[...].astype(F32)
    inverse = inverse_rms(state)
    grads = back_normed[...]
    gain_grad_ref[...] = norm_factor * jnp.sum(grads * state * inverse, axis=0, keepdims=True)
    result = back_ref[frame : frame + cells, :].astype(F32) + norm_back(
        grads, state, inverse, gain_ref[...]
    )
    for row in range(row_count):
        start = row * frame + SIDE
        input_ref[row] = result[start : start + lon_count].astype(BF16)
    for send in sends:
        send.wait()


def backward(
    which, back, state, gain, earlier, order, shrink_weight, slope, activated, expand_weight,
    expand_slope, kernel, norm_factor, lat_size, row_count, lon_count,
):
    cells, channels = state.shape
    frame = cells // row_count
    steps, size, part = activated.shape
    stride = 1
    if which is None:
        which = 0
    else:
        steps, stride = steps // 2, 2
    block = channels // lat_size
    lane = block
    part_shape = (lat_size, steps, part // lane * block, lane)
    here, away = pl.BlockSpec(memory_space=pltpu.VMEM), pl.BlockSpec(memory_space=pl.ANY)
    operands = (back, state, gain, kernel)
    if earlier is not None:
        operands = (earlier,) + operands
    return pl.pallas_call(
        functools.partial(backward_kernel, frame, norm_factor, stride),
        in_specs=[pl.BlockSpec(memory_space=pltpu.SMEM)] + [here] * len(operands) + [away] * 6,
        out_specs=(away,) + (here,) * 4,
        scratch_shapes=[
            pltpu.VMEM((steps, part, channels), BF16),
            pltpu.VMEM((steps, size, part), BF16),
            pltpu.VMEM((steps, cells, part), BF16),
            pltpu.VMEM((steps, channels, part), BF16),
            pltpu.VMEM((steps, size, part), BF16),
            pltpu.VMEM(part_shape, BF16),
            pltpu.VMEM((channels, cells), BF16),
            pltpu.SemaphoreType.DMA((steps, 5)),
            pltpu.SemaphoreType.DMA((steps,)),
        ],
        out_shape=(
            jax.ShapeDtypeStruct(part_shape, BF16),
            jax.ShapeDtypeStruct((steps, 9, part), F32),
            jax.ShapeDtypeStruct((row_count, lon_count, channels), BF16),
            jax.ShapeDtypeStruct((1, channels), F32),
            jax.ShapeDtypeStruct((cells, channels), F32),
        ),
        compiler_params=pltpu.CompilerParams(vmem_limit_bytes=56 * 1024 * 1024),
        cost_estimate=pl.CostEstimate(
            flops=8 * cells * channels * part * steps,
            bytes_accessed=(6 * channels + 12 * size) * part * steps,
            transcendentals=0,
        ),
        name="backward",
    )(
        jnp.reshape(which, (1,)).astype(jnp.int32), *operands, order, shrink_weight, slope,
        expand_slope, expand_weight, activated,
    )


def attention_kernel(
    head_width, query_block, qkv_ref, early_ref, order_ref, out_ref, heads_t, query_grad_t, key_t,
    value_t, back_ref, bias_ref, key_grad, value_grad, score_ref, back_prob_ref, prob_low_ref, back_score_ref,
):
    head = pl.program_id(0)
    cells = qkv_ref.shape[0]
    width = qkv_ref.shape[1] // 3
    sources = early_ref.shape[0]
    frame = cells // sources
    scale = 1.0 / math.sqrt(head_width)
    keys = qkv_ref[:, width : 2 * width]
    values = qkv_ref[:, 2 * width : 3 * width]
    part = 2 * frame

    @pl.when(head == 0)
    def _():
        key_t[...] = keys.T
        value_t[...] = values.T
        for source in range(sources):
            at = slice(source * frame, (source + 1) * frame)
            back_ref[at, :] = early_ref[source, 0:frame, 0:width]
            if early_ref.shape[1] > frame:
                bias_ref[at, :] = early_ref[source, frame:, :].astype(F32).T[0:frame]
            else:
                bias_ref[at, :] = early_ref[source, :, width:].astype(F32)
        key_grad[...] = jnp.zeros_like(key_grad)
        value_grad[...] = jnp.zeros_like(value_grad)

    lanes = lax.broadcasted_iota(jnp.int32, (1, width), 1) // head_width == head
    zero = jnp.zeros((), BF16)
    heads = lax.broadcasted_iota(jnp.int32, bias_ref.shape, 1)
    bias = LOG2E * jnp.sum(
        jnp.where(heads == head, bias_ref[...], 0.0), axis=1, keepdims=True
    )
    rows = pl.ds(pl.multiple_of(head * head_width, head_width), head_width)
    head_key_t = key_t[rows, :]
    head_value_t = value_t[rows, :]
    last_dims = (((1,), (1,)), ((), ()))

    def fold(values, combine):
        result = values[0:8]
        for start in range(8, values.shape[0], 8):
            result = combine(result, values[start : start + 8])
        return result

    def block(start):
        cols = pl.ds(start, query_block)
        queries = jnp.where(lanes, qkv_ref[cols, 0:width], zero)
        backs = jnp.where(lanes, back_ref[cols, :], zero)
        parts = [slice(i, i + part) for i in range(0, cells, part)]
        highest = jnp.full((8, query_block), -jnp.inf, F32)
        for at in parts:
            scores = lax.dot_general(
                qkv_ref[at, width : 2 * width], queries, last_dims, preferred_element_type=F32
            )
            scores = scores * (scale * LOG2E) + bias[at]
            score_ref[at, :] = scores
            highest = jnp.maximum(highest, fold(scores, jnp.maximum))
        highest = jnp.max(highest, axis=0, keepdims=True)
        total = jnp.zeros((8, query_block), F32)
        centred = jnp.zeros((8, query_block), F32)
        for at in parts:
            back_probs = lax.dot_general(
                qkv_ref[at, 2 * width : 3 * width], backs, last_dims, preferred_element_type=F32
            )
            exponent = jnp.exp2(score_ref[at, :] - highest)
            total = total + fold(exponent, jnp.add)
            centred = centred + fold(exponent * back_probs, jnp.add)
            score_ref[at, :] = exponent
            back_prob_ref[at, :] = back_probs
        inverse = 1.0 / jnp.sum(total, axis=0, keepdims=True)
        centred = jnp.sum(centred, axis=0, keepdims=True) * inverse
        for at in parts:
            probs = score_ref[at, :] * inverse
            probs_low = probs.astype(BF16)
            back_scores = (probs * (back_prob_ref[at, :] - centred)).astype(BF16)
            prob_low_ref[at, :] = probs_low
            back_score_ref[at, :] = back_scores
            value_grad[at, :] += matmul(probs_low, backs)
            key_grad[at, :] += matmul(back_scores, queries)
        heads_t[rows, cols] = matmul(head_value_t, prob_low_ref[...])
        query_grad_t[rows, cols] = matmul(head_key_t, back_score_ref[...])

    block_count = cells // query_block
    if block_count <= 4:
        for index in range(block_count):
            block(index * query_block)
    else:

        def step(index, carry):
            block(pl.multiple_of(index * query_block, query_block))
            return carry

        lax.fori_loop(0, block_count, step, 0)

    @pl.when(head == pl.num_programs(0) - 1)
    def _():
        out_ref[:, 0:width] = heads_t[...].T.astype(BF16)
        out_ref[:, width : 2 * width] = (query_grad_t[...] * scale).T.astype(BF16)
        out_ref[:, 2 * width : 3 * width] = (key_grad[...] * scale).astype(BF16)
        out_ref[:, 3 * width : 4 * width] = value_grad[...].astype(BF16)


def attention(qkv, early, order, head_width):
    cells = qkv.shape[0]
    width = qkv.shape[1] // 3
    items = width // head_width
    bias_columns = BIAS_ROWS if early.shape[2] == width else items
    query_block = cells if cells <= 1024 else 256
    whole = lambda shape: pl.BlockSpec(shape, lambda head: (0,) * len(shape))
    return pl.pallas_call(
        functools.partial(attention_kernel, head_width, query_block),
        grid=(items,),
        out_shape=jax.ShapeDtypeStruct((cells, 4 * width), BF16),
        in_specs=[whole(qkv.shape), whole(early.shape), pl.BlockSpec(memory_space=pl.ANY)],
        out_specs=whole((cells, 4 * width)),
        scratch_shapes=[
            pltpu.VMEM((width, cells), F32),
            pltpu.VMEM((width, cells), F32),
            pltpu.VMEM((width, cells), BF16),
            pltpu.VMEM((width, cells), BF16),
            pltpu.VMEM((cells, width), BF16),
            pltpu.VMEM((cells, bias_columns), F32),
            pltpu.VMEM((cells, width), F32),
            pltpu.VMEM((cells, width), F32),
            pltpu.VMEM((cells, query_block), F32),
            pltpu.VMEM((cells, query_block), F32),
            pltpu.VMEM((cells, query_block), BF16),
            pltpu.VMEM((cells, query_block), BF16),
        ],
        compiler_params=pltpu.CompilerParams(
            vmem_limit_bytes=(20 if cells <= 1024 else 48) * 1024 * 1024, dimension_semantics=("arbitrary",)
        ),
        cost_estimate=pl.CostEstimate(
            flops=items * cells * cells * 32 * 14,
            bytes_accessed=cells * width * 16,
            transcendentals=items * cells * cells,
        ),
        name="attention",
    )(qkv, early, order)


def per_device(
    state_field,
    cotangent,
    key_bias,
    input_gain,
    expand_weight,
    depth_weight,
    shrink_weight,
    attention_gain,
    attention_in,
    attention_out,
):
    row_count, lon_count, channels = state_field.shape
    head_count = key_bias.shape[2]
    head_width = channels // head_count
    wide = expand_weight.shape[1]
    lat_size, z_size = lax.axis_size("lat"), lax.axis_size("z")
    lon_size = 2 * z_size
    core = lax.axis_index("core")
    norm_factor = 1.0 / math.sqrt(row_count * lon_count * lat_size * lon_size)
    items = row_count * head_count // lon_size
    groups = head_count // items
    width = items * head_width
    frame = lon_count + 2 * SIDE
    own = row_count * frame
    kernel = depth_weight.astype(F32).reshape(9, wide)
    kernel_blocks = kernel.reshape(9, -1, step_width(wide)).transpose(1, 0, 2)
    input_gain = input_gain.reshape(1, channels)
    attention_gain = attention_gain.reshape(1, channels)

    low, high = from_sides(state_field, SIDE, 1, LON, True)
    state = jnp.concatenate([low, state_field, high], axis=1)
    if row_count == 1:
        below, above = from_sides(state, 1, 0, "lat", False)
        far_below = lax.ppermute(below, "lat", shifts(lat_size, 1, False))
        far_above = lax.ppermute(above, "lat", shifts(lat_size, -1, False))
        all_rows = [far_below, below, state, above, far_above]
    else:
        below, above = from_sides(state, 2, 0, "lat", False)
        all_rows = [below, state, above]
    all_rows = jnp.concatenate(all_rows, axis=0)

    early, cot = early_parts(cotangent, key_bias, attention_out, state, groups)
    early = exchange(early, LON)

    qkv, inner = forward(
        all_rows, input_gain, expand_weight, depth_weight, shrink_weight, attention_gain,
        attention_in,
        groups,
    )
    activated, slope, mixed, expand_slope = around(
        all_rows, input_gain, expand_weight, kernel_blocks, inner
    )
    qkv = exchange(qkv, LON).reshape(lon_size * frame, 3 * width)

    attended = attention(qkv, early, mixed, head_width)
    attended = exchange(attended.reshape(lon_size, frame, 4 * width), LON)
    cot = cot.reshape(own, channels)
    output_field, back_inner, unpacked, gain_two = call(
        functools.partial(inner_kernel, groups, norm_factor),
        "back_inner",
        (
            jax.ShapeDtypeStruct((row_count, lon_count, channels), BF16),
            jax.ShapeDtypeStruct((own, channels), BF16),
            jax.ShapeDtypeStruct((own, 4 * channels), BF16),
            jax.ShapeDtypeStruct((1, channels), F32),
        ),
        attended,
        inner,
        cot,
        attention_out,
        attention_in,
        attention_gain,
        flops=8 * own * channels * channels,
    )

    back = back_inner.reshape(row_count, frame, channels)
    centre = back[:, SIDE : SIDE + lon_count]
    low, high = from_sides(centre, 1, 1, LON, True)
    edge = jnp.zeros((row_count, SIDE - 1, channels), BF16)
    back_sides = jnp.concatenate([edge, low, centre, high, edge], axis=1)
    below, above = from_sides(back_sides, 1, 0, "lat", False)
    back = jnp.concatenate([below, back_sides, above], axis=0).reshape(-1, channels)

    lane = channels // lat_size
    in_split, out_split, split = 3 * channels // lon_size, channels // lon_size, wide // lon_size
    grads = lambda which, order, added: weight_grads(
        which, unpacked, inner, attention_gain, cot, back_inner, mixed, order, added, norm_factor,
        lat_size, z_size,
    )
    theirs = grads(1 - core, back_sides, None)
    first = after(grads(core, back_sides, core_swap(theirs)), below, above)
    first_sums = sum_parts(exchange(first, "lat"))
    first_sums = lax.psum_scatter(first_sums, "z", scatter_dimension=0, tiled=True)
    flat = lambda parts: parts.reshape(lat_size, -1, lane)

    state = state.reshape(own, channels)

    def backward_part(which, earlier, order):
        return backward(
            which, back, state, input_gain, earlier, order, shrink_weight, slope, activated,
            expand_weight, expand_slope, kernel_blocks, norm_factor, lat_size, row_count, lon_count,
        )

    if split == step_width(wide):
        theirs, depth_theirs, _, _, partial = backward_part(1 - core, None, first)
        theirs = core_swap(theirs)
        depth_theirs = core_swap(depth_theirs)
        mine, depth_mine, input_grad, gain_one, _ = backward_part(core, partial, first)
    else:
        parts, depth, input_grad, gain_one, _ = backward_part(None, None, first)
        steps = parts.shape[1]
        parts = parts.reshape(lat_size, steps, -1, split // lane, lane, lane)
        parts = parts.reshape(lat_size, z_size, 2, split // lane * lane, lane)
        theirs = core_swap(lax.dynamic_index_in_dim(parts, 1 - core, 2, False))
        mine = lax.dynamic_index_in_dim(parts, core, 2, False)
        depth = depth.reshape(steps, 9, -1, split).transpose(0, 2, 1, 3)
        depth = depth.reshape(z_size, 2, 9, split)
        depth_theirs = core_swap(lax.dynamic_index_in_dim(depth, 1 - core, 1, False))
        depth_mine = lax.dynamic_index_in_dim(depth, core, 1, False)

    mine, theirs = flat(mine), flat(theirs)
    block_rows = mine.shape[1] // z_size
    small_rows = (9 * wide // 2 + 2 * channels) // lane
    output_field = output_field.transpose(1, 0, 2)
    input_grad = input_grad.transpose(1, 0, 2)
    second = call(
        pack_kernel,
        "pack",
        jax.ShapeDtypeStruct((lat_size, z_size * block_rows + small_rows, lane), BF16),
        mine,
        theirs,
        depth_mine,
        depth_theirs,
        gain_one,
        gain_two,
        megabytes=56,
    )
    field = jax.ShapeDtypeStruct(output_field.shape, BF16)
    second, output_field, input_grad = call(
        merge_kernel,
        "merge",
        (jax.ShapeDtypeStruct((z_size, block_rows + small_rows, lane), BF16), field, field),
        exchange(second, "lat"),
        output_field,
        input_grad,
        specs=[pl.BlockSpec(memory_space=pltpu.VMEM)] + [pl.BlockSpec(memory_space=pl.ANY)] * 2,
        out_specs=(pl.BlockSpec(memory_space=pltpu.VMEM),)
        + (pl.BlockSpec(memory_space=pl.ANY),) * 2,
        aliases={1: 1, 2: 2},
    )
    weight = lambda rows, cols: jax.ShapeDtypeStruct((rows, cols), F32)
    second = exchange(second, "z")
    small = call(small_sum_kernel, "small_sums", weight(small_rows, lane), second)
    expand_grad, shrink_grad, attention_in_grad, attention_out_grad = call(
        finish_kernel,
        "finish",
        (
            weight(lane, split),
            weight(out_split, wide // lat_size),
            weight(in_split, lane),
            weight(out_split, lane),
        ),
        second,
        first_sums,
    )
    other = core_swap(small)
    if split % 128 == 0:
        depth_grad, input_gain_grad, attention_gain_grad = pl.pallas_call(
            functools.partial(small_kernel, split),
            out_shape=(
                jax.ShapeDtypeStruct((3, 3, wide), F32),
                weight(1, channels),
                weight(1, channels),
            ),
            in_specs=[
                pl.BlockSpec(memory_space=pltpu.SMEM),
                pl.BlockSpec(memory_space=pltpu.VMEM),
                pl.BlockSpec(memory_space=pltpu.VMEM),
                pl.BlockSpec(memory_space=pl.ANY),
            ],
        name="small_grads",
        )(core.reshape(1), small, other, attention_out_grad)
    else:
        rows = 9 * wide // 2 // lane
        own_half, other_half = small[:rows], other[:rows]
        depth_grad = jnp.where(
            core == 0, jnp.stack([own_half, other_half]), jnp.stack([other_half, own_half])
        )
        depth_grad = depth_grad.reshape(2, z_size, split // lane, 9, lane).transpose(3, 1, 0, 2, 4)
        depth_grad = depth_grad.reshape(3, 3, wide)
        gains = (small[rows:] + other[rows:]).reshape(2, channels)
        input_gain_grad, attention_gain_grad = gains[0], gains[1]
    return (
        output_field.transpose(1, 0, 2),
        input_grad.transpose(1, 0, 2),
        expand_grad,
        shrink_grad.T,
        attention_in_grad.T,
        attention_out_grad.T,
        depth_grad,
        input_gain_grad.reshape(channels),
        attention_gain_grad.reshape(channels),
    )


def solution(mesh):
    lat_size, lon_size = mesh.devices.shape
    split = Mesh(mesh.devices.reshape(lat_size, lon_size // 2, 2), ("lat", "z", "core"))
    grid = P("lat", LON, None)
    weight = P("lat", LON)

    def step(*arrays):
        outputs = jax.shard_map(
            per_device,
            mesh=split,
            in_specs=(grid, grid, grid) + (P(),) * 7,
            out_specs=(grid, grid, weight, weight, weight, weight, P(), P(), P()),
            check_vma=False,
        )(*arrays)
        return outputs

    return step
```
